32 devices in a mesh: wide: 16 (over z, y, core), narrow: 2 (over x).
Axes of the slice: x: 2, y: 2, z: 4, core: 2. Of those that a mesh axis runs over, the one named last changes fastest.
Arguments:
- right_side: float32 [128, 32, 512], P('wide', 'narrow'), may hold values from -18 to 18
- diagonal: float32 [128, 32, 512], P('wide', 'narrow'), may hold values from 0.01 to 2
- coarse_slot: int32 [16, 4, 64], P('wide', 'narrow'), may hold values from 0 to 127, as said below
- coarse_factor: float32 [4096, 2048], P(('wide', 'narrow')), may hold values from -0.125 to 0.125
Outputs:
- solution_field: float32 [128, 32, 512], P('wide', 'narrow')
- residual: float32 [128, 32, 512], P('wide', 'narrow')
The draws below stay inside these ranges and needn't reach their ends.
Inputs may be any that keep to these rules, and one draw needn't show every extreme that they name: `coarse_slot`: within each device block the slots of its 128 elements, in row-major order over the block's elements, are a permutation of 0 to 127.
All inputs are finite; a program needn't handle non-finite values.
Results may differ from the reference program's by a relative error of at most 0.0003.
Values sent between devices are 32-bit elements; how exact they have to be, the bound alone decides.
No kernel may reach another device: no remote copies, remote signals or barrier semaphores. Data moves between devices by JAX's collectives and lax.ppermute only.
A program may use at most 64 MiB of HBM per device.

```python
import jax
import jax.numpy as jnp
from jax import lax

CX = 8
CY = 16
KCOL = 2048
ITERS = 2
ELEM_DEV = 128
NX = 128
NY = 32
NZ = 512
ELEMS = 4096
N_NARROW = 2


def draw_right_side(key, part):
    scale_ramp = 1.0 + 2.0 * jnp.arange(NX, dtype=jnp.float32) / (NX - 1)
    scale_ramp = scale_ramp[:, None, None]
    random_part = jax.random.truncated_normal(key, -6.0, 6.0, (NX, NY, NZ), jnp.float32)
    return random_part * scale_ramp


def draw_diagonal(key, part):
    key_levels = jax.random.fold_in(key, 11)
    key_cells = jax.random.fold_in(key, 12)
    levels = jnp.exp(jax.random.uniform(key_levels, (NX // 8, NY // 8, NZ // 8), jnp.float32, jnp.log(0.02), 0.0))
    levels = jnp.repeat(jnp.repeat(jnp.repeat(levels, 8, 0), 8, 1), 8, 2)
    roughness = jnp.exp(jax.random.uniform(key_cells, (NX, NY, NZ), jnp.float32, jnp.log(0.5), jnp.log(2.0)))
    return levels * roughness


def draw_coarse_slot(key, part):
    per_x = CX // 8
    per_y = CY // 8
    per_z = NZ // 8
    groups_x = NX // CX
    groups_y = NY // CY
    key_list = jax.random.split(key, groups_x * groups_y)
    orders = jax.vmap(lambda single: jax.random.permutation(single, ELEM_DEV))(key_list)
    orders = orders.reshape(groups_x, groups_y, per_x, per_y, per_z).transpose(0, 2, 1, 3, 4)
    return orders.reshape(NX // 8, NY // 8, per_z).astype(jnp.int32)


def shard_levels(key, shape, pieces, least, high):
    level = 1.0
    for axis_at, parts in pieces:
        heights = jax.random.uniform(jax.random.fold_in(jax.random.fold_in(key, 6), axis_at), (parts,), jnp.float32, least / len(pieces), high / len(pieces))
        level = level * jnp.repeat(jnp.exp(heights), shape[axis_at] // parts).reshape((-1,) + (1,) * (len(shape) - 1 - axis_at))
    return level


def centred(stream_key, extent, scale, most, cuts=(), kind=jnp.bfloat16):
    array = jax.random.normal(stream_key, extent, jnp.float32) * scale
    if len(cuts) > 0:
        array = shard_levels(stream_key, extent, cuts, -0.22, 0.18) * array
    return jnp.clip(array, min=-most, max=most).astype(kind)


def setup_inputs(seed: int = 0) -> dict:
    streams_of = jax.random.split(jax.random.key(seed), 5)
    return {
        "right_side": draw_right_side(jax.random.fold_in(streams_of[4], 71), 0),
        "diagonal": draw_diagonal(jax.random.fold_in(streams_of[4], 71), 0),
        "coarse_slot": draw_coarse_slot(jax.random.fold_in(streams_of[4], 71), 0),
        "coarse_factor": centred(streams_of[3], (ELEMS, KCOL), KCOL ** -0.5, 0.125, ((0, 32),), jnp.float32),
    }


def sine_table():
    indices = jnp.arange(10, dtype=jnp.float32)
    sine_basis = jnp.sqrt(2.0 / 11.0) * jnp.sin(jnp.pi * (indices[:, None] + 1.0) * (indices[None, :] + 1.0) / 11.0)
    values = 2.0 - 2.0 * jnp.cos(jnp.pi * (indices + 1.0) / 11.0)
    return (sine_basis, values)

def front_windows(values_in):
    length = values_in.shape[0] - 2
    count = length // 8
    middle = values_in[1:length + 1].reshape((count, 8) + values_in.shape[1:])
    before = values_in[0:length:8][:, None]
    after = values_in[9:length + 2:8][:, None]
    return jnp.concatenate([before, middle, after], axis=1)

def schwarz(extended, sigma):
    count_x, count_y, count_z = sigma.shape
    sine_basis, values = sine_table()
    precise = lax.Precision.HIGHEST
    blocks = front_windows(extended)
    blocks = front_windows(jnp.moveaxis(blocks, 2, 0))
    blocks = front_windows(jnp.moveaxis(blocks, 4, 0))
    blocks = blocks.transpose(5, 3, 1, 4, 2, 0).reshape(10, 10, 10, -1)
    spectra = jnp.einsum('ia,ijke->ajke', sine_basis, blocks, precision=precise)
    spectra = jnp.einsum('jb,ajke->abke', sine_basis, spectra, precision=precise)
    spectra = jnp.einsum('kc,abke->abce', sine_basis, spectra, precision=precise)
    spread = values[:, None, None] + values[None, :, None] + values[None, None, :]
    spectra = spectra / (spread[:, :, :, None] + sigma.reshape(-1)[None, None, None, :])
    interior_basis = sine_basis[1:9]
    nodal = jnp.einsum('ia,abce->ibce', interior_basis, spectra, precision=precise)
    nodal = jnp.einsum('jb,ibce->ijce', interior_basis, nodal, precision=precise)
    nodal = jnp.einsum('kc,ijce->ijke', interior_basis, nodal, precision=precise)
    nodal = nodal.reshape(8, 8, 8, count_x, count_y, count_z).transpose(3, 0, 4, 1, 5, 2)
    return nodal.reshape(8 * count_x, 8 * count_y, 8 * count_z)

def element_sums(field_values):
    size_x, size_y, size_z = field_values.shape
    return field_values.reshape(size_x // 8, 8, size_y // 8, 8, size_z // 8, 8).sum(axis=(1, 3, 5))

def expand(element_values):
    count_x, count_y, count_z = element_values.shape
    spread_out = jnp.broadcast_to(element_values[:, None, :, None, :, None], (count_x, 8, count_y, 8, count_z, 8))
    return spread_out.reshape(8 * count_x, 8 * count_y, 8 * count_z)

def operate(padded, coefficient):
    centre = padded[1:-1, 1:-1, 1:-1]
    beside = padded[2:, 1:-1, 1:-1] + padded[:-2, 1:-1, 1:-1]
    beside = beside + padded[1:-1, 2:, 1:-1] + padded[1:-1, :-2, 1:-1]
    beside = beside + padded[1:-1, 1:-1, 2:] + padded[1:-1, 1:-1, :-2]
    return (6.0 + coefficient) * centre - beside

def coarse_reference(residual, coarse_slot, coarse_factor):
    totals = element_sums(residual) / 16.0
    grid_x, grid_y, grid_z = totals.shape
    owner_share = ELEM_DEV // N_NARROW
    wide_part = (jnp.arange(grid_x, dtype=jnp.int32) // (CX // 8))[:, None, None]
    narrow_part = (jnp.arange(grid_y, dtype=jnp.int32) // (CY // 8))[None, :, None]
    owner_part = coarse_slot // owner_share
    coarse_rows = ((wide_part * N_NARROW + owner_part) * ELEM_DEV + narrow_part * owner_share + coarse_slot % owner_share).reshape(-1).astype(jnp.int32)
    ordered = jnp.zeros((grid_x * grid_y * grid_z,), jnp.float32).at[coarse_rows].set(totals.reshape(-1))
    precise = lax.Precision.HIGHEST
    projected = jnp.dot(ordered, coarse_factor, precision=precise)
    corrected = jnp.dot(coarse_factor, projected, precision=precise)
    return expand(corrected[coarse_rows].reshape(grid_x, grid_y, grid_z) / 16.0)

def precondition(residual, sigma, coarse_slot, coarse_factor):
    padded = jnp.pad(residual, 1)
    rows_x = residual.shape[0] // 8

    def slab_solve(element_x):
        start = (element_x * 8).astype(jnp.int32)
        window = lax.dynamic_slice_in_dim(padded, start, 10, 0)
        local_sigma = lax.dynamic_slice_in_dim(sigma, element_x, 1, 0)
        return schwarz(window, local_sigma)
    slabs = lax.map(slab_solve, jnp.arange(rows_x, dtype=jnp.int32))
    return slabs.reshape(residual.shape) + coarse_reference(residual, coarse_slot, coarse_factor)

def reference(right_side, diagonal, coarse_slot, coarse_factor):
    sigma = element_sums(diagonal) / 512.0
    solution = jnp.zeros_like(right_side)
    residual = right_side
    search = precondition(residual, sigma, coarse_slot, coarse_factor)
    product_now = jnp.sum(residual * search)
    direction = search
    for sweep in range(ITERS):
        image_field = operate(jnp.pad(direction, 1), diagonal)
        step_size = product_now / jnp.sum(direction * image_field)
        solution = solution + step_size * direction
        residual = residual - step_size * image_field
        if sweep + 1 < ITERS:
            search = precondition(residual, sigma, coarse_slot, coarse_factor)
            product_next = jnp.sum(residual * search)
            direction = search + product_next / product_now * direction
            product_now = product_next
    return (solution, residual)
```

```python
import functools

import jax
import jax.numpy as jnp
import numpy as np
from jax import lax
from jax.experimental import pallas as pl
from jax.experimental.pallas import tpu as pltpu
from jax.sharding import PartitionSpec as P

F32 = jnp.float32
BF16 = jnp.bfloat16
BX, BY, BZ = 8, 16, 512
EY, EZ = 2, 64
ELEMS = EY * EZ
YR = 24
YW = YR * (BX + 2)
AB = 208
KCOL = 2048
WIDTH = KCOL + 128
AXES = ("wide", "narrow")


def split_const(values):
    high = values.astype(jnp.bfloat16)
    low = (values - high.astype(np.float64)).astype(jnp.bfloat16)
    return high, low


@functools.lru_cache(maxsize=None)
def tables():
    index = np.arange(10, dtype=np.float64)
    basis = np.sqrt(2.0 / 11.0) * np.sin(np.pi * (index[:, None] + 1.0) * (index[None, :] + 1.0) / 11.0)
    values = 2.0 - 2.0 * np.cos(np.pi * (index + 1.0) / 11.0)
    to_z = np.zeros((BZ, 10 * EZ))
    from_z = np.zeros((10 * EZ, BZ))
    for e in range(EZ):
        for k in range(10):
            z = 8 * e + k - 1
            if 0 <= z < BZ:
                to_z[z, e::EZ] = basis[k]
            if 1 <= k <= 8:
                from_z[e::EZ, z] = basis[k]
    to_xy = np.zeros((10, EY, 10, 10, YR))
    from_xy = np.zeros((BX, BY, 10, EY, 10))
    for e in range(EY):
        for j in range(10):
            y = 8 * e + j - 1
            to_xy[:, e, :, :, y % YR] += basis.T[:, None, :] * basis[j][None, :, None]
            if 1 <= j <= 8:
                from_xy[:, y, :, e, :] = basis[1:9, :, None] * basis[j][None, None, :]
    to_xy = np.pad(to_xy.reshape(200, YW), ((0, AB - 200), (0, 0)))
    from_xy = np.pad(from_xy.reshape(BX * BY, 200), ((0, 0), (0, AB - 200)))
    column = np.zeros((AB, 128), np.float32)
    grid = np.zeros((10, EY, 10, 2))
    grid[..., 0] = values[:, None, None] + values[None, None, :]
    grid[..., 1] = np.arange(EY)[None, :, None]
    column[:200, :2] = grid.reshape(200, 2)
    column[200:, 0] = 1.0
    line = np.repeat(values, EZ)[None, :].astype(np.float32)
    gather = np.zeros((BZ, EY * ELEMS), np.float32)
    spread = np.zeros((ELEMS, EY * BZ), np.float32)
    for e in range(EY):
        for z in range(BZ):
            gather[z, e * ELEMS + e * EZ + z // 8] = 1.0
            spread[e * EZ + z // 8, e * BZ + z] = 1.0
    fine = split_const(to_xy) + split_const(to_z) + split_const(from_xy) + split_const(from_z) + (column, line)
    return fine, gather.astype(jnp.bfloat16), spread.astype(jnp.bfloat16)


def dot(a, b):
    return jnp.dot(a, b, preferred_element_type=F32)


def split2(x):
    high = x.astype(BF16)
    return high, (x - high.astype(F32)).astype(BF16)


def split3(x):
    high = x.astype(BF16)
    rest = x - high.astype(F32)
    middle = rest.astype(BF16)
    return high, middle, (rest - middle.astype(F32)).astype(BF16)


def dot3(a, b):
    return dot(a[0], b[0]) + dot(a[0], b[1]) + dot(a[1], b[0])


def iota(shape, axis):
    return lax.broadcasted_iota(jnp.int32, shape, axis)


def total(x):
    while x.ndim > 2:
        x = jnp.sum(x, axis=0)
    return jnp.sum(jnp.sum(x, axis=0, keepdims=True), axis=1, keepdims=True)


def element_row(field, gather):
    parts = jnp.concatenate(split3(jnp.sum(field, axis=0)), axis=0)
    sums = dot(parts, gather)
    sums = sums[0:16] + sums[16:32] + sums[32:48]
    return jnp.sum(sums[0:8, 0:ELEMS], axis=0, keepdims=True) + jnp.sum(sums[8:16, ELEMS:], axis=0, keepdims=True)


def expand_rows(rows, spread):
    count = rows.shape[0]
    tall = jnp.broadcast_to(rows, (16, ELEMS)) if count == 1 else jnp.concatenate([rows, jnp.zeros((16 - count, ELEMS), F32)], axis=0)
    wide = dot(jnp.concatenate(split3(tall), axis=0), spread)
    return (wide[0:16] + wide[16:32] + wide[32:48])[0:count]


def expand_block(row, spread):
    wide = expand_rows(row, spread)
    low = jnp.broadcast_to(wide[:, 0:BZ], (8, BZ))
    high = jnp.broadcast_to(wide[:, BZ:], (8, BZ))
    return jnp.concatenate([low, high], axis=0)


def row_to_column(row):
    eye = iota((ELEMS, ELEMS), 0) == iota((ELEMS, ELEMS), 1)
    return jnp.sum(jnp.where(eye, row, 0.0), axis=1, keepdims=True)


def slot_mask(slots, offset):
    slot_of_row = lax.rem(iota((ELEMS, ELEMS), 0) + offset, ELEMS)
    return slot_of_row == slots


def to_rows(element_values, slots, offset):
    return jnp.sum(jnp.where(slot_mask(slots, offset), element_values, 0.0), axis=1, keepdims=True)


def to_elements(row_values, slots, offset):
    return jnp.sum(jnp.where(slot_mask(slots, offset), row_values, 0.0), axis=0, keepdims=True)


def project(column, parts):
    out = 0.0
    at = 0
    for part in parts:
        size = part.shape[0]
        out = out + jnp.sum(column[at : at + size] * part[...], axis=0, keepdims=True)
        at += size
    return out


def correct(row, parts):
    out = []
    for part in parts:
        products = part[...] * row
        folded = products[:, 0:128]
        for at in range(128, KCOL, 128):
            folded = folded + products[:, at : at + 128]
        out.append(jnp.sum(folded, axis=1, keepdims=True))
    return jnp.concatenate(out, axis=0)


def store_sum(out_ref, projection, extra):
    count = out_ref.shape[0]
    out_ref[:, 0:KCOL] = jnp.broadcast_to(projection, (count, KCOL))
    out_ref[:, KCOL:WIDTH] = jnp.broadcast_to(extra, (count, WIDTH - KCOL))


def lanes(values):
    at = iota((1, 128), 1)
    row = jnp.zeros((1, 128), F32)
    for i, value in enumerate(values):
        row = jnp.where(at == i, value, row)
    return row


def lane(row, i):
    return jnp.sum(jnp.where(iota(row.shape, 1) == i, row, 0.0), axis=1, keepdims=True)


def odd(index):
    return lax.rem(index, 2) == 1


def pair_out(index, low, high):
    return jnp.where(odd(index), low, high), jnp.where(odd(index), high, low)


def pair_in(index, first, second):
    return jnp.where(odd(index), first, second), jnp.where(odd(index), second, first)


def extend_y(block, low, high, depth):
    at = iota((8, BZ), 0)
    tails = []
    for x in range(block.shape[0]):
        tail = jnp.zeros((8, BZ), F32)
        for i in range(depth):
            tail = jnp.where(at == i, high[i][x : x + 1], tail)
            tail = jnp.where(at == 8 - depth + i, low[i][x : x + 1], tail)
        tails.append(tail)
    return jnp.concatenate([block, jnp.stack(tails)], axis=1)


def roll_sum(x):
    count, rows, _ = x.shape
    beside = pltpu.roll(x, 1, 1) + pltpu.roll(x, rows - 1, 1)
    flat = x.reshape(count * rows, BZ)
    at = iota(flat.shape, 1)
    beside_z = jnp.where(at == 0, 0.0, pltpu.roll(flat, 1, 1)) + jnp.where(at == BZ - 1, 0.0, pltpu.roll(flat, BZ - 1, 1))
    return beside + beside_z.reshape(x.shape)


def fine_solve(rows, sigma, consts):
    wh, wl, th, tl, vh, vl, uh, ul, column, line = [ref[...] for ref in consts]
    sig = jnp.where(column[:, 1:2] == 0.0, tile_lanes(sigma, 0), tile_lanes(sigma, 1))
    inverse = 1.0 / (column[:, 0:1] + line + sig)
    spectra = dot3((wh, wl), split2(rows))
    spectra = dot3(split2(spectra), (th, tl)) * inverse
    nodal = dot3((vh, vl), split2(spectra))
    return dot3(split2(nodal), (uh, ul)).reshape(BX, BY, BZ)


def tile_lanes(sigma, e):
    low = iota((1, ELEMS), 1) < EZ
    rolled = pltpu.roll(sigma, EZ, 1)
    both = jnp.where(low, sigma, rolled) if e == 0 else jnp.where(low, rolled, sigma)
    return jnp.concatenate([both] * 5, axis=1)


def start_kernel(right_ref, diag_ref, slot_ref, gather_ref, c_ref, sigma_ref, ya_ref, yb_ref):
    d = lax.axis_index("narrow")
    gather = gather_ref[...]
    totals = element_row(right_ref[...], gather) * (1.0 / 16.0)
    sigma_ref[...] = element_row(diag_ref[...], gather) * (1.0 / 512.0)
    column = to_rows(totals, slot_ref[...], 0)
    eye = iota((ELEMS, ELEMS), 0) == iota((ELEMS, ELEMS), 1)
    row = jnp.sum(jnp.where(eye, column, 0.0), axis=0, keepdims=True)
    c_ref[...] = row
    for i, ref in enumerate((right_ref, diag_ref)):
        first, second = pair_out(d, ref[:, 0, :], ref[:, BY - 1, :])
        ya_ref[i] = first
        yb_ref[i] = second
    ya_ref[2] = jnp.concatenate([jnp.broadcast_to(row, (8, ELEMS)), jnp.zeros((8, BZ - ELEMS), F32)], axis=1)
    yb_ref[2] = jnp.zeros((8, BZ), F32)


def project_kernel(c_ref, ra_ref, rb_ref, right_ref, diag_ref, xa_ref, xb_ref, swapped, sum_ref, re_ref, de_ref, oa_ref, ob_ref):
    w, d = lax.axis_index("wide"), lax.axis_index("narrow")
    row = c_ref[...]
    if swapped:
        half = ELEMS // 2
        other = pltpu.roll(ra_ref[2, 0:1, 0:ELEMS], half, 1)
        row = jnp.where(iota((1, ELEMS), 1) // half == d, row, other)
    store_sum(sum_ref, project(row_to_column(row), (xa_ref, xb_ref)), jnp.zeros((1, 128), F32))
    for i, (ref, out) in enumerate(((right_ref, re_ref), (diag_ref, de_ref))):
        low, high = pair_in(d, ra_ref[i], rb_ref[i])
        block = extend_y(ref[...], [low], [high], 1)
        out[...] = block
        oa_ref[i], ob_ref[i] = pair_out(w, block[0], block[BX - 1])


def first_fine_kernel(re_ref, ra_ref, rb_ref, sigma_ref, *rest):
    w = lax.axis_index("wide")
    low, high = pair_in(w, ra_ref[0], rb_ref[0])
    rows = jnp.concatenate([low[None], re_ref[...], high[None]], axis=0).reshape(YW, BZ)
    rest[-1][...] = fine_solve(rows, sigma_ref[...], rest[:-1])


def first_coarse_kernel(sum_ref, fine_ref, slot_ref, offset_ref, spread_ref, xa_ref, xb_ref, out_ref, ya_ref, yb_ref):
    d = lax.axis_index("narrow")
    row = jnp.sum(sum_ref[...], axis=0, keepdims=True)
    values = to_elements(correct(row[:, 0:KCOL], (xa_ref, xb_ref)), slot_ref[...], offset_ref[0])
    out_ref[...] = fine_ref[...] + expand_block(values * (1.0 / 16.0), spread_ref[...])[None]
    for i in range(2):
        ya_ref[i], yb_ref[i] = pair_out(d, out_ref[:, i, :], out_ref[:, BY - 2 + i, :])


def extend_kernel(s_ref, ra_ref, rb_ref, se_ref, xa_ref, xb_ref):
    w, d = lax.axis_index("wide"), lax.axis_index("narrow")
    pairs = [pair_in(d, ra_ref[i], rb_ref[i]) for i in range(2)]
    block = extend_y(s_ref[...], [p[0] for p in pairs], [p[1] for p in pairs], 2)
    se_ref[...] = block
    xa_ref[...], xb_ref[...] = pair_out(w, block[0:2], block[BX - 2 : BX])


def operator_kernel(
    sizes, se_ref, sa_ref, sb_ref, right_ref, de_ref, da_ref, db_ref, slot_ref, offset_ref, gather_ref, xa_ref, xb_ref, sum_ref, we_ref
):
    w, d = lax.axis_index("wide"), lax.axis_index("narrow")
    s_low, s_high = pair_in(w, sa_ref[...], sb_ref[...])
    d_low, d_high = pair_in(w, da_ref[1], db_ref[1])
    search = jnp.concatenate([s_low, se_ref[...], s_high], axis=0)
    diagonal = jnp.concatenate([d_low[None], de_ref[...], d_high[None]], axis=0)
    centre = search[1 : BX + 3]
    image = (6.0 + diagonal) * centre - (search[0 : BX + 2] + search[2 : BX + 4] + roll_sum(centre))
    x = iota(image.shape, 0)
    y = iota(image.shape, 1)
    inside = (y < BY) | ((y == BY) & (d < sizes[1] - 1)) | ((y == YR - 1) & (d > 0))
    inside &= ((x > 0) | (w > 0)) & ((x < BX + 1) | (w < sizes[0] - 1))
    image = jnp.where(inside, image, 0.0)
    we_ref[...] = image
    own = image[1 : BX + 1, 0:BY]
    own_search = se_ref[:, 0:BY, :]
    totals = element_row(own, gather_ref[...]) * (1.0 / 16.0)
    column = to_rows(totals, slot_ref[...], offset_ref[0])
    extra = lanes([total(right_ref[...] * own_search), total(own_search * own)])
    store_sum(sum_ref, project(column, (xa_ref, xb_ref)), extra)


def second_fine_kernel(we_ref, sigma_ref, *rest):
    w, d = lax.axis_index("wide"), lax.axis_index("narrow")
    out_ref, ya_ref, yb_ref, xa_ref, xb_ref = rest[-5:]
    out = fine_solve(we_ref[...].reshape(YW, BZ), sigma_ref[...], rest[:-5])
    out_ref[...] = out
    ya_ref[...], yb_ref[...] = pair_out(d, out_ref[:, 0, :], out_ref[:, BY - 1, :])
    xa_ref[...], xb_ref[...] = pair_out(w, out[0], out[BX - 1])


def second_coarse_kernel(
    sum_ref, fine_ref, fya_ref, fyb_ref, fxa_ref, fxb_ref, right_ref, se_ref, sa_ref, sb_ref, we_ref, de_ref,
    slot_ref, offset_ref, spread_ref, xa_ref, xb_ref, s1_ref, t1_ref, last_ref,
):
    w, d = lax.axis_index("wide"), lax.axis_index("narrow")
    row = jnp.sum(sum_ref[...], axis=0, keepdims=True)
    step = lane(row[:, KCOL:WIDTH], 0) / lane(row[:, KCOL:WIDTH], 1)
    values = to_elements(correct(row[:, 0:KCOL], (xa_ref, xb_ref)), slot_ref[...], offset_ref[0])
    coarse = expand_block(values * (1.0 / 16.0), spread_ref[...])[None]
    own_search = se_ref[:, 0:BY, :]
    own_image = we_ref[1 : BX + 1, 0:BY, :]
    search = own_search - step * (fine_ref[...] + coarse)
    s_low, s_high = pair_in(w, sa_ref[...], sb_ref[...])
    f_low, f_high = pair_in(w, fxa_ref[...], fxb_ref[...])
    x_low = s_low[1, 0:BY] - step * f_low
    x_high = s_high[0, 0:BY] - step * f_high
    g_low, g_high = pair_in(d, fya_ref[...], fyb_ref[...])
    y_low = se_ref[:, YR - 1, :] - step * g_low
    y_high = se_ref[:, BY, :] - step * g_high
    block = extend_y(search, [y_low], [y_high], 1)
    beside = roll_sum(block)[:, 0:BY]
    beside = beside + jnp.concatenate([x_low[None], search[0 : BX - 1]], axis=0)
    beside = beside + jnp.concatenate([search[1:BX], x_high[None]], axis=0)
    image = (6.0 + de_ref[:, 0:BY, :]) * search - beside
    s1_ref[...] = search
    t1_ref[...] = image
    residual = right_ref[...] - step * own_image
    edges = total(coarse[0] * (x_low + x_high))
    edges = edges + total(y_low * coarse[0, 0:1]) + total(y_high * coarse[0, BY - 1 : BY])
    extra = lanes([total(residual * search), total(search * image) + step * edges, total(search * own_image)])
    count = last_ref.shape[0]
    last_ref[:, 0:ELEMS] = jnp.broadcast_to(values, (count, ELEMS))
    last_ref[:, ELEMS:] = jnp.broadcast_to(extra, (count, 128))


def last_kernel(sizes, sum_ref, last_ref, right_ref, se_ref, we_ref, s1_ref, t1_ref, spread_ref, x_ref, r_ref):
    w, d = lax.axis_index("wide"), lax.axis_index("narrow")
    groups = sizes[1]
    count = sizes[0] * groups
    product = jnp.sum(sum_ref[:, KCOL:WIDTH], axis=0, keepdims=True)
    product, bottom = lane(product, 0), lane(product, 1)
    step = product / bottom
    z = last_ref[:, 0:ELEMS]
    rows = iota((count, ELEMS), 0)
    at = iota((count, ELEMS), 1)
    faces = jnp.where(rows < count - groups, z * pltpu.roll(z, count - groups, 0), 0.0)
    across = pltpu.roll(pltpu.roll(z, count - 1, 0), EZ, 1)
    faces = faces + jnp.where((lax.rem(rows, groups) < groups - 1) & (at >= EZ), z * across, 0.0)
    sums = jnp.sum(last_ref[:, ELEMS:], axis=0, keepdims=True)
    next_product = lane(sums, 0)
    quadratic = lane(sums, 1) - step * step * 0.5 * total(faces)
    cross = lane(sums, 2)
    me = w * groups + d
    picked = []
    for index, there in ((me - groups, w > 0), (me + groups, w < sizes[0] - 1), (me - 1, d > 0), (me + 1, d < groups - 1)):
        picked.append(jnp.sum(jnp.where((rows == index) & there, z, 0.0), axis=0, keepdims=True))
    wide = expand_rows(jnp.concatenate(picked, axis=0), spread_ref[...]) * (1.0 / 16.0)
    layers = []
    for i in range(2):
        layers.append(
            jnp.concatenate(
                [jnp.broadcast_to(wide[i : i + 1, 0:BZ], (8, BZ)), jnp.broadcast_to(wide[i : i + 1, BZ:], (8, BZ))], axis=0
            )
        )
    shape = (BX, BY, BZ)
    x, y = iota(shape, 0), iota(shape, 1)
    missing = jnp.where(x == 0, layers[0][None], 0.0) + jnp.where(x == BX - 1, layers[1][None], 0.0)
    missing = missing + jnp.where(y == 0, wide[2:3, BZ:][None], 0.0) + jnp.where(y == BY - 1, wide[3:4, 0:BZ][None], 0.0)
    ratio = next_product / product
    curvature = quadratic + 2.0 * ratio * cross + ratio * ratio * bottom
    step_next = next_product / curvature
    own_search = se_ref[:, 0:BY, :]
    own_image = we_ref[1 : BX + 1, 0:BY, :]
    direction = s1_ref[...] + ratio * own_search
    image = t1_ref[...] + step * missing + ratio * own_image
    x_ref[...] = step * own_search + step_next * direction
    r_ref[...] = (right_ref[...] - step * own_image) - step_next * image


def call(kernel, shapes, args, smem=()):
    specs = [pl.BlockSpec(memory_space=pltpu.SMEM if i in smem else pltpu.VMEM) for i in range(len(args))]
    return pl.pallas_call(
        kernel,
        out_shape=[jax.ShapeDtypeStruct(shape, F32) for shape in shapes],
        in_specs=specs,
        out_specs=[pl.BlockSpec(memory_space=pltpu.VMEM)] * len(shapes),
        compiler_params=pltpu.CompilerParams(vmem_limit_bytes=48 * 1024 * 1024),
    )(*args)


def pair_swap(first, second, axis):
    size = lax.axis_size(axis)
    received = []
    for value, begin in ((first, 0), (second, 1)):
        perm = []
        for i in range(begin, size - 1, 2):
            perm += [(i, i + 1), (i + 1, i)]
        received.append(lax.ppermute(value, axis, perm) if perm else jnp.zeros_like(value))
    return received


def everywhere(rows):
    return lax.all_to_all(rows, AXES, split_axis=0, concat_axis=0, tiled=True)


def body(right, diagonal, coarse_slot, factor):
    sizes = (lax.axis_size("wide"), lax.axis_size("narrow"))
    groups = sizes[1]
    count = sizes[0] * groups
    d = lax.axis_index("narrow")
    fine, gather, spread = tables()
    fine = [jnp.asarray(c) for c in fine]
    gather, spread = jnp.asarray(gather), jnp.asarray(spread)
    slots = coarse_slot.reshape(1, ELEMS)
    share = ELEMS // groups
    swapped = groups == 2
    if swapped:
        kept = lax.dynamic_slice_in_dim(factor, d * share, share, 0)
        sent = lax.dynamic_slice_in_dim(factor, (1 - d) * share, share, 0)
        owned = (kept, lax.ppermute(sent, "narrow", [(0, 1), (1, 0)]))
        offset = (d * share).reshape(1).astype(jnp.int32)
        first = (factor,)
    else:
        ours = lax.all_to_all(factor.reshape(groups, share, KCOL), "narrow", split_axis=0, concat_axis=0, tiled=True)
        ours = ours.reshape(ELEMS, KCOL)
        owned = (ours[: ELEMS // 2], ours[ELEMS // 2 :])
        offset = jnp.zeros((1,), jnp.int32)
        first = (ours,)

    block, layer, extended = (BX, BY, BZ), (YR, BZ), (BX, YR, BZ)
    y_shape, x_shape = (3, BX, BZ), (2, YR, BZ)
    c_row, sigma, ya, yb = call(start_kernel, [(1, ELEMS), (1, ELEMS), y_shape, y_shape], [right, diagonal, slots, gather])
    ya, yb = pair_swap(ya, yb, "narrow")

    def project_first(c_ref, ra_ref, rb_ref, right_ref, diag_ref, x_ref, *outs):
        half = ELEMS // 2
        project_kernel(
            c_ref, ra_ref, rb_ref, right_ref, diag_ref, x_ref.at[0:half], x_ref.at[half:ELEMS], swapped, *outs
        )

    sums, right_e, diag_e, xa, xb = call(
        project_first, [(count, WIDTH), extended, extended, x_shape, x_shape], [c_row, ya, yb, right, diagonal, *first]
    )
    sums = everywhere(sums)
    xa, xb = pair_swap(xa, xb, "wide")
    (solved,) = call(first_fine_kernel, [block], [right_e, xa, xb, sigma, *fine])
    search, ya, yb = call(
        first_coarse_kernel, [block, (2, BX, BZ), (2, BX, BZ)], [sums, solved, slots, offset, spread, *owned], (3,)
    )
    ya, yb = pair_swap(ya, yb, "narrow")
    search_e, sa, sb = call(extend_kernel, [extended, (2,) + layer, (2,) + layer], [search, ya, yb])
    sa, sb = pair_swap(sa, sb, "wide")
    sums, image_e = call(
        functools.partial(operator_kernel, sizes),
        [(count, WIDTH), (BX + 2, YR, BZ)],
        [search_e, sa, sb, right, diag_e, xa, xb, slots, offset, gather, *owned],
        (8,),
    )
    sums = everywhere(sums)
    solved, ya, yb, fa, fb = call(
        second_fine_kernel, [block, (BX, BZ), (BX, BZ), (BY, BZ), (BY, BZ)], [image_e, sigma, *fine]
    )
    ya, yb = pair_swap(ya, yb, "narrow")
    fa, fb = pair_swap(fa, fb, "wide")
    search_next, image_next, last = call(
        second_coarse_kernel,
        [block, block, (count, 256)],
        [sums, solved, ya, yb, fa, fb, right, search_e, sa, sb, image_e, diag_e, slots, offset, spread, *owned],
        (13,),
    )
    last = everywhere(last)
    return tuple(
        call(
            functools.partial(last_kernel, sizes),
            [block, block],
            [sums, last, right, search_e, image_e, search_next, image_next, spread],
        )
    )


def solution(mesh):
    in_specs = (
        P("wide", "narrow", None),
        P("wide", "narrow", None),
        P("wide", "narrow", None),
        P(("wide", "narrow"), None),
    )
    out_specs = (P("wide", "narrow", None), P("wide", "narrow", None))
    return jax.shard_map(body, mesh=mesh, in_specs=in_specs, out_specs=out_specs, check_vma=False)
```

```python
import functools

import jax
import jax.numpy as jnp
import numpy as np
from jax import lax
from jax.experimental import pallas as pl
from jax.experimental.pallas import tpu as pltpu
from jax.sharding import PartitionSpec as P

F32 = jnp.float32
BF16 = jnp.bfloat16
BX, BY, BZ = 8, 16, 512
EY, EZ = 2, 64
ELEMS = EY * EZ
YR = 24
YW = YR * (BX + 2)
AB = 208
KCOL = 2048
WIDTH = KCOL + 128
AXES = ("wide", "narrow")


def split_const(values):
    high = values.astype(jnp.bfloat16)
    low = (values - high.astype(np.float64)).astype(jnp.bfloat16)
    return high, low


@functools.lru_cache(maxsize=None)
def tables():
    index = np.arange(10, dtype=np.float64)
    basis = np.sqrt(2.0 / 11.0) * np.sin(np.pi * (index[:, None] + 1.0) * (index[None, :] + 1.0) / 11.0)
    values = 2.0 - 2.0 * np.cos(np.pi * (index + 1.0) / 11.0)
    to_z = np.zeros((BZ, 10 * EZ))
    from_z = np.zeros((10 * EZ, BZ))
    for e in range(EZ):
        for k in range(10):
            z = 8 * e + k - 1
            if 0 <= z < BZ:
                to_z[z, e::EZ] = basis[k]
            if 1 <= k <= 8:
                from_z[e::EZ, z] = basis[k]
    to_xy = np.zeros((10, EY, 10, 10, YR))
    from_xy = np.zeros((BX, BY, 10, EY, 10))
    for e in range(EY):
        for j in range(10):
            y = 8 * e + j - 1
            to_xy[:, e, :, :, y % YR] += basis.T[:, None, :] * basis[j][None, :, None]
            if 1 <= j <= 8:
                from_xy[:, y, :, e, :] = basis[1:9, :, None] * basis[j][None, None, :]
    to_xy = np.pad(to_xy.reshape(200, YW), ((0, AB - 200), (0, 0)))
    from_xy = np.pad(from_xy.reshape(BX * BY, 200), ((0, 0), (0, AB - 200)))
    column = np.zeros((AB, 128), np.float32)
    grid = np.zeros((10, EY, 10, 2))
    grid[..., 0] = values[:, None, None] + values[None, None, :]
    grid[..., 1] = np.arange(EY)[None, :, None]
    column[:200, :2] = grid.reshape(200, 2)
    column[200:, 0] = 1.0
    line = np.repeat(values, EZ)[None, :].astype(np.float32)
    return split_const(to_xy) + split_const(to_z) + split_const(from_xy) + split_const(from_z) + (column, line)


def dot(a, b):
    return jnp.dot(a, b, preferred_element_type=F32)


def split2(x):
    high = x.astype(BF16)
    return high, (x - high.astype(F32)).astype(BF16)


def split3(x):
    high = x.astype(BF16)
    rest = x - high.astype(F32)
    middle = rest.astype(BF16)
    return high, middle, (rest - middle.astype(F32)).astype(BF16)


def dot3(a, b):
    return dot(a[0], b[0]) + dot(a[0], b[1]) + dot(a[1], b[0])


def iota(shape, axis):
    return lax.broadcasted_iota(jnp.int32, shape, axis)


def total(x):
    while x.ndim > 2:
        x = jnp.sum(x, axis=0)
    return jnp.sum(jnp.sum(x, axis=0, keepdims=True), axis=1, keepdims=True)


def gather_table():
    shape = (BZ, EY * ELEMS)
    node, at = iota(shape, 0), iota(shape, 1)
    return jnp.where(at == node // 8 + (at // ELEMS) * (ELEMS + EZ), 1.0, 0.0).astype(BF16)


def spread_table():
    shape = (ELEMS, EY * BZ)
    element, at = iota(shape, 0), iota(shape, 1)
    return jnp.where(at // 8 == element, 1.0, 0.0).astype(BF16)


def element_row(field):
    parts = jnp.concatenate(split3(jnp.sum(field, axis=0)), axis=0)
    sums = dot(parts, gather_table())
    sums = sums[0:16] + sums[16:32] + sums[32:48]
    return jnp.sum(sums[0:8, 0:ELEMS], axis=0, keepdims=True) + jnp.sum(sums[8:16, ELEMS:], axis=0, keepdims=True)


def expand_rows(rows):
    count = rows.shape[0]
    tall = jnp.broadcast_to(rows, (16, ELEMS)) if count == 1 else jnp.concatenate([rows, jnp.zeros((16 - count, ELEMS), F32)], axis=0)
    wide = dot(jnp.concatenate(split3(tall), axis=0), spread_table())
    return (wide[0:16] + wide[16:32] + wide[32:48])[0:count]


def expand_block(row):
    wide = expand_rows(row)
    low = jnp.broadcast_to(wide[:, 0:BZ], (8, BZ))
    high = jnp.broadcast_to(wide[:, BZ:], (8, BZ))
    return jnp.concatenate([low, high], axis=0)


def slot_mask(slots, offset):
    slot_of_row = lax.rem(iota((ELEMS, ELEMS), 0) + offset, ELEMS)
    return slot_of_row == slots


def to_rows(element_values, slots, offset):
    return jnp.sum(jnp.where(slot_mask(slots, offset), element_values, 0.0), axis=1, keepdims=True)


def to_elements(row_values, slots, offset):
    return jnp.sum(jnp.where(slot_mask(slots, offset), row_values, 0.0), axis=0, keepdims=True)


def project(column, parts):
    out = 0.0
    at = 0
    for part in parts:
        size = part.shape[0]
        out = out + jnp.sum(column[at : at + size] * part[...], axis=0, keepdims=True)
        at += size
    return out


def correct(row, parts):
    out = []
    for part in parts:
        products = part[...] * row
        folded = products[:, 0:128]
        for at in range(128, KCOL, 128):
            folded = folded + products[:, at : at + 128]
        out.append(jnp.sum(folded, axis=1, keepdims=True))
    return jnp.concatenate(out, axis=0)


def store_sum(out_ref, first, second):
    count, _, width = out_ref.shape
    cut = width - 128
    out_ref[:, :, 0:cut] = jnp.broadcast_to(first[None], (count, 1, cut))
    out_ref[:, :, cut:width] = jnp.broadcast_to(second[None], (count, 1, 128))


def lanes(values):
    at = iota((1, 128), 1)
    row = jnp.zeros((1, 128), F32)
    for i, value in enumerate(values):
        row = jnp.where(at == i, value, row)
    return row


def lane(row, i):
    return jnp.sum(jnp.where(iota(row.shape, 1) == i, row, 0.0), axis=1, keepdims=True)


def odd(index):
    return lax.rem(index, 2) == 1


def pair_out(index, low, high):
    return jnp.where(odd(index), low, high), jnp.where(odd(index), high, low)


def pair_in(index, first, second):
    return jnp.where(odd(index), first, second), jnp.where(odd(index), second, first)


def extend_y(block, low, high, depth):
    at = iota((8, BZ), 0)
    tails = []
    for x in range(block.shape[0]):
        tail = jnp.zeros((8, BZ), F32)
        for i in range(depth):
            tail = jnp.where(at == i, high[i][x : x + 1], tail)
            tail = jnp.where(at == 8 - depth + i, low[i][x : x + 1], tail)
        tails.append(tail)
    return jnp.concatenate([block, jnp.stack(tails)], axis=1)


def roll_sum(x):
    count, rows, _ = x.shape
    beside = pltpu.roll(x, 1, 1) + pltpu.roll(x, rows - 1, 1)
    flat = x.reshape(count * rows, BZ)
    at = iota(flat.shape, 1)
    beside_z = jnp.where(at == 0, 0.0, pltpu.roll(flat, 1, 1)) + jnp.where(at == BZ - 1, 0.0, pltpu.roll(flat, BZ - 1, 1))
    return beside + beside_z.reshape(x.shape)


def fine_solve(rows, sigma, consts):
    wh, wl, th, tl, vh, vl, uh, ul, column, line = consts
    spectra = split2(dot3((wh.here()[...], wl.here()[...]), split2(rows)))
    column = column.here()
    sig = jnp.where(column[:, 1:2] == 0.0, tile_lanes(sigma, 0), tile_lanes(sigma, 1))
    inverse = 1.0 / (column[:, 0:1] + line.here()[...] + sig)
    spectra = dot3(spectra, (th.here()[...], tl.here()[...])) * inverse
    nodal = dot3((vh.here()[...], vl.here()[...]), split2(spectra))
    return dot3(split2(nodal), (uh.here()[...], ul.here()[...])).reshape(BX, BY, BZ)


def tile_lanes(sigma, e):
    low = iota((1, ELEMS), 1) < EZ
    rolled = pltpu.roll(sigma, EZ, 1)
    both = jnp.where(low, sigma, rolled) if e == 0 else jnp.where(low, rolled, sigma)
    return jnp.concatenate([both] * 5, axis=1)


def eye_mask():
    return iota((ELEMS, ELEMS), 0) == iota((ELEMS, ELEMS), 1)


def row_to_column(row):
    return jnp.sum(jnp.where(eye_mask(), row, 0.0), axis=1, keepdims=True)


def column_to_row(column):
    return jnp.sum(jnp.where(eye_mask(), column, 0.0), axis=0, keepdims=True)


def pad_tile(rows):
    at = iota((8, ELEMS), 0)
    tile = jnp.zeros((8, ELEMS), F32)
    for i, row in enumerate(rows):
        tile = jnp.where(at == i, row, tile)
    return jnp.concatenate([tile, jnp.zeros((8, BZ - ELEMS), F32)], axis=1)


def start_kernel(swapped, late, factor, right, diagonal, slots, c, ya, yb, ends, factor_here, *sent):
    d = lax.axis_index("narrow")
    half = ELEMS // 2
    late.start(factor, factor_here)
    if swapped:
        late.start(factor.at[pl.ds(pl.multiple_of((1 - d) * half, half), half)], sent[0])
    row = column_to_row(to_rows(element_row(right.here()[...]) * (1.0 / 16.0), slots[...], 0))
    c[...] = row
    for i, source in enumerate((right, diagonal)):
        ref = source.here()
        ya[i], yb[i] = pair_out(d, ref[:, 0, :], ref[:, BY - 1, :])
        ends[i, 0], ends[i, 1] = ref[0], ref[BX - 1]
    ya[2] = pad_tile([row, slots[...].astype(F32)])
    yb[2] = jnp.zeros((8, BZ), F32)


def project_kernel(swapped, late, c, ra, rb, ends, factor, sums, xa, xb):
    w, d = lax.axis_index("wide"), lax.axis_index("narrow")
    row = c[...]
    if swapped:
        half = ELEMS // 2
        other = pltpu.roll(ra[2, 0:1, 0:ELEMS], half, 1)
        row = jnp.where(iota((1, ELEMS), 1) // half == d, row, other)
    store_sum(sums, project(row_to_column(row), (factor,)), jnp.zeros((1, 128), F32))
    for i in range(2):
        low, high = pair_in(d, ra[i], rb[i])
        layers = [
            extend_y(ends[i, end][None], [low[x : x + 1]], [high[x : x + 1]], 1)[0] for end, x in ((0, 0), (1, BX - 1))
        ]
        xa[i], xb[i] = pair_out(w, *layers)


def widened(block, ya, yb, xa, xb, i):
    w, d = lax.axis_index("wide"), lax.axis_index("narrow")
    low, high = pair_in(d, ya[i], yb[i])
    x_low, x_high = pair_in(w, xa[i], xb[i])
    return jnp.concatenate([x_low[None], extend_y(block, [low], [high], 1), x_high[None]], axis=0)


def first_fine_kernel(late, factor, right, diagonal, *rest):
    ya, yb, xa, xb = rest[10:14]
    solved, sigma_out, factor_here = rest[14:]
    late.start(factor, factor_here)
    rows = widened(right.here()[...], ya, yb, xa, xb, 0)
    sigma = element_row(diagonal.here()[...]) * (1.0 / 512.0)
    sigma_out[...] = sigma
    solved[...] = fine_solve(rows.reshape(YW, BZ), sigma, rest[:10])


def first_coarse_kernel(swapped, late, sums, solved, slots, factor, ya, yb):
    d = lax.axis_index("narrow")
    row = jnp.sum(sums[...], axis=0)[:, 0:KCOL]
    column = correct(row, (factor,))
    for i in range(2):
        ya[i], yb[i] = pair_out(d, solved[:, i, :], solved[:, BY - 2 + i, :])
    ya[2] = pad_tile([column_to_row(column) if swapped else to_elements(column, slots[...], 0)])
    yb[2] = ya[2]


def extend_kernel(swapped, late, solved, slots, ra_first, own_ref, ra, rb, search, xa, xb):
    w, d = lax.axis_index("wide"), lax.axis_index("narrow")
    groups = lax.axis_size("narrow")
    own = own_ref[2, 0:1, 0:ELEMS]
    theirs = ra[2, 0:1, 0:ELEMS]
    if swapped:
        half = ELEMS // 2
        at = iota((1, ELEMS), 1) // half
        other = jnp.where(at == d, pltpu.roll(own, half, 1), theirs)
        own = jnp.where(at == d, own, pltpu.roll(theirs, half, 1))
        own = to_elements(row_to_column(own), slots[...], 0)
        other = to_elements(row_to_column(other), ra_first[2, 1:2, 0:ELEMS].astype(jnp.int32), 0)
        values_low, values_high = other, other
    else:
        values_low, values_high = pair_in(d, theirs, rb[2, 0:1, 0:ELEMS])
    values_low = jnp.where(d > 0, values_low, 0.0)
    values_high = jnp.where(d < groups - 1, values_high, 0.0)
    wide = expand_rows(jnp.concatenate([own, values_low, values_high], axis=0)) * (1.0 / 16.0)
    coarse = jnp.concatenate(
        [jnp.broadcast_to(wide[0:1, 0:BZ], (8, BZ)), jnp.broadcast_to(wide[0:1, BZ:], (8, BZ))], axis=0
    )
    low, high = [], []
    for i in range(2):
        one, two = pair_in(d, ra[i], rb[i])
        low.append(one + wide[1:2, BZ:])
        high.append(two + wide[2:3, 0:BZ])
    block = extend_y(solved[...] + coarse[None], low, high, 2)
    search[...] = block
    xa[...], xb[...] = pair_out(w, block[0:2], block[BX - 2 : BX])


def operator_kernel(
    swapped, sizes, late, factor, right, diagonal, search, sa, sb, ya, yb, xa, xb, slots, received, sums, image_out, halo, kept
):
    w, d = lax.axis_index("wide"), lax.axis_index("narrow")
    half = ELEMS // 2
    offset = d * half if swapped else 0
    load = late.start(factor.at[pl.ds(pl.multiple_of(offset, half), half)] if swapped else factor.at[0:half], kept)
    s_low, s_high = pair_in(w, sa[...], sb[...])
    vector = jnp.concatenate([s_low, search[...], s_high], axis=0)
    coefficient = widened(diagonal.here()[...], ya, yb, xa, xb, 1)
    centre = vector[1 : BX + 3]
    image = (6.0 + coefficient) * centre - (vector[0 : BX + 2] + vector[2 : BX + 4] + roll_sum(centre))
    x = iota(image.shape, 0)
    y = iota(image.shape, 1)
    inside = (y < BY) | ((y == BY) & (d < sizes[1] - 1)) | ((y == YR - 1) & (d > 0))
    inside &= ((x > 0) | (w > 0)) & ((x < BX + 1) | (w < sizes[0] - 1))
    image = jnp.where(inside, image, 0.0)
    image_out[...] = image
    halo[0:BY] = s_low[1, 0:BY]
    halo[BY : 2 * BY] = s_high[0, 0:BY]
    halo[2 * BY : 2 * BY + 8] = search[:, YR - 1, :]
    halo[2 * BY + 8 : 3 * BY] = search[:, BY, :]
    own = image[1 : BX + 1, 0:BY]
    own_search = search[:, 0:BY, :]
    column = to_rows(element_row(own) * (1.0 / 16.0), slots[...], offset)
    extra = lanes([total(right.here()[...] * own_search), total(own_search * own)])
    load.wait()
    store_sum(sums, project(column, (kept, received)), extra)


def second_fine_kernel(swapped, late, factor, *rest):
    w, d = lax.axis_index("wide"), lax.axis_index("narrow")
    image, sigma, received = rest[10:13]
    solved, ya, yb, xa, xb, owned = rest[13:]
    half = ELEMS // 2
    at = pl.multiple_of(d * half, half) if swapped else 0
    late.start(factor.at[pl.ds(at, half)], owned.at[0:half])
    late.start(received, owned.at[half:ELEMS])
    out = fine_solve(image[...].reshape(YW, BZ), sigma[...], rest[:10])
    solved[...] = out
    ya[...], yb[...] = pair_out(d, solved[:, 0, :], solved[:, BY - 1, :])
    xa[...], xb[...] = pair_out(w, out[0], out[BX - 1])


def second_coarse_kernel(
    swapped, late, right, diagonal, sums, solved, fya, fyb, fxa, fxb, search, halo, image, slots, owned,
    search_out, image_out, last, products,
):
    w, d = lax.axis_index("wide"), lax.axis_index("narrow")
    offset = d * (ELEMS // 2) if swapped else 0
    row = jnp.sum(sums[...], axis=0)
    products[...] = row[:, KCOL:WIDTH]
    step = lane(row[:, KCOL:WIDTH], 0) / lane(row[:, KCOL:WIDTH], 1)
    values = to_elements(correct(row[:, 0:KCOL], (owned,)), slots[...], offset)
    coarse = expand_block(values * (1.0 / 16.0))
    own_search = search[:, 0:BY, :]
    own_image = image[1 : BX + 1, 0:BY, :]
    vector = own_search - step * (solved[...] + coarse[None])
    f_low, f_high = pair_in(w, fxa[...], fxb[...])
    x_low = halo[0:BY] - step * f_low
    x_high = halo[BY : 2 * BY] - step * f_high
    g_low, g_high = pair_in(d, fya[...], fyb[...])
    y_low = halo[2 * BY : 2 * BY + 8] - step * g_low
    y_high = halo[2 * BY + 8 : 3 * BY] - step * g_high
    beside = roll_sum(extend_y(vector, [y_low], [y_high], 1))[:, 0:BY]
    beside = beside + jnp.concatenate([x_low[None], vector[0 : BX - 1]], axis=0)
    beside = beside + jnp.concatenate([vector[1:BX], x_high[None]], axis=0)
    next_image = (6.0 + diagonal.here()[...]) * vector - beside
    search_out[...] = vector
    image_out[...] = next_image
    residual = right.here()[...] - step * own_image
    edges = total(coarse * (x_low + x_high)) + total(y_low * coarse[0:1]) + total(y_high * coarse[BY - 1 : BY])
    store_sum(
        last,
        values,
        lanes([total(residual * vector), total(vector * next_image) + step * edges, total(vector * own_image)]),
    )


def last_kernel(sizes, late, right, products, last, search, image, next_search, next_image, x_out, r_out):
    w, d = lax.axis_index("wide"), lax.axis_index("narrow")
    groups = sizes[1]
    count = sizes[0] * groups
    product, bottom = lane(products[...], 0), lane(products[...], 1)
    step = product / bottom
    z = last[:, 0, 0:ELEMS]
    rows = iota((count, ELEMS), 0)
    at = iota((count, ELEMS), 1)
    faces = jnp.where(rows < count - groups, z * pltpu.roll(z, count - groups, 0), 0.0)
    across = pltpu.roll(pltpu.roll(z, count - 1, 0), EZ, 1)
    faces = faces + jnp.where((lax.rem(rows, groups) < groups - 1) & (at >= EZ), z * across, 0.0)
    sums = jnp.sum(last[:, :, ELEMS:], axis=0)
    next_product = lane(sums, 0)
    quadratic = lane(sums, 1) - step * step * 0.5 * total(faces)
    cross = lane(sums, 2)
    me = w * groups + d
    picked = []
    for index, there in ((me - groups, w > 0), (me + groups, w < sizes[0] - 1), (me - 1, d > 0), (me + 1, d < groups - 1)):
        picked.append(jnp.sum(jnp.where((rows == index) & there, z, 0.0), axis=0, keepdims=True))
    wide = expand_rows(jnp.concatenate(picked, axis=0)) * (1.0 / 16.0)
    layers = []
    for i in range(2):
        low = jnp.broadcast_to(wide[i : i + 1, 0:BZ], (8, BZ))
        high = jnp.broadcast_to(wide[i : i + 1, BZ:], (8, BZ))
        layers.append(jnp.concatenate([low, high], axis=0)[None])
    shape = (BX, BY, BZ)
    x, y = iota(shape, 0), iota(shape, 1)
    missing = jnp.where(x == 0, layers[0], 0.0) + jnp.where(x == BX - 1, layers[1], 0.0)
    missing = missing + jnp.where(y == 0, wide[2:3, BZ:][None], 0.0) + jnp.where(y == BY - 1, wide[3:4, 0:BZ][None], 0.0)
    ratio = next_product / product
    curvature = quadratic + 2.0 * ratio * cross + ratio * ratio * bottom
    step_next = next_product / curvature
    own_search = search[:, 0:BY, :]
    own_image = image[1 : BX + 1, 0:BY, :]
    direction = next_search[...] + ratio * own_search
    total_image = next_image[...] + step * missing + ratio * own_image
    x_out[...] = step * own_search + step_next * direction
    r_out[...] = (right.here()[...] - step * own_image) - step_next * total_image


class Loaded:
    def __init__(self, copy, ref):
        self.copy, self.ref, self.ready = copy, ref, False

    def wait(self):
        if not self.ready:
            self.copy.wait()
            self.ready = True

    def here(self):
        self.wait()
        return self.ref


class Copies:
    def __init__(self, semaphores):
        self.semaphores, self.all = semaphores, []

    def start(self, source, target):
        copy = pltpu.make_async_copy(source, target, self.semaphores.at[len(self.all)])
        copy.start()
        self.all.append(Loaded(copy, target))
        return self.all[-1]

    def finish(self):
        for loaded in self.all:
            loaded.wait()


def call(kernel, outs, far=(), late=(), near=(), far_outs=(), scratch=(), final=False):
    counts = (len(far), len(late), len(near), len(outs) + len(far_outs), len(scratch), len(late))

    def run(*refs):
        parts, at = [], 0
        for size in counts:
            parts.append(refs[at : at + size])
            at += size
        copies = Copies(refs[at])
        loaded = [copies.start(source, target) for source, target in zip(parts[1], parts[5])]
        kernel(copies, *parts[0], *loaded, *parts[2], *parts[3], *parts[4])
        copies.finish()

    near_shape = jax.ShapeDtypeStruct if final else pltpu.VMEM
    spaces = [pltpu.HBM] * (len(far) + len(late)) + [pltpu.VMEM] * len(near)
    out_spaces = [pltpu.VMEM] * len(outs) + [pltpu.HBM] * len(far_outs)
    return pl.pallas_call(
        run,
        out_shape=[*(near_shape(shape, F32) for shape in outs), *(pltpu.HBM(shape, F32) for shape in far_outs)],
        in_specs=[pl.BlockSpec(memory_space=space) for space in spaces],
        out_specs=[pl.BlockSpec(memory_space=space) for space in out_spaces],
        scratch_shapes=[
            *(pltpu.VMEM(shape, F32) for shape in scratch),
            *(pltpu.VMEM(array.shape, array.dtype) for array in late),
            pltpu.SemaphoreType.DMA((len(late) + 3,)),
        ],
        compiler_params=pltpu.CompilerParams(vmem_limit_bytes=16 * 1024 * 1024),
    )(*(pltpu.with_memory_space_constraint(array, pltpu.HBM) for array in (*far, *late)), *near)


def pair_swap(first, second, axis):
    size = lax.axis_size(axis)
    received = []
    for value, begin in ((first, 0), (second, 1)):
        perm = []
        for i in range(begin, size - 1, 2):
            perm += [(i, i + 1), (i + 1, i)]
        received.append(lax.ppermute(value, axis, perm) if perm else jnp.zeros_like(value))
    return received


def everywhere(rows):
    return lax.all_to_all(rows, AXES, split_axis=0, concat_axis=0, tiled=True)


def body(right, diagonal, coarse_slot, factor):
    sizes = (lax.axis_size("wide"), lax.axis_size("narrow"))
    groups = sizes[1]
    count = sizes[0] * groups
    fine = [jnp.asarray(c) for c in tables()]
    slots = coarse_slot.reshape(1, ELEMS)
    swapped = groups == 2
    if not swapped:
        factor = factor.reshape(groups, ELEMS // groups, KCOL)
        factor = lax.all_to_all(factor, "narrow", split_axis=0, concat_axis=0, tiled=True).reshape(ELEMS, KCOL)
    part = functools.partial

    block, layer, extended = (BX, BY, BZ), (YR, BZ), (BX, YR, BZ)
    y_shape, x_shape, half, whole = (3, BX, BZ), (2, YR, BZ), (ELEMS // 2, KCOL), (ELEMS, KCOL)
    c, ya, yb, ends, near_factor, *sent = call(
        part(start_kernel, swapped),
        [(1, ELEMS), y_shape, y_shape, (2, 2, BY, BZ), whole],
        far=[factor],
        late=[right, diagonal],
        near=[slots],
        far_outs=[half] * swapped,
    )
    ya, yb = pair_swap(ya, yb, "narrow")
    received = lax.ppermute(sent[0], "narrow", [(0, 1), (1, 0)]) if swapped else factor[ELEMS // 2 :]
    sums, xa, xb = call(
        part(project_kernel, swapped), [(count, 1, WIDTH), x_shape, x_shape], near=[c, ya, yb, ends, near_factor]
    )
    sums = everywhere(sums)
    xa, xb = pair_swap(xa, xb, "wide")
    solved, sigma, near_factor = call(
        first_fine_kernel,
        [block, (1, ELEMS), whole],
        far=[factor],
        late=[right, diagonal, *fine],
        near=[ya, yb, xa, xb],
    )
    ta, tb = call(part(first_coarse_kernel, swapped), [y_shape, y_shape], near=[sums, solved, slots, near_factor])
    ra, rb = pair_swap(ta, tb, "narrow")
    search, sa, sb = call(
        part(extend_kernel, swapped), [extended, (2,) + layer, (2,) + layer], near=[solved, slots, ya, ta, ra, rb]
    )
    sa, sb = pair_swap(sa, sb, "wide")
    sums, image, halo = call(
        part(operator_kernel, swapped, sizes),
        [(count, 1, WIDTH), (BX + 2, YR, BZ), (3 * BY, BZ)],
        far=[factor],
        late=[right, diagonal],
        near=[search, sa, sb, ya, yb, xa, xb, slots, received],
        scratch=[half],
    )
    sums = everywhere(sums)
    solved, ya, yb, fa, fb, owned = call(
        part(second_fine_kernel, swapped),
        [block, (BX, BZ), (BX, BZ), (BY, BZ), (BY, BZ), whole],
        far=[factor],
        late=fine,
        near=[image, sigma, received],
    )
    ya, yb = pair_swap(ya, yb, "narrow")
    fa, fb = pair_swap(fa, fb, "wide")
    next_search, next_image, last, products = call(
        part(second_coarse_kernel, swapped),
        [block, block, (count, 1, 2 * ELEMS), (1, 128)],
        late=[right, diagonal],
        near=[sums, solved, ya, yb, fa, fb, search, halo, image, slots, owned],
    )
    last = everywhere(last)
    return tuple(
        call(
            part(last_kernel, sizes),
            [block, block],
            late=[right],
            near=[products, last, search, image, next_search, next_image],
            final=True,
        )
    )


def solution(mesh):
    in_specs = (
        P("wide", "narrow", None),
        P("wide", "narrow", None),
        P("wide", "narrow", None),
        P(("wide", "narrow"), None),
    )
    out_specs = (P("wide", "narrow", None), P("wide", "narrow", None))
    return jax.shard_map(body, mesh=mesh, in_specs=in_specs, out_specs=out_specs, check_vma=False)
```

```python
import functools

import jax
import jax.numpy as jnp
import numpy as np
from jax import lax
from jax.experimental import pallas as pl
from jax.experimental.pallas import tpu as pltpu
from jax.sharding import PartitionSpec as P

F32 = jnp.float32
BF16 = jnp.bfloat16
BX, BY, BZ = 8, 16, 512
EY, EZ = 2, 64
ELEMS = EY * EZ
YR = 24
YW = YR * (BX + 2)
AB = 208
HZ = 256
HW = 384
KCOL = 2048
WIDTH = KCOL + 128
AXES = ("wide", "narrow")


def split_const(values):
    high = values.astype(jnp.bfloat16)
    low = (values - high.astype(np.float64)).astype(jnp.bfloat16)
    return high, low


@functools.lru_cache(maxsize=None)
def tables():
    index = np.arange(10, dtype=np.float64)
    basis = np.sqrt(2.0 / 11.0) * np.sin(np.pi * (index[:, None] + 1.0) * (index[None, :] + 1.0) / 11.0)
    values = 2.0 - 2.0 * np.cos(np.pi * (index + 1.0) / 11.0)
    to_z = np.zeros((HZ, HW))
    from_z = np.zeros((HW, HZ))
    beyond = np.zeros((8, HW), np.float32)
    last = HZ // 8 - 1
    for e in range(last + 1):
        at = slice(e, 10 * (last + 1), last + 1)
        for k in range(10):
            z = 8 * e + k - 1
            if 0 <= z < HZ:
                to_z[z, at] = basis[k]
            if 1 <= k <= 8:
                from_z[at, z] = basis[k]
    beyond[0, last : 10 * (last + 1) : last + 1] = basis[9]
    beyond[1, 0 : 10 * (last + 1) : last + 1] = basis[0]
    beyond[2] = 1.0
    beyond[2, : 10 * (last + 1)] = np.repeat(values, last + 1)
    to_xy = np.zeros((10, EY, 10, 10, YR))
    from_xy = np.zeros((BX, BY, 10, EY, 10))
    for e in range(EY):
        for j in range(10):
            y = 8 * e + j - 1
            to_xy[:, e, :, :, y % YR] += basis.T[:, None, :] * basis[j][None, :, None]
            if 1 <= j <= 8:
                from_xy[:, y, :, e, :] = basis[1:9, :, None] * basis[j][None, None, :]
    to_xy = np.pad(to_xy.reshape(200, YW), ((0, AB - 200), (0, 0)))
    from_xy = np.pad(from_xy.reshape(BX * BY, 200), ((0, 0), (0, AB - 200)))
    column = np.zeros((AB, 128), np.float32)
    grid = np.zeros((10, EY, 10, 2))
    grid[..., 0] = values[:, None, None] + values[None, None, :]
    grid[..., 1] = np.arange(EY)[None, :, None]
    column[:200, :2] = grid.reshape(200, 2)
    column[200:, 0] = 1.0
    return split_const(to_xy) + split_const(to_z) + split_const(from_xy) + split_const(from_z) + (column, beyond)


def dot(a, b):
    return jnp.dot(a, b, preferred_element_type=F32)


def split2(x):
    high = x.astype(BF16)
    return high, (x - high.astype(F32)).astype(BF16)


def split3(x):
    high = x.astype(BF16)
    rest = x - high.astype(F32)
    middle = rest.astype(BF16)
    return high, middle, (rest - middle.astype(F32)).astype(BF16)


def dot3(a, b):
    return dot(a[0], b[0]) + dot(a[0], b[1]) + dot(a[1], b[0])


def iota(shape, axis):
    return lax.broadcasted_iota(jnp.int32, shape, axis)


def total(x):
    while x.ndim > 2:
        x = jnp.sum(x, axis=0)
    return jnp.sum(jnp.sum(x, axis=0, keepdims=True), axis=1, keepdims=True)


def gather_table():
    shape = (BZ, EY * ELEMS)
    node, at = iota(shape, 0), iota(shape, 1)
    return jnp.where(at == node // 8 + (at // ELEMS) * (ELEMS + EZ), 1.0, 0.0).astype(BF16)


def spread_table():
    shape = (ELEMS, EY * BZ)
    element, at = iota(shape, 0), iota(shape, 1)
    return jnp.where(at // 8 == element, 1.0, 0.0).astype(BF16)


def element_row(field):
    parts = jnp.concatenate(split3(jnp.sum(field, axis=0)), axis=0)
    sums = dot(parts, gather_table())
    sums = sums[0:16] + sums[16:32] + sums[32:48]
    return jnp.sum(sums[0:8, 0:ELEMS], axis=0, keepdims=True) + jnp.sum(sums[8:16, ELEMS:], axis=0, keepdims=True)


def expand_rows(rows):
    count = rows.shape[0]
    tall = jnp.broadcast_to(rows, (16, ELEMS)) if count == 1 else jnp.concatenate([rows, jnp.zeros((16 - count, ELEMS), F32)], axis=0)
    wide = dot(jnp.concatenate(split3(tall), axis=0), spread_table())
    return (wide[0:16] + wide[16:32] + wide[32:48])[0:count]


def expand_block(row):
    wide = expand_rows(row)
    low = jnp.broadcast_to(wide[:, 0:BZ], (8, BZ))
    high = jnp.broadcast_to(wide[:, BZ:], (8, BZ))
    return jnp.concatenate([low, high], axis=0)


def slot_mask(slots, offset):
    slot_of_row = lax.rem(iota((ELEMS, ELEMS), 0) + offset, ELEMS)
    return slot_of_row == slots


def to_rows(element_values, slots, offset):
    return jnp.sum(jnp.where(slot_mask(slots, offset), element_values, 0.0), axis=1, keepdims=True)


def to_elements(row_values, slots, offset):
    return jnp.sum(jnp.where(slot_mask(slots, offset), row_values, 0.0), axis=0, keepdims=True)


def project(column, parts):
    out = 0.0
    at = 0
    for part in parts:
        size = part.shape[0]
        out = out + jnp.sum(column[at : at + size] * part[...], axis=0, keepdims=True)
        at += size
    return out


def correct(row, parts):
    out = []
    for part in parts:
        products = part[...] * row
        folded = products[:, 0:128]
        for at in range(128, KCOL, 128):
            folded = folded + products[:, at : at + 128]
        out.append(jnp.sum(folded, axis=1, keepdims=True))
    return jnp.concatenate(out, axis=0)


def store_sum(out_ref, first, second):
    count, _, width = out_ref.shape
    cut = width - 128
    out_ref[:, :, 0:cut] = jnp.broadcast_to(first[None], (count, 1, cut))
    out_ref[:, :, cut:width] = jnp.broadcast_to(second[None], (count, 1, 128))


def lanes(values):
    at = iota((1, 128), 1)
    row = jnp.zeros((1, 128), F32)
    for i, value in enumerate(values):
        row = jnp.where(at == i, value, row)
    return row


def lane(row, i):
    return jnp.sum(jnp.where(iota(row.shape, 1) == i, row, 0.0), axis=1, keepdims=True)


def odd(index):
    return lax.rem(index, 2) == 1


def pair_out(index, low, high):
    return jnp.where(odd(index), low, high), jnp.where(odd(index), high, low)


def pair_in(index, first, second):
    return jnp.where(odd(index), first, second), jnp.where(odd(index), second, first)


def extend_y(block, low, high, depth):
    at = iota((8, BZ), 0)
    tails = []
    for x in range(block.shape[0]):
        tail = jnp.zeros((8, BZ), F32)
        for i in range(depth):
            tail = jnp.where(at == i, high[i][x : x + 1], tail)
            tail = jnp.where(at == 8 - depth + i, low[i][x : x + 1], tail)
        tails.append(tail)
    return jnp.concatenate([block, jnp.stack(tails)], axis=1)


def roll_sum(x):
    count, rows, _ = x.shape
    beside = pltpu.roll(x, 1, 1) + pltpu.roll(x, rows - 1, 1)
    flat = x.reshape(count * rows, BZ)
    at = iota(flat.shape, 1)
    beside_z = jnp.where(at == 0, 0.0, pltpu.roll(flat, 1, 1)) + jnp.where(at == BZ - 1, 0.0, pltpu.roll(flat, BZ - 1, 1))
    return beside + beside_z.reshape(x.shape)


def fine_solve(rows, sigma, tables):
    wh, wl, th, tl, vh, vl, uh, ul, column, beyond = tables
    spectra = dot3((wh.here()[...], wl.here()[...]), split2(rows))
    th, tl, column, beyond, vh, vl, uh, ul = [table.here()[...] for table in (th, tl, column, beyond, vh, vl, uh, ul)]
    nodal = []
    for half in range(2):
        part = spectra[:, half * HZ : (half + 1) * HZ]
        edge = spectra[:, HZ : HZ + 1] if half == 0 else spectra[:, HZ - 1 : HZ]
        part = dot3(split2(part), (th, tl)) + edge * beyond[half : half + 1]
        sig = jnp.where(column[:, 1:2] == 0.0, repeat_lanes(sigma, half), repeat_lanes(sigma, 2 + half))
        part = part / (column[:, 0:1] + beyond[2:3] + sig)
        part = dot3((vh, vl), split2(part))
        nodal.append(dot3(split2(part), (uh, ul)).reshape(BX, BY, HZ))
    return jnp.concatenate(nodal, axis=2)


def repeat_lanes(row, group):
    only = jnp.where(iota((1, ELEMS), 1) // 32 == group, row, 0.0)
    only = only + pltpu.roll(only, 64, 1)
    only = only + pltpu.roll(only, 32, 1)
    return jnp.concatenate([only] * 3, axis=1)


def eye_mask():
    return iota((ELEMS, ELEMS), 0) == iota((ELEMS, ELEMS), 1)


def row_to_column(row):
    return jnp.sum(jnp.where(eye_mask(), row, 0.0), axis=1, keepdims=True)


def column_to_row(column):
    return jnp.sum(jnp.where(eye_mask(), column, 0.0), axis=0, keepdims=True)


def pad_tile(rows):
    at = iota((8, ELEMS), 0)
    tile = jnp.zeros((8, ELEMS), F32)
    for i, row in enumerate(rows):
        tile = jnp.where(at == i, row, tile)
    return jnp.concatenate([tile, jnp.zeros((8, BZ - ELEMS), F32)], axis=1)


def start_kernel(swapped, late, right_far, diagonal_far, factor, slots, c, ya, yb, right, diagonal, factor_here, sent):
    d = lax.axis_index("narrow")
    half = ELEMS // 2
    right_load = late.start(right_far, right)
    diagonal_load = late.start(diagonal_far, diagonal)
    late.start(factor.at[pl.ds(pl.multiple_of((1 - d) * half, half), half)] if swapped else factor.at[half:ELEMS], sent)
    late.start(factor, factor_here)
    right_load.wait()
    row = column_to_row(to_rows(element_row(right[...]) * (1.0 / 16.0), slots[...], 0))
    c[...] = row
    diagonal_load.wait()
    for i, ref in enumerate((right, diagonal)):
        ya[i], yb[i] = pair_out(d, ref[:, 0, :], ref[:, BY - 1, :])
    ya[2] = pad_tile([row, slots[...].astype(F32)])
    yb[2] = jnp.zeros((8, BZ), F32)


def project_kernel(swapped, late, c, ra, rb, right, diagonal, factor, sums, xa, xb):
    w, d = lax.axis_index("wide"), lax.axis_index("narrow")
    row = c[...]
    if swapped:
        half = ELEMS // 2
        other = pltpu.roll(ra[2, 0:1, 0:ELEMS], half, 1)
        row = jnp.where(iota((1, ELEMS), 1) // half == d, row, other)
    store_sum(sums, project(row_to_column(row), (factor,)), jnp.zeros((1, 128), F32))
    for i, ref in enumerate((right, diagonal)):
        low, high = pair_in(d, ra[i], rb[i])
        layers = [extend_y(ref[x : x + 1], [low[x : x + 1]], [high[x : x + 1]], 1)[0] for x in (0, BX - 1)]
        xa[i], xb[i] = pair_out(w, *layers)


def widened(block, ya, yb, xa, xb, i):
    w, d = lax.axis_index("wide"), lax.axis_index("narrow")
    low, high = pair_in(d, ya[i], yb[i])
    x_low, x_high = pair_in(w, xa[i], xb[i])
    return jnp.concatenate([x_low[None], extend_y(block, [low], [high], 1), x_high[None]], axis=0)


def first_fine_kernel(late, *rest):
    right, diagonal, ya, yb, xa, xb, solved, sigma_out = rest[10:]
    rows = widened(right[...], ya, yb, xa, xb, 0)
    sigma = element_row(diagonal[...]) * (1.0 / 512.0)
    sigma_out[...] = sigma
    solved[...] = fine_solve(rows.reshape(YW, BZ), sigma, rest[:10])


def first_coarse_kernel(swapped, late, sums, solved, slots, factor, ya, yb):
    d = lax.axis_index("narrow")
    row = jnp.sum(sums[...], axis=0)[:, 0:KCOL]
    column = correct(row, (factor,))
    for i in range(2):
        ya[i], yb[i] = pair_out(d, solved[:, i, :], solved[:, BY - 2 + i, :])
    ya[2] = pad_tile([column_to_row(column) if swapped else to_elements(column, slots[...], 0)])
    yb[2] = ya[2]


def extend_kernel(swapped, late, solved, slots, ra_first, own_ref, ra, rb, search, xa, xb):
    w, d = lax.axis_index("wide"), lax.axis_index("narrow")
    groups = lax.axis_size("narrow")
    own = own_ref[2, 0:1, 0:ELEMS]
    theirs = ra[2, 0:1, 0:ELEMS]
    if swapped:
        half = ELEMS // 2
        at = iota((1, ELEMS), 1) // half
        other = jnp.where(at == d, pltpu.roll(own, half, 1), theirs)
        own = jnp.where(at == d, own, pltpu.roll(theirs, half, 1))
        own = to_elements(row_to_column(own), slots[...], 0)
        other = to_elements(row_to_column(other), ra_first[2, 1:2, 0:ELEMS].astype(jnp.int32), 0)
        values_low, values_high = other, other
    else:
        values_low, values_high = pair_in(d, theirs, rb[2, 0:1, 0:ELEMS])
    values_low = jnp.where(d > 0, values_low, 0.0)
    values_high = jnp.where(d < groups - 1, values_high, 0.0)
    wide = expand_rows(jnp.concatenate([own, values_low, values_high], axis=0)) * (1.0 / 16.0)
    coarse = jnp.concatenate(
        [jnp.broadcast_to(wide[0:1, 0:BZ], (8, BZ)), jnp.broadcast_to(wide[0:1, BZ:], (8, BZ))], axis=0
    )
    low, high = [], []
    for i in range(2):
        one, two = pair_in(d, ra[i], rb[i])
        low.append(one + wide[1:2, BZ:])
        high.append(two + wide[2:3, 0:BZ])
    block = extend_y(solved[...] + coarse[None], low, high, 2)
    search[...] = block
    xa[...], xb[...] = pair_out(w, block[0:2], block[BX - 2 : BX])


def owned_rows(swapped, factor, received):
    half = ELEMS // 2
    if not swapped:
        return (factor,), 0
    at = lax.axis_index("narrow") * half
    return (factor.at[pl.ds(pl.multiple_of(at, half), half)], received), at


def operator_kernel(
    swapped, sizes, late, right, diagonal, factor, received, search, sa, sb, ya, yb, xa, xb, slots, sums, image_out, halo
):
    w, d = lax.axis_index("wide"), lax.axis_index("narrow")
    owned, offset = owned_rows(swapped, factor, received)
    s_low, s_high = pair_in(w, sa[...], sb[...])
    vector = jnp.concatenate([s_low, search[...], s_high], axis=0)
    coefficient = widened(diagonal[...], ya, yb, xa, xb, 1)
    centre = vector[1 : BX + 3]
    image = (6.0 + coefficient) * centre - (vector[0 : BX + 2] + vector[2 : BX + 4] + roll_sum(centre))
    x = iota(image.shape, 0)
    y = iota(image.shape, 1)
    inside = (y < BY) | ((y == BY) & (d < sizes[1] - 1)) | ((y == YR - 1) & (d > 0))
    inside &= ((x > 0) | (w > 0)) & ((x < BX + 1) | (w < sizes[0] - 1))
    image = jnp.where(inside, image, 0.0)
    image_out[...] = image
    halo[0:BY] = s_low[1, 0:BY]
    halo[BY : 2 * BY] = s_high[0, 0:BY]
    halo[2 * BY : 2 * BY + 8] = search[:, YR - 1, :]
    halo[2 * BY + 8 : 3 * BY] = search[:, BY, :]
    own = image[1 : BX + 1, 0:BY]
    own_search = search[:, 0:BY, :]
    column = to_rows(element_row(own) * (1.0 / 16.0), slots[...], offset)
    extra = lanes([total(right[...] * own_search), total(own_search * own)])
    store_sum(sums, project(column, owned), extra)


def second_fine_kernel(late, *rest):
    w, d = lax.axis_index("wide"), lax.axis_index("narrow")
    image, sigma, solved, ya, yb, xa, xb = rest[10:]
    out = fine_solve(image[...].reshape(YW, BZ), sigma[...], rest[:10])
    solved[...] = out
    ya[...], yb[...] = pair_out(d, solved[:, 0, :], solved[:, BY - 1, :])
    xa[...], xb[...] = pair_out(w, out[0], out[BX - 1])


def second_coarse_kernel(
    swapped, late, right, diagonal, factor, received, sums, solved, fya, fyb, fxa, fxb, search, halo, image, slots,
    search_out, image_out, last, products,
):
    w, d = lax.axis_index("wide"), lax.axis_index("narrow")
    owned, offset = owned_rows(swapped, factor, received)
    row = jnp.sum(sums[...], axis=0)
    products[...] = row[:, KCOL:WIDTH]
    step = lane(row[:, KCOL:WIDTH], 0) / lane(row[:, KCOL:WIDTH], 1)
    values = to_elements(correct(row[:, 0:KCOL], owned), slots[...], offset)
    coarse = expand_block(values * (1.0 / 16.0))
    own_search = search[:, 0:BY, :]
    own_image = image[1 : BX + 1, 0:BY, :]
    vector = own_search - step * (solved[...] + coarse[None])
    f_low, f_high = pair_in(w, fxa[...], fxb[...])
    x_low = halo[0:BY] - step * f_low
    x_high = halo[BY : 2 * BY] - step * f_high
    g_low, g_high = pair_in(d, fya[...], fyb[...])
    y_low = halo[2 * BY : 2 * BY + 8] - step * g_low
    y_high = halo[2 * BY + 8 : 3 * BY] - step * g_high
    beside = roll_sum(extend_y(vector, [y_low], [y_high], 1))[:, 0:BY]
    beside = beside + jnp.concatenate([x_low[None], vector[0 : BX - 1]], axis=0)
    beside = beside + jnp.concatenate([vector[1:BX], x_high[None]], axis=0)
    next_image = (6.0 + diagonal[...]) * vector - beside
    search_out[...] = vector
    image_out[...] = next_image
    residual = right[...] - step * own_image
    edges = total(coarse * (x_low + x_high)) + total(y_low * coarse[0:1]) + total(y_high * coarse[BY - 1 : BY])
    store_sum(
        last,
        values,
        lanes([total(residual * vector), total(vector * next_image) + step * edges, total(vector * own_image)]),
    )


def last_kernel(sizes, late, right, products, last, search, image, next_search, next_image, x_out, r_out):
    w, d = lax.axis_index("wide"), lax.axis_index("narrow")
    groups = sizes[1]
    count = sizes[0] * groups
    product, bottom = lane(products[...], 0), lane(products[...], 1)
    step = product / bottom
    z = last[:, 0, 0:ELEMS]
    rows = iota((count, ELEMS), 0)
    at = iota((count, ELEMS), 1)
    faces = jnp.where(rows < count - groups, z * pltpu.roll(z, count - groups, 0), 0.0)
    across = pltpu.roll(pltpu.roll(z, count - 1, 0), EZ, 1)
    faces = faces + jnp.where((lax.rem(rows, groups) < groups - 1) & (at >= EZ), z * across, 0.0)
    sums = jnp.sum(last[:, :, ELEMS:], axis=0)
    next_product = lane(sums, 0)
    quadratic = lane(sums, 1) - step * step * 0.5 * total(faces)
    cross = lane(sums, 2)
    me = w * groups + d
    picked = []
    for index, there in ((me - groups, w > 0), (me + groups, w < sizes[0] - 1), (me - 1, d > 0), (me + 1, d < groups - 1)):
        picked.append(jnp.sum(jnp.where((rows == index) & there, z, 0.0), axis=0, keepdims=True))
    wide = expand_rows(jnp.concatenate(picked, axis=0)) * (1.0 / 16.0)
    layers = []
    for i in range(2):
        low = jnp.broadcast_to(wide[i : i + 1, 0:BZ], (8, BZ))
        high = jnp.broadcast_to(wide[i : i + 1, BZ:], (8, BZ))
        layers.append(jnp.concatenate([low, high], axis=0)[None])
    shape = (BX, BY, BZ)
    x, y = iota(shape, 0), iota(shape, 1)
    missing = jnp.where(x == 0, layers[0], 0.0) + jnp.where(x == BX - 1, layers[1], 0.0)
    missing = missing + jnp.where(y == 0, wide[2:3, BZ:][None], 0.0) + jnp.where(y == BY - 1, wide[3:4, 0:BZ][None], 0.0)
    ratio = next_product / product
    curvature = quadratic + 2.0 * ratio * cross + ratio * ratio * bottom
    step_next = next_product / curvature
    own_search = search[:, 0:BY, :]
    own_image = image[1 : BX + 1, 0:BY, :]
    direction = next_search[...] + ratio * own_search
    total_image = next_image[...] + step * missing + ratio * own_image
    x_out[...] = step * own_search + step_next * direction
    r_out[...] = (right[...] - step * own_image) - step_next * total_image


class Loaded:
    def __init__(self, copy, ref):
        self.copy, self.ref, self.ready = copy, ref, False

    def wait(self):
        if not self.ready:
            self.copy.wait()
            self.ready = True

    def here(self):
        self.wait()
        return self.ref


class Copies:
    def __init__(self, semaphores):
        self.semaphores, self.all = semaphores, []

    def start(self, source, target):
        copy = pltpu.make_async_copy(source, target, self.semaphores.at[len(self.all)])
        copy.start()
        self.all.append(Loaded(copy, target))
        return self.all[-1]

    def finish(self):
        for loaded in self.all:
            loaded.wait()


def call(kernel, outs, far=(), late=(), near=(), final=False):
    first, second = len(far), len(far) + len(late)

    def run(*refs):
        end = len(refs) - 1 - len(late)
        copies = Copies(refs[-1])
        loaded = [copies.start(source, target) for source, target in zip(refs[first:second], refs[end:-1])]
        kernel(copies, *refs[:first], *loaded, *refs[second:end])
        copies.finish()

    shape_of = jax.ShapeDtypeStruct if final else pltpu.VMEM
    spaces = [pltpu.HBM] * second + [pltpu.VMEM] * len(near)
    return pl.pallas_call(
        run,
        out_shape=[shape_of(out, F32) for out in outs],
        in_specs=[pl.BlockSpec(memory_space=space) for space in spaces],
        out_specs=[pl.BlockSpec(memory_space=pltpu.VMEM)] * len(outs),
        scratch_shapes=[*(pltpu.VMEM(array.shape, array.dtype) for array in late), pltpu.SemaphoreType.DMA((second + 2,))],
        compiler_params=pltpu.CompilerParams(vmem_limit_bytes=16 * 1024 * 1024),
    )(*(pltpu.with_memory_space_constraint(array, pltpu.HBM) for array in (*far, *late)), *near)


def pair_swap(first, second, axis):
    size = lax.axis_size(axis)
    received = []
    for value, begin in ((first, 0), (second, 1)):
        perm = []
        for i in range(begin, size - 1, 2):
            perm += [(i, i + 1), (i + 1, i)]
        received.append(lax.ppermute(value, axis, perm) if perm else jnp.zeros_like(value))
    return received


def everywhere(rows):
    return lax.all_to_all(rows, AXES, split_axis=0, concat_axis=0, tiled=True)


def body(right, diagonal, coarse_slot, factor):
    sizes = (lax.axis_size("wide"), lax.axis_size("narrow"))
    groups = sizes[1]
    count = sizes[0] * groups
    fine = [jnp.asarray(c) for c in tables()]
    slots = coarse_slot.reshape(1, ELEMS)
    swapped = groups == 2
    if not swapped:
        factor = factor.reshape(groups, ELEMS // groups, KCOL)
        factor = lax.all_to_all(factor, "narrow", split_axis=0, concat_axis=0, tiled=True).reshape(ELEMS, KCOL)
    part = functools.partial

    block, layer, extended = (BX, BY, BZ), (YR, BZ), (BX, YR, BZ)
    y_shape, x_shape, half, whole = (3, BX, BZ), (2, YR, BZ), (ELEMS // 2, KCOL), (ELEMS, KCOL)
    c, ya, yb, right, diagonal, factor, sent = call(
        part(start_kernel, swapped),
        [(1, ELEMS), y_shape, y_shape, block, block, whole, half],
        far=[right, diagonal, factor],
        near=[slots],
    )
    ya, yb = pair_swap(ya, yb, "narrow")
    received = lax.ppermute(sent, "narrow", [(0, 1), (1, 0)]) if swapped else sent
    sums, xa, xb = call(
        part(project_kernel, swapped), [(count, 1, WIDTH), x_shape, x_shape], near=[c, ya, yb, right, diagonal, factor]
    )
    sums = everywhere(sums)
    xa, xb = pair_swap(xa, xb, "wide")
    solved, sigma = call(first_fine_kernel, [block, (1, ELEMS)], late=fine, near=[right, diagonal, ya, yb, xa, xb])
    ta, tb = call(part(first_coarse_kernel, swapped), [y_shape, y_shape], near=[sums, solved, slots, factor])
    ra, rb = pair_swap(ta, tb, "narrow")
    search, sa, sb = call(
        part(extend_kernel, swapped), [extended, (2,) + layer, (2,) + layer], near=[solved, slots, ya, ta, ra, rb]
    )
    sa, sb = pair_swap(sa, sb, "wide")
    sums, image, halo = call(
        part(operator_kernel, swapped, sizes),
        [(count, 1, WIDTH), (BX + 2, YR, BZ), (3 * BY, BZ)],
        near=[right, diagonal, factor, received, search, sa, sb, ya, yb, xa, xb, slots],
    )
    sums = everywhere(sums)
    solved, ya, yb, fa, fb = call(
        second_fine_kernel, [block, (BX, BZ), (BX, BZ), (BY, BZ), (BY, BZ)], late=fine, near=[image, sigma]
    )
    ya, yb = pair_swap(ya, yb, "narrow")
    fa, fb = pair_swap(fa, fb, "wide")
    next_search, next_image, last, products = call(
        part(second_coarse_kernel, swapped),
        [block, block, (count, 1, 2 * ELEMS), (1, 128)],
        near=[right, diagonal, factor, received, sums, solved, ya, yb, fa, fb, search, halo, image, slots],
    )
    last = everywhere(last)
    return tuple(
        call(
            part(last_kernel, sizes),
            [block, block],
            near=[right, products, last, search, image, next_search, next_image],
            final=True,
        )
    )


def solution(mesh):
    in_specs = (
        P("wide", "narrow", None),
        P("wide", "narrow", None),
        P("wide", "narrow", None),
        P(("wide", "narrow"), None),
    )
    out_specs = (P("wide", "narrow", None), P("wide", "narrow", None))
    return jax.shard_map(body, mesh=mesh, in_specs=in_specs, out_specs=out_specs, check_vma=False)
```

```python
import functools

import jax
import jax.numpy as jnp
import numpy as np
from jax import lax
from jax.experimental import pallas as pl
from jax.experimental.pallas import tpu as pltpu
from jax.sharding import PartitionSpec as P

F32 = jnp.float32
BF16 = jnp.bfloat16
BX, BY, BZ = 8, 16, 512
EY, EZ = 2, 64
ELEMS = EY * EZ
YR = 24
YW = YR * (BX + 2)
AB = 208
HZ = 256
HW = 384
KCOL = 2048
WIDTH = KCOL + 128
AXES = ("wide", "narrow")


def split_const(values):
    high = values.astype(jnp.bfloat16)
    low = (values - high.astype(np.float64)).astype(jnp.bfloat16)
    return high, low


@functools.lru_cache(maxsize=None)
def tables():
    index = np.arange(10, dtype=np.float64)
    basis = np.sqrt(2.0 / 11.0) * np.sin(np.pi * (index[:, None] + 1.0) * (index[None, :] + 1.0) / 11.0)
    values = 2.0 - 2.0 * np.cos(np.pi * (index + 1.0) / 11.0)
    to_z = np.zeros((HZ, HW))
    from_z = np.zeros((HW, HZ))
    beyond = np.zeros((8, HW), np.float32)
    last = HZ // 8 - 1
    for e in range(last + 1):
        at = slice(e, 10 * (last + 1), last + 1)
        for k in range(10):
            z = 8 * e + k - 1
            if 0 <= z < HZ:
                to_z[z, at] = basis[k]
            if 1 <= k <= 8:
                from_z[at, z] = basis[k]
    beyond[0, last : 10 * (last + 1) : last + 1] = basis[9]
    beyond[1, 0 : 10 * (last + 1) : last + 1] = basis[0]
    beyond[2] = 1.0
    beyond[2, : 10 * (last + 1)] = np.repeat(values, last + 1)
    to_xy = np.zeros((10, EY, 10, 10, YR))
    from_xy = np.zeros((BX, BY, 10, EY, 10))
    for e in range(EY):
        for j in range(10):
            y = 8 * e + j - 1
            to_xy[:, e, :, :, y % YR] += basis.T[:, None, :] * basis[j][None, :, None]
            if 1 <= j <= 8:
                from_xy[:, y, :, e, :] = basis[1:9, :, None] * basis[j][None, None, :]
    to_xy = np.pad(to_xy.reshape(200, YW), ((0, AB - 200), (0, 0)))
    from_xy = np.pad(from_xy.reshape(BX * BY, 200), ((0, 0), (0, AB - 200)))
    column = np.zeros((AB, 128), np.float32)
    grid = np.zeros((10, EY, 10, 2))
    grid[..., 0] = values[:, None, None] + values[None, None, :]
    grid[..., 1] = np.arange(EY)[None, :, None]
    column[:200, :2] = grid.reshape(200, 2)
    column[200:, 0] = 1.0
    return split_const(to_xy) + split_const(to_z) + split_const(from_xy) + split_const(from_z) + (column, beyond)


def dot(a, b):
    return jnp.dot(a, b, preferred_element_type=F32)


def split2(x):
    high = x.astype(BF16)
    return high, (x - high.astype(F32)).astype(BF16)


def split3(x):
    high = x.astype(BF16)
    rest = x - high.astype(F32)
    middle = rest.astype(BF16)
    return high, middle, (rest - middle.astype(F32)).astype(BF16)


def dot3(a, b):
    return dot(a[0], b[0]) + dot(a[0], b[1]) + dot(a[1], b[0])


def iota(shape, axis):
    return lax.broadcasted_iota(jnp.int32, shape, axis)


def total(x):
    while x.ndim > 2:
        x = jnp.sum(x, axis=0)
    return jnp.sum(jnp.sum(x, axis=0, keepdims=True), axis=1, keepdims=True)


def gather_table():
    shape = (BZ, EY * ELEMS)
    node, at = iota(shape, 0), iota(shape, 1)
    return jnp.where(at == node // 8 + (at // ELEMS) * (ELEMS + EZ), 1.0, 0.0).astype(BF16)


def spread_table():
    shape = (ELEMS, EY * BZ)
    element, at = iota(shape, 0), iota(shape, 1)
    return jnp.where(at // 8 == element, 1.0, 0.0).astype(BF16)


def element_row(field):
    parts = jnp.concatenate(split3(jnp.sum(field, axis=0)), axis=0)
    sums = dot(parts, gather_table())
    sums = sums[0:16] + sums[16:32] + sums[32:48]
    return jnp.sum(sums[0:8, 0:ELEMS], axis=0, keepdims=True) + jnp.sum(sums[8:16, ELEMS:], axis=0, keepdims=True)


def expand_rows(rows):
    count = rows.shape[0]
    tall = jnp.broadcast_to(rows, (16, ELEMS)) if count == 1 else jnp.concatenate([rows, jnp.zeros((16 - count, ELEMS), F32)], axis=0)
    wide = dot(jnp.concatenate(split3(tall), axis=0), spread_table())
    return (wide[0:16] + wide[16:32] + wide[32:48])[0:count]


def expand_block(row):
    wide = expand_rows(row)
    low = jnp.broadcast_to(wide[:, 0:BZ], (8, BZ))
    high = jnp.broadcast_to(wide[:, BZ:], (8, BZ))
    return jnp.concatenate([low, high], axis=0)


def slot_mask(slots, offset):
    slot_of_row = lax.rem(iota((ELEMS, ELEMS), 0) + offset, ELEMS)
    return slot_of_row.astype(F32) == slots


def to_rows(element_values, slots, offset):
    return jnp.sum(jnp.where(slot_mask(slots, offset), element_values, 0.0), axis=1, keepdims=True)


def to_elements(row_values, slots, offset):
    return jnp.sum(jnp.where(slot_mask(slots, offset), row_values, 0.0), axis=0, keepdims=True)


def project(column, parts):
    out = 0.0
    at = 0
    for part in parts:
        size = part.shape[0]
        out = out + jnp.sum(column[at : at + size] * part[...], axis=0, keepdims=True)
        at += size
    return out


def correct(row, parts):
    out = []
    for part in parts:
        products = part[...] * row
        folded = products[:, 0:128]
        for at in range(128, KCOL, 128):
            folded = folded + products[:, at : at + 128]
        out.append(jnp.sum(folded, axis=1, keepdims=True))
    return jnp.concatenate(out, axis=0)


def store_sum(out_ref, first, second):
    count, _, width = out_ref.shape
    cut = width - 128
    out_ref[:, :, 0:cut] = jnp.broadcast_to(first[None], (count, 1, cut))
    out_ref[:, :, cut:width] = jnp.broadcast_to(second[None], (count, 1, 128))


def lanes(values):
    at = iota((1, 128), 1)
    row = jnp.zeros((1, 128), F32)
    for i, value in enumerate(values):
        row = jnp.where(at == i, value, row)
    return row


def lane(row, i):
    return jnp.sum(jnp.where(iota(row.shape, 1) == i, row, 0.0), axis=1, keepdims=True)


def odd(index):
    return lax.rem(index, 2) == 1


def pair_out(index, low, high):
    return jnp.where(odd(index), low, high), jnp.where(odd(index), high, low)


def pair_in(index, first, second):
    return jnp.where(odd(index), first, second), jnp.where(odd(index), second, first)


def extend_y(block, low, high, depth):
    at = iota((8, BZ), 0)
    tails = []
    for x in range(block.shape[0]):
        tail = jnp.zeros((8, BZ), F32)
        for i in range(depth):
            tail = jnp.where(at == i, high[i][x : x + 1], tail)
            tail = jnp.where(at == 8 - depth + i, low[i][x : x + 1], tail)
        tails.append(tail)
    return jnp.concatenate([block, jnp.stack(tails)], axis=1)


def roll_sum(x):
    count, rows, _ = x.shape
    beside = pltpu.roll(x, 1, 1) + pltpu.roll(x, rows - 1, 1)
    flat = x.reshape(count * rows, BZ)
    at = iota(flat.shape, 1)
    beside_z = jnp.where(at == 0, 0.0, pltpu.roll(flat, 1, 1)) + jnp.where(at == BZ - 1, 0.0, pltpu.roll(flat, BZ - 1, 1))
    return beside + beside_z.reshape(x.shape)


def fine_solve(rows, sigma, tables):
    wh, wl, th, tl, vh, vl, uh, ul, column, beyond = tables
    spectra = dot3((wh.here()[...], wl.here()[...]), split2(rows))
    th, tl, column, beyond, vh, vl, uh, ul = [table.here()[...] for table in (th, tl, column, beyond, vh, vl, uh, ul)]
    nodal = []
    for half in range(2):
        part = spectra[:, half * HZ : (half + 1) * HZ]
        edge = spectra[:, HZ : HZ + 1] if half == 0 else spectra[:, HZ - 1 : HZ]
        part = dot3(split2(part), (th, tl)) + edge * beyond[half : half + 1]
        sig = jnp.where(column[:, 1:2] == 0.0, repeat_lanes(sigma, half), repeat_lanes(sigma, 2 + half))
        part = part / (column[:, 0:1] + beyond[2:3] + sig)
        part = dot3((vh, vl), split2(part))
        nodal.append(dot3(split2(part), (uh, ul)).reshape(BX, BY, HZ))
    return jnp.concatenate(nodal, axis=2)


def repeat_lanes(row, group):
    only = jnp.where(iota((1, ELEMS), 1) // 32 == group, row, 0.0)
    only = only + pltpu.roll(only, 64, 1)
    only = only + pltpu.roll(only, 32, 1)
    return jnp.concatenate([only] * 3, axis=1)


def eye_mask():
    return iota((ELEMS, ELEMS), 0) == iota((ELEMS, ELEMS), 1)


def row_to_column(row):
    return jnp.sum(jnp.where(eye_mask(), row, 0.0), axis=1, keepdims=True)


def column_to_row(column):
    return jnp.sum(jnp.where(eye_mask(), column, 0.0), axis=0, keepdims=True)


def pad_tile(rows):
    at = iota((8, ELEMS), 0)
    tile = jnp.zeros((8, ELEMS), F32)
    for i, row in enumerate(rows):
        tile = jnp.where(at == i, row, tile)
    return jnp.concatenate([tile, jnp.zeros((8, BZ - ELEMS), F32)], axis=1)


def start_kernel(
    swapped, late, right_far, diagonal_far, factor, slots_far, c, ya, yb, right, diagonal, kept, sent, slots_out
):
    d = lax.axis_index("narrow")
    half = ELEMS // 2
    at = pl.multiple_of(d * half, half) if swapped else 0
    there = pl.multiple_of((1 - d) * half, half) if swapped else half
    right_load = late.start(right_far, right)
    diagonal_load = late.start(diagonal_far, diagonal)
    late.start(factor.at[pl.ds(there, half)], sent)
    late.start(factor.at[pl.ds(at, half)], kept)
    slots_in = slots_far.here()
    slots = jnp.concatenate([slots_in[0:1], slots_in[1:2]], axis=1).astype(F32)
    slots_out[...] = slots
    right_load.wait()
    row = column_to_row(to_rows(element_row(right[...]) * (1.0 / 16.0), slots, 0))
    c[...] = row
    diagonal_load.wait()
    for i, ref in enumerate((right, diagonal)):
        ya[i], yb[i] = pair_out(d, ref[:, 0, :], ref[:, BY - 1, :])
    ya[2] = pad_tile([row, slots])
    yb[2] = jnp.zeros((8, BZ), F32)


def project_kernel(swapped, late, c, ra, rb, right, diagonal, kept, sent, sums, xa, xb):
    w, d = lax.axis_index("wide"), lax.axis_index("narrow")
    row = c[...]
    if swapped:
        half = ELEMS // 2
        other = ra[2, 0:1, 0:ELEMS]
        row = jnp.where(d == 0, row, pltpu.roll(row, half, 1))
        other = jnp.where(d == 0, pltpu.roll(other, half, 1), other)
        row = jnp.where(iota((1, ELEMS), 1) < half, row, other)
    store_sum(sums, project(row_to_column(row), (kept, sent)), jnp.zeros((1, 128), F32))
    for i, ref in enumerate((right, diagonal)):
        low, high = pair_in(d, ra[i], rb[i])
        layers = [extend_y(ref[x : x + 1], [low[x : x + 1]], [high[x : x + 1]], 1)[0] for x in (0, BX - 1)]
        xa[i], xb[i] = pair_out(w, *layers)


def widened(block, ya, yb, xa, xb, i):
    w, d = lax.axis_index("wide"), lax.axis_index("narrow")
    low, high = pair_in(d, ya[i], yb[i])
    x_low, x_high = pair_in(w, xa[i], xb[i])
    return jnp.concatenate([x_low[None], extend_y(block, [low], [high], 1), x_high[None]], axis=0)


def first_fine_kernel(late, *rest):
    right, diagonal, ya, yb, xa, xb, solved, sigma_out = rest[10:]
    rows = widened(right[...], ya, yb, xa, xb, 0)
    sigma = element_row(diagonal[...]) * (1.0 / 512.0)
    sigma_out[...] = sigma
    solved[...] = fine_solve(rows.reshape(YW, BZ), sigma, rest[:10])


def first_coarse_kernel(swapped, late, sums, solved, slots, kept, sent, ya, yb):
    d = lax.axis_index("narrow")
    row = jnp.sum(sums[...], axis=0)[:, 0:KCOL]
    column = correct(row, (kept, sent))
    for i in range(2):
        ya[i], yb[i] = pair_out(d, solved[:, i, :], solved[:, BY - 2 + i, :])
    if swapped:
        values = column_to_row(column)
        values = jnp.where(d == 0, values, pltpu.roll(values, ELEMS // 2, 1))
    else:
        values = to_elements(column, slots[...], 0)
    ya[2] = pad_tile([values])
    yb[2] = ya[2]


def extend_kernel(swapped, late, solved, slots, ra_first, own_ref, ra, rb, search, xa, xb):
    w, d = lax.axis_index("wide"), lax.axis_index("narrow")
    groups = lax.axis_size("narrow")
    own = own_ref[2, 0:1, 0:ELEMS]
    theirs = ra[2, 0:1, 0:ELEMS]
    if swapped:
        half = ELEMS // 2
        at = iota((1, ELEMS), 1) // half
        other = jnp.where(at == d, pltpu.roll(own, half, 1), theirs)
        own = jnp.where(at == d, own, pltpu.roll(theirs, half, 1))
        own = to_elements(row_to_column(own), slots[...], 0)
        other = to_elements(row_to_column(other), ra_first[2, 1:2, 0:ELEMS], 0)
        values_low, values_high = other, other
    else:
        values_low, values_high = pair_in(d, theirs, rb[2, 0:1, 0:ELEMS])
    values_low = jnp.where(d > 0, values_low, 0.0)
    values_high = jnp.where(d < groups - 1, values_high, 0.0)
    wide = expand_rows(jnp.concatenate([own, values_low, values_high], axis=0)) * (1.0 / 16.0)
    coarse = jnp.concatenate(
        [jnp.broadcast_to(wide[0:1, 0:BZ], (8, BZ)), jnp.broadcast_to(wide[0:1, BZ:], (8, BZ))], axis=0
    )
    low, high = [], []
    for i in range(2):
        one, two = pair_in(d, ra[i], rb[i])
        low.append(one + wide[1:2, BZ:])
        high.append(two + wide[2:3, 0:BZ])
    block = extend_y(solved[...] + coarse[None], low, high, 2)
    search[...] = block
    xa[...], xb[...] = pair_out(w, block[0:2], block[BX - 2 : BX])


def operator_kernel(
    swapped, sizes, late, right, diagonal, kept, received, search, sa, sb, ya, yb, xa, xb, slots, sums, image_out, halo
):
    w, d = lax.axis_index("wide"), lax.axis_index("narrow")
    owned, offset = (kept, received), d * (ELEMS // 2) if swapped else 0
    s_low, s_high = pair_in(w, sa[...], sb[...])
    vector = jnp.concatenate([s_low, search[...], s_high], axis=0)
    coefficient = widened(diagonal[...], ya, yb, xa, xb, 1)
    centre = vector[1 : BX + 3]
    image = (6.0 + coefficient) * centre - (vector[0 : BX + 2] + vector[2 : BX + 4] + roll_sum(centre))
    x = iota(image.shape, 0)
    y = iota(image.shape, 1)
    inside = (y < BY) | ((y == BY) & (d < sizes[1] - 1)) | ((y == YR - 1) & (d > 0))
    inside &= ((x > 0) | (w > 0)) & ((x < BX + 1) | (w < sizes[0] - 1))
    image = jnp.where(inside, image, 0.0)
    image_out[...] = image
    halo[0:BY] = s_low[1, 0:BY]
    halo[BY : 2 * BY] = s_high[0, 0:BY]
    halo[2 * BY : 2 * BY + 8] = search[:, YR - 1, :]
    halo[2 * BY + 8 : 3 * BY] = search[:, BY, :]
    own = image[1 : BX + 1, 0:BY]
    own_search = search[:, 0:BY, :]
    column = to_rows(element_row(own) * (1.0 / 16.0), slots[...], offset)
    extra = lanes([total(right[...] * own_search), total(own_search * own)])
    store_sum(sums, project(column, owned), extra)


def second_fine_kernel(late, *rest):
    w, d = lax.axis_index("wide"), lax.axis_index("narrow")
    image, sigma, solved, ya, yb, xa, xb = rest[10:]
    out = fine_solve(image[...].reshape(YW, BZ), sigma[...], rest[:10])
    solved[...] = out
    ya[...], yb[...] = pair_out(d, solved[:, 0, :], solved[:, BY - 1, :])
    xa[...], xb[...] = pair_out(w, out[0], out[BX - 1])


def second_coarse_kernel(
    swapped, late, right, diagonal, kept, received, sums, solved, fya, fyb, fxa, fxb, search, halo, image, slots,
    search_out, image_out, last, products,
):
    w, d = lax.axis_index("wide"), lax.axis_index("narrow")
    owned, offset = (kept, received), d * (ELEMS // 2) if swapped else 0
    row = jnp.sum(sums[...], axis=0)
    products[...] = row[:, KCOL:WIDTH]
    step = lane(row[:, KCOL:WIDTH], 0) / lane(row[:, KCOL:WIDTH], 1)
    values = to_elements(correct(row[:, 0:KCOL], owned), slots[...], offset)
    coarse = expand_block(values * (1.0 / 16.0))
    own_search = search[:, 0:BY, :]
    own_image = image[1 : BX + 1, 0:BY, :]
    vector = own_search - step * (solved[...] + coarse[None])
    f_low, f_high = pair_in(w, fxa[...], fxb[...])
    x_low = halo[0:BY] - step * f_low
    x_high = halo[BY : 2 * BY] - step * f_high
    g_low, g_high = pair_in(d, fya[...], fyb[...])
    y_low = halo[2 * BY : 2 * BY + 8] - step * g_low
    y_high = halo[2 * BY + 8 : 3 * BY] - step * g_high
    beside = roll_sum(extend_y(vector, [y_low], [y_high], 1))[:, 0:BY]
    beside = beside + jnp.concatenate([x_low[None], vector[0 : BX - 1]], axis=0)
    beside = beside + jnp.concatenate([vector[1:BX], x_high[None]], axis=0)
    next_image = (6.0 + diagonal[...]) * vector - beside
    search_out[...] = vector
    image_out[...] = next_image
    residual = right[...] - step * own_image
    edges = total(coarse * (x_low + x_high)) + total(y_low * coarse[0:1]) + total(y_high * coarse[BY - 1 : BY])
    store_sum(
        last,
        values,
        lanes([total(residual * vector), total(vector * next_image) + step * edges, total(vector * own_image)]),
    )


def last_kernel(sizes, late, right, products, last, search, image, next_search, next_image, x_out, r_out):
    w, d = lax.axis_index("wide"), lax.axis_index("narrow")
    groups = sizes[1]
    count = sizes[0] * groups
    product, bottom = lane(products[...], 0), lane(products[...], 1)
    step = product / bottom
    z = last[:, 0, 0:ELEMS]
    rows = iota((count, ELEMS), 0)
    at = iota((count, ELEMS), 1)
    faces = jnp.where(rows < count - groups, z * pltpu.roll(z, count - groups, 0), 0.0)
    across = pltpu.roll(pltpu.roll(z, count - 1, 0), EZ, 1)
    faces = faces + jnp.where((lax.rem(rows, groups) < groups - 1) & (at >= EZ), z * across, 0.0)
    sums = jnp.sum(last[:, :, ELEMS:], axis=0)
    next_product = lane(sums, 0)
    quadratic = lane(sums, 1) - step * step * 0.5 * total(faces)
    cross = lane(sums, 2)
    me = w * groups + d
    picked = []
    for index, there in ((me - groups, w > 0), (me + groups, w < sizes[0] - 1), (me - 1, d > 0), (me + 1, d < groups - 1)):
        picked.append(jnp.sum(jnp.where((rows == index) & there, z, 0.0), axis=0, keepdims=True))
    wide = expand_rows(jnp.concatenate(picked, axis=0)) * (1.0 / 16.0)
    layers = []
    for i in range(2):
        low = jnp.broadcast_to(wide[i : i + 1, 0:BZ], (8, BZ))
        high = jnp.broadcast_to(wide[i : i + 1, BZ:], (8, BZ))
        layers.append(jnp.concatenate([low, high], axis=0)[None])
    shape = (BX, BY, BZ)
    x, y = iota(shape, 0), iota(shape, 1)
    missing = jnp.where(x == 0, layers[0], 0.0) + jnp.where(x == BX - 1, layers[1], 0.0)
    missing = missing + jnp.where(y == 0, wide[2:3, BZ:][None], 0.0) + jnp.where(y == BY - 1, wide[3:4, 0:BZ][None], 0.0)
    ratio = next_product / product
    curvature = quadratic + 2.0 * ratio * cross + ratio * ratio * bottom
    step_next = next_product / curvature
    own_search = search[:, 0:BY, :]
    own_image = image[1 : BX + 1, 0:BY, :]
    direction = next_search[...] + ratio * own_search
    total_image = next_image[...] + step * missing + ratio * own_image
    x_out[...] = step * own_search + step_next * direction
    r_out[...] = (right[...] - step * own_image) - step_next * total_image


class Loaded:
    def __init__(self, copy, ref):
        self.copy, self.ref, self.ready = copy, ref, False

    def wait(self):
        if not self.ready:
            self.copy.wait()
            self.ready = True

    def here(self):
        self.wait()
        return self.ref


class Copies:
    def __init__(self, semaphores):
        self.semaphores, self.all = semaphores, []

    def start(self, source, target):
        copy = pltpu.make_async_copy(source, target, self.semaphores.at[len(self.all)])
        copy.start()
        self.all.append(Loaded(copy, target))
        return self.all[-1]

    def finish(self):
        for loaded in self.all:
            loaded.wait()


def call(kernel, outs, far=(), late=(), near=(), final=False):
    first, second = len(far), len(far) + len(late)

    def run(*refs):
        end = len(refs) - 1 - len(late)
        copies = Copies(refs[-1])
        loaded = [copies.start(source, target) for source, target in zip(refs[first:second], refs[end:-1])]
        kernel(copies, *refs[:first], *loaded, *refs[second:end])
        copies.finish()

    shape_of = jax.ShapeDtypeStruct if final else pltpu.VMEM
    spaces = [pltpu.HBM] * second + [pltpu.VMEM] * len(near)
    return pl.pallas_call(
        run,
        out_shape=[shape_of(out, F32) for out in outs],
        in_specs=[pl.BlockSpec(memory_space=space) for space in spaces],
        out_specs=[pl.BlockSpec(memory_space=pltpu.VMEM)] * len(outs),
        scratch_shapes=[*(pltpu.VMEM(array.shape, array.dtype) for array in late), pltpu.SemaphoreType.DMA((second + 4,))],
        compiler_params=pltpu.CompilerParams(vmem_limit_bytes=16 * 1024 * 1024),
    )(*(pltpu.with_memory_space_constraint(array, pltpu.HBM) for array in (*far, *late)), *near)


def pair_swap(first, second, axis):
    size = lax.axis_size(axis)
    received = []
    for value, begin in ((first, 0), (second, 1)):
        perm = []
        for i in range(begin, size - 1, 2):
            perm += [(i, i + 1), (i + 1, i)]
        received.append(lax.ppermute(value, axis, perm) if perm else jnp.zeros_like(value))
    return received


def everywhere(rows):
    return lax.all_to_all(rows, AXES, split_axis=0, concat_axis=0, tiled=True)


def body(right, diagonal, coarse_slot, factor):
    sizes = (lax.axis_size("wide"), lax.axis_size("narrow"))
    groups = sizes[1]
    count = sizes[0] * groups
    fine = [jnp.asarray(c) for c in tables()]
    slots = coarse_slot.reshape(EY, EZ)
    swapped = groups == 2
    if not swapped:
        factor = factor.reshape(groups, ELEMS // groups, KCOL)
        factor = lax.all_to_all(factor, "narrow", split_axis=0, concat_axis=0, tiled=True).reshape(ELEMS, KCOL)
    part = functools.partial

    block, layer, extended = (BX, BY, BZ), (YR, BZ), (BX, YR, BZ)
    y_shape, x_shape, half = (3, BX, BZ), (2, YR, BZ), (ELEMS // 2, KCOL)
    c, ya, yb, right, diagonal, kept, sent, slots = call(
        part(start_kernel, swapped),
        [(1, ELEMS), y_shape, y_shape, block, block, half, half, (1, ELEMS)],
        far=[right, diagonal, factor],
        late=[slots],
    )
    ya, yb = pair_swap(ya, yb, "narrow")
    sums, xa, xb = call(
        part(project_kernel, swapped), [(count, 1, WIDTH), x_shape, x_shape], near=[c, ya, yb, right, diagonal, kept, sent]
    )
    sums = everywhere(sums)
    xa, xb = pair_swap(xa, xb, "wide")
    solved, sigma = call(first_fine_kernel, [block, (1, ELEMS)], late=fine, near=[right, diagonal, ya, yb, xa, xb])
    ta, tb = call(part(first_coarse_kernel, swapped), [y_shape, y_shape], near=[sums, solved, slots, kept, sent])
    ra, rb = pair_swap(ta, tb, "narrow")
    if swapped:
        ra, sent = lax.optimization_barrier((ra, sent))
    received = lax.ppermute(sent, "narrow", [(0, 1), (1, 0)]) if swapped else sent
    search, sa, sb = call(
        part(extend_kernel, swapped), [extended, (2,) + layer, (2,) + layer], near=[solved, slots, ya, ta, ra, rb]
    )
    sa, sb = pair_swap(sa, sb, "wide")
    sums, image, halo = call(
        part(operator_kernel, swapped, sizes),
        [(count, 1, WIDTH), (BX + 2, YR, BZ), (3 * BY, BZ)],
        near=[right, diagonal, kept, received, search, sa, sb, ya, yb, xa, xb, slots],
    )
    sums = everywhere(sums)
    solved, ya, yb, fa, fb = call(
        second_fine_kernel, [block, (BX, BZ), (BX, BZ), (BY, BZ), (BY, BZ)], late=fine, near=[image, sigma]
    )
    ya, yb = pair_swap(ya, yb, "narrow")
    fa, fb = pair_swap(fa, fb, "wide")
    next_search, next_image, last, products = call(
        part(second_coarse_kernel, swapped),
        [block, block, (count, 1, 2 * ELEMS), (1, 128)],
        near=[right, diagonal, kept, received, sums, solved, ya, yb, fa, fb, search, halo, image, slots],
    )
    last = everywhere(last)
    return tuple(
        call(
            part(last_kernel, sizes),
            [block, block],
            near=[right, products, last, search, image, next_search, next_image],
            final=True,
        )
    )


def solution(mesh):
    in_specs = (
        P("wide", "narrow", None),
        P("wide", "narrow", None),
        P("wide", "narrow", None),
        P(("wide", "narrow"), None),
    )
    out_specs = (P("wide", "narrow", None), P("wide", "narrow", None))
    return jax.shard_map(body, mesh=mesh, in_specs=in_specs, out_specs=out_specs, check_vma=False)
```

```python
import functools

import jax
import jax.numpy as jnp
import numpy as np
from jax import lax
from jax.experimental import pallas as pl
from jax.experimental.pallas import tpu as pltpu
from jax.sharding import PartitionSpec as P

F32 = jnp.float32
BF16 = jnp.bfloat16
BX, BY, BZ = 8, 16, 512
EY, EZ = 2, 64
ELEMS = EY * EZ
YR = 24
YW = YR * (BX + 2)
AB = 208
HZ = 256
HW = 384
STAGED = 4
TABLES = 10
KCOL = 2048
WIDTH = KCOL + 128
AXES = ("wide", "narrow")


def split_const(values):
    high = values.astype(jnp.bfloat16)
    low = (values - high.astype(np.float64)).astype(jnp.bfloat16)
    return high, low


@functools.lru_cache(maxsize=None)
def tables():
    index = np.arange(10, dtype=np.float64)
    basis = np.sqrt(2.0 / 11.0) * np.sin(np.pi * (index[:, None] + 1.0) * (index[None, :] + 1.0) / 11.0)
    values = 2.0 - 2.0 * np.cos(np.pi * (index + 1.0) / 11.0)
    to_z = np.zeros((HZ, HW))
    from_z = np.zeros((HW, HZ))
    beyond = np.zeros((8, HW), np.float32)
    last = HZ // 8 - 1
    for e in range(last + 1):
        at = slice(e, 10 * (last + 1), last + 1)
        for k in range(10):
            z = 8 * e + k - 1
            if 0 <= z < HZ:
                to_z[z, at] = basis[k]
            if 1 <= k <= 8:
                from_z[at, z] = basis[k]
    beyond[0, last : 10 * (last + 1) : last + 1] = basis[9]
    beyond[1, 0 : 10 * (last + 1) : last + 1] = basis[0]
    beyond[2] = 1.0
    beyond[2, : 10 * (last + 1)] = np.repeat(values, last + 1)
    to_xy = np.zeros((10, EY, 10, 10, YR))
    from_xy = np.zeros((BX, BY, 10, EY, 10))
    for e in range(EY):
        for j in range(10):
            y = 8 * e + j - 1
            to_xy[:, e, :, :, y % YR] += basis.T[:, None, :] * basis[j][None, :, None]
            if 1 <= j <= 8:
                from_xy[:, y, :, e, :] = basis[1:9, :, None] * basis[j][None, None, :]
    to_xy = np.pad(to_xy.reshape(200, YW), ((0, AB - 200), (0, 0)))
    from_xy = np.pad(from_xy.reshape(BX * BY, 200), ((0, 0), (0, AB - 200)))
    column = np.zeros((AB, 128), np.float32)
    grid = np.zeros((10, EY, 10, 2))
    grid[..., 0] = values[:, None, None] + values[None, None, :]
    grid[..., 1] = np.arange(EY)[None, :, None]
    column[:200, :2] = grid.reshape(200, 2)
    column[200:, 0] = 1.0
    return split_const(to_xy) + split_const(to_z) + split_const(from_xy) + split_const(from_z) + (column, beyond)


def dot(a, b):
    return jnp.dot(a, b, preferred_element_type=F32)


def split2(x):
    high = x.astype(BF16)
    return high, (x - high.astype(F32)).astype(BF16)


def split3(x):
    high = x.astype(BF16)
    rest = x - high.astype(F32)
    middle = rest.astype(BF16)
    return high, middle, (rest - middle.astype(F32)).astype(BF16)


def dot3(a, b):
    return dot(a[0], b[0]) + dot(a[0], b[1]) + dot(a[1], b[0])


def iota(shape, axis):
    return lax.broadcasted_iota(jnp.int32, shape, axis)


def total(x):
    while x.ndim > 2:
        x = jnp.sum(x, axis=0)
    return jnp.sum(jnp.sum(x, axis=0, keepdims=True), axis=1, keepdims=True)


def gather_table():
    shape = (BZ, EY * ELEMS)
    node, at = iota(shape, 0), iota(shape, 1)
    return jnp.where(at == node // 8 + (at // ELEMS) * (ELEMS + EZ), 1.0, 0.0).astype(BF16)


def spread_table():
    shape = (ELEMS, EY * BZ)
    element, at = iota(shape, 0), iota(shape, 1)
    return jnp.where(at // 8 == element, 1.0, 0.0).astype(BF16)


def element_row(field):
    parts = jnp.concatenate(split3(jnp.sum(field, axis=0)), axis=0)
    sums = dot(parts, gather_table())
    sums = sums[0:16] + sums[16:32] + sums[32:48]
    return jnp.sum(sums[0:8, 0:ELEMS], axis=0, keepdims=True) + jnp.sum(sums[8:16, ELEMS:], axis=0, keepdims=True)


def expand_rows(rows):
    count = rows.shape[0]
    tall = jnp.broadcast_to(rows, (16, ELEMS)) if count == 1 else jnp.concatenate([rows, jnp.zeros((16 - count, ELEMS), F32)], axis=0)
    wide = dot(jnp.concatenate(split3(tall), axis=0), spread_table())
    return (wide[0:16] + wide[16:32] + wide[32:48])[0:count]


def expand_block(row):
    wide = expand_rows(row)
    low = jnp.broadcast_to(wide[:, 0:BZ], (8, BZ))
    high = jnp.broadcast_to(wide[:, BZ:], (8, BZ))
    return jnp.concatenate([low, high], axis=0)


def slot_mask(slots, offset):
    slot_of_row = lax.rem(iota((ELEMS, ELEMS), 0) + offset, ELEMS)
    return slot_of_row.astype(F32) == slots


def to_rows(element_values, slots, offset):
    return jnp.sum(jnp.where(slot_mask(slots, offset), element_values, 0.0), axis=1, keepdims=True)


def to_elements(row_values, slots, offset):
    return jnp.sum(jnp.where(slot_mask(slots, offset), row_values, 0.0), axis=0, keepdims=True)


def project(column, parts):
    out = 0.0
    at = 0
    for part in parts:
        size = part.shape[0]
        out = out + jnp.sum(column[at : at + size] * part[...], axis=0, keepdims=True)
        at += size
    return out


def correct(row, parts):
    out = []
    for part in parts:
        products = part[...] * row
        folded = products[:, 0:128]
        for at in range(128, KCOL, 128):
            folded = folded + products[:, at : at + 128]
        out.append(jnp.sum(folded, axis=1, keepdims=True))
    return jnp.concatenate(out, axis=0)


def store_sum(out_ref, first, second):
    count, _, width = out_ref.shape
    cut = width - 128
    out_ref[:, :, 0:cut] = jnp.broadcast_to(first[None], (count, 1, cut))
    out_ref[:, :, cut:width] = jnp.broadcast_to(second[None], (count, 1, 128))


def lanes(values):
    at = iota((1, 128), 1)
    row = jnp.zeros((1, 128), F32)
    for i, value in enumerate(values):
        row = jnp.where(at == i, value, row)
    return row


def lane(row, i):
    return jnp.sum(jnp.where(iota(row.shape, 1) == i, row, 0.0), axis=1, keepdims=True)


def odd(index):
    return lax.rem(index, 2) == 1


def pair_out(index, low, high):
    return jnp.where(odd(index), low, high), jnp.where(odd(index), high, low)


def pair_in(index, first, second):
    return jnp.where(odd(index), first, second), jnp.where(odd(index), second, first)


def extend_y(block, low, high, depth):
    at = iota((8, BZ), 0)
    tails = []
    for x in range(block.shape[0]):
        tail = jnp.zeros((8, BZ), F32)
        for i in range(depth):
            tail = jnp.where(at == i, high[i][x : x + 1], tail)
            tail = jnp.where(at == 8 - depth + i, low[i][x : x + 1], tail)
        tails.append(tail)
    return jnp.concatenate([block, jnp.stack(tails)], axis=1)


def roll_sum(x):
    count, rows, _ = x.shape
    beside = pltpu.roll(x, 1, 1) + pltpu.roll(x, rows - 1, 1)
    flat = x.reshape(count * rows, BZ)
    at = iota(flat.shape, 1)
    beside_z = jnp.where(at == 0, 0.0, pltpu.roll(flat, 1, 1)) + jnp.where(at == BZ - 1, 0.0, pltpu.roll(flat, BZ - 1, 1))
    return beside + beside_z.reshape(x.shape)


def fine_solve(rows, sigma, tables):
    wh, wl, th, tl, vh, vl, uh, ul, column, beyond = tables
    spectra = dot3((value(wh), value(wl)), split2(rows))
    th, tl, vh, vl, uh, ul, column, beyond = [value(table) for table in (th, tl, vh, vl, uh, ul, column, beyond)]
    nodal = []
    for half in range(2):
        part = spectra[:, half * HZ : (half + 1) * HZ]
        edge = spectra[:, HZ : HZ + 1] if half == 0 else spectra[:, HZ - 1 : HZ]
        part = dot3(split2(part), (th, tl)) + edge * beyond[half : half + 1]
        sig = jnp.where(column[:, 1:2] == 0.0, repeat_lanes(sigma, half), repeat_lanes(sigma, 2 + half))
        part = part / (column[:, 0:1] + beyond[2:3] + sig)
        part = dot3((vh, vl), split2(part))
        nodal.append(dot3(split2(part), (uh, ul)).reshape(BX, BY, HZ))
    return jnp.concatenate(nodal, axis=2)


def value(table):
    return (table.here() if isinstance(table, Loaded) else table)[...]


def repeat_lanes(row, group):
    only = jnp.where(iota((1, ELEMS), 1) // 32 == group, row, 0.0)
    only = only + pltpu.roll(only, 64, 1)
    only = only + pltpu.roll(only, 32, 1)
    return jnp.concatenate([only] * 3, axis=1)


def eye_mask():
    return iota((ELEMS, ELEMS), 0) == iota((ELEMS, ELEMS), 1)


def row_to_column(row):
    return jnp.sum(jnp.where(eye_mask(), row, 0.0), axis=1, keepdims=True)


def column_to_row(column):
    return jnp.sum(jnp.where(eye_mask(), column, 0.0), axis=0, keepdims=True)


def pad_tile(rows):
    at = iota((8, ELEMS), 0)
    tile = jnp.zeros((8, ELEMS), F32)
    for i, row in enumerate(rows):
        tile = jnp.where(at == i, row, tile)
    return jnp.concatenate([tile, jnp.zeros((8, BZ - ELEMS), F32)], axis=1)


def start_kernel(
    late, right_far, diagonal_far, slots_far, c, ya, yb, right, diagonal, slots_out
):
    d = lax.axis_index("narrow")
    right_load = late.start(right_far, right)
    diagonal_load = late.start(diagonal_far, diagonal)
    slots_in = slots_far.here()
    slots = jnp.concatenate([slots_in[0:1], slots_in[1:2]], axis=1).astype(F32)
    slots_out[...] = slots
    right_load.wait()
    row = column_to_row(to_rows(element_row(right[...]) * (1.0 / 16.0), slots, 0))
    c[...] = row
    diagonal_load.wait()
    for i, ref in enumerate((right, diagonal)):
        ya[i], yb[i] = pair_out(d, ref[:, 0, :], ref[:, BY - 1, :])
    ya[2] = pad_tile([row, slots])
    yb[2] = jnp.zeros((8, BZ), F32)


def stage_kernel(swapped, late, factor, *refs):
    d = lax.axis_index("narrow")
    half = ELEMS // 2
    at = pl.multiple_of(d * half, half) if swapped else 0
    there = pl.multiple_of((1 - d) * half, half) if swapped else half
    after, sent, kept, done = refs[STAGED : STAGED + 4]
    late.start(factor.at[pl.ds(at, half)], kept)
    late.start(factor.at[pl.ds(there, half)], sent)
    for source, target in zip(refs[:STAGED], refs[STAGED + 4 :]):
        late.start(source, target)
    done[...] = after[...]


def project_kernel(swapped, late, c, ra, rb, right, diagonal, kept, sent, sums, xa, xb):
    w, d = lax.axis_index("wide"), lax.axis_index("narrow")
    row = c[...]
    if swapped:
        half = ELEMS // 2
        other = ra[2, 0:1, 0:ELEMS]
        row = jnp.where(d == 0, row, pltpu.roll(row, half, 1))
        other = jnp.where(d == 0, pltpu.roll(other, half, 1), other)
        row = jnp.where(iota((1, ELEMS), 1) < half, row, other)
    store_sum(sums, project(row_to_column(row), (kept, sent)), jnp.zeros((1, 128), F32))
    for i, ref in enumerate((right, diagonal)):
        low, high = pair_in(d, ra[i], rb[i])
        layers = [extend_y(ref[x : x + 1], [low[x : x + 1]], [high[x : x + 1]], 1)[0] for x in (0, BX - 1)]
        xa[i], xb[i] = pair_out(w, *layers)


def widened(block, ya, yb, xa, xb, i):
    w, d = lax.axis_index("wide"), lax.axis_index("narrow")
    low, high = pair_in(d, ya[i], yb[i])
    x_low, x_high = pair_in(w, xa[i], xb[i])
    return jnp.concatenate([x_low[None], extend_y(block, [low], [high], 1), x_high[None]], axis=0)


def first_fine_kernel(late, *rest):
    right, diagonal, ya, yb, xa, xb, solved, sigma_out = rest[TABLES:]
    rows = widened(right[...], ya, yb, xa, xb, 0)
    sigma = element_row(diagonal[...]) * (1.0 / 512.0)
    sigma_out[...] = sigma
    tables = rest[TABLES - STAGED : TABLES] + rest[: TABLES - STAGED]
    solved[...] = fine_solve(rows.reshape(YW, BZ), sigma, tables)


def first_coarse_kernel(swapped, late, sums, solved, slots, kept, sent, ya, yb):
    d = lax.axis_index("narrow")
    row = jnp.sum(sums[...], axis=0)[:, 0:KCOL]
    column = correct(row, (kept, sent))
    for i in range(2):
        ya[i], yb[i] = pair_out(d, solved[:, i, :], solved[:, BY - 2 + i, :])
    if swapped:
        values = column_to_row(column)
        values = jnp.where(d == 0, values, pltpu.roll(values, ELEMS // 2, 1))
    else:
        values = to_elements(column, slots[...], 0)
    ya[2] = pad_tile([values])
    yb[2] = ya[2]


def extend_kernel(swapped, late, solved, slots, ra_first, own_ref, ra, rb, search, xa, xb):
    w, d = lax.axis_index("wide"), lax.axis_index("narrow")
    groups = lax.axis_size("narrow")
    own = own_ref[2, 0:1, 0:ELEMS]
    theirs = ra[2, 0:1, 0:ELEMS]
    if swapped:
        half = ELEMS // 2
        at = iota((1, ELEMS), 1) // half
        other = jnp.where(at == d, pltpu.roll(own, half, 1), theirs)
        own = jnp.where(at == d, own, pltpu.roll(theirs, half, 1))
        own = to_elements(row_to_column(own), slots[...], 0)
        other = to_elements(row_to_column(other), ra_first[2, 1:2, 0:ELEMS], 0)
        values_low, values_high = other, other
    else:
        values_low, values_high = pair_in(d, theirs, rb[2, 0:1, 0:ELEMS])
    values_low = jnp.where(d > 0, values_low, 0.0)
    values_high = jnp.where(d < groups - 1, values_high, 0.0)
    wide = expand_rows(jnp.concatenate([own, values_low, values_high], axis=0)) * (1.0 / 16.0)
    coarse = jnp.concatenate(
        [jnp.broadcast_to(wide[0:1, 0:BZ], (8, BZ)), jnp.broadcast_to(wide[0:1, BZ:], (8, BZ))], axis=0
    )
    low, high = [], []
    for i in range(2):
        one, two = pair_in(d, ra[i], rb[i])
        low.append(one + wide[1:2, BZ:])
        high.append(two + wide[2:3, 0:BZ])
    block = extend_y(solved[...] + coarse[None], low, high, 2)
    search[...] = block
    xa[...], xb[...] = pair_out(w, block[0:2], block[BX - 2 : BX])


def operator_kernel(
    swapped, sizes, late, right, diagonal, kept, received, search, sa, sb, ya, yb, xa, xb, slots, sums, image_out, halo
):
    w, d = lax.axis_index("wide"), lax.axis_index("narrow")
    owned, offset = (kept, received), d * (ELEMS // 2) if swapped else 0
    s_low, s_high = pair_in(w, sa[...], sb[...])
    vector = jnp.concatenate([s_low, search[...], s_high], axis=0)
    coefficient = widened(diagonal[...], ya, yb, xa, xb, 1)
    centre = vector[1 : BX + 3]
    image = (6.0 + coefficient) * centre - (vector[0 : BX + 2] + vector[2 : BX + 4] + roll_sum(centre))
    x = iota(image.shape, 0)
    y = iota(image.shape, 1)
    inside = (y < BY) | ((y == BY) & (d < sizes[1] - 1)) | ((y == YR - 1) & (d > 0))
    inside &= ((x > 0) | (w > 0)) & ((x < BX + 1) | (w < sizes[0] - 1))
    image = jnp.where(inside, image, 0.0)
    image_out[...] = image
    halo[0:BY] = s_low[1, 0:BY]
    halo[BY : 2 * BY] = s_high[0, 0:BY]
    halo[2 * BY : 2 * BY + 8] = search[:, YR - 1, :]
    halo[2 * BY + 8 : 3 * BY] = search[:, BY, :]
    own = image[1 : BX + 1, 0:BY]
    own_search = search[:, 0:BY, :]
    column = to_rows(element_row(own) * (1.0 / 16.0), slots[...], offset)
    extra = lanes([total(right[...] * own_search), total(own_search * own)])
    store_sum(sums, project(column, owned), extra)


def second_fine_kernel(late, *rest):
    w, d = lax.axis_index("wide"), lax.axis_index("narrow")
    image, sigma, solved, ya, yb, xa, xb = rest[TABLES:]
    out = fine_solve(image[...].reshape(YW, BZ), sigma[...], rest[:TABLES])
    solved[...] = out
    ya[...], yb[...] = pair_out(d, solved[:, 0, :], solved[:, BY - 1, :])
    xa[...], xb[...] = pair_out(w, out[0], out[BX - 1])


def second_coarse_kernel(
    swapped, late, right, diagonal, kept, received, sums, solved, fya, fyb, fxa, fxb, search, halo, image, slots,
    search_out, image_out, last, products,
):
    w, d = lax.axis_index("wide"), lax.axis_index("narrow")
    owned, offset = (kept, received), d * (ELEMS // 2) if swapped else 0
    row = jnp.sum(sums[...], axis=0)
    products[...] = row[:, KCOL:WIDTH]
    step = lane(row[:, KCOL:WIDTH], 0) / lane(row[:, KCOL:WIDTH], 1)
    values = to_elements(correct(row[:, 0:KCOL], owned), slots[...], offset)
    coarse = expand_block(values * (1.0 / 16.0))
    own_search = search[:, 0:BY, :]
    own_image = image[1 : BX + 1, 0:BY, :]
    vector = own_search - step * (solved[...] + coarse[None])
    f_low, f_high = pair_in(w, fxa[...], fxb[...])
    x_low = halo[0:BY] - step * f_low
    x_high = halo[BY : 2 * BY] - step * f_high
    g_low, g_high = pair_in(d, fya[...], fyb[...])
    y_low = halo[2 * BY : 2 * BY + 8] - step * g_low
    y_high = halo[2 * BY + 8 : 3 * BY] - step * g_high
    beside = roll_sum(extend_y(vector, [y_low], [y_high], 1))[:, 0:BY]
    beside = beside + jnp.concatenate([x_low[None], vector[0 : BX - 1]], axis=0)
    beside = beside + jnp.concatenate([vector[1:BX], x_high[None]], axis=0)
    next_image = (6.0 + diagonal.here()[...]) * vector - beside
    search_out[...] = vector
    image_out[...] = next_image
    residual = right.here()[...] - step * own_image
    edges = total(coarse * (x_low + x_high)) + total(y_low * coarse[0:1]) + total(y_high * coarse[BY - 1 : BY])
    store_sum(
        last,
        values,
        lanes([total(residual * vector), total(vector * next_image) + step * edges, total(vector * own_image)]),
    )


def last_kernel(sizes, late, right, products, last, search, image, next_search, next_image, x_out, r_out):
    w, d = lax.axis_index("wide"), lax.axis_index("narrow")
    groups = sizes[1]
    count = sizes[0] * groups
    product, bottom = lane(products[...], 0), lane(products[...], 1)
    step = product / bottom
    z = last[:, 0, 0:ELEMS]
    rows = iota((count, ELEMS), 0)
    at = iota((count, ELEMS), 1)
    faces = jnp.where(rows < count - groups, z * pltpu.roll(z, count - groups, 0), 0.0)
    across = pltpu.roll(pltpu.roll(z, count - 1, 0), EZ, 1)
    faces = faces + jnp.where((lax.rem(rows, groups) < groups - 1) & (at >= EZ), z * across, 0.0)
    sums = jnp.sum(last[:, :, ELEMS:], axis=0)
    next_product = lane(sums, 0)
    quadratic = lane(sums, 1) - step * step * 0.5 * total(faces)
    cross = lane(sums, 2)
    me = w * groups + d
    picked = []
    for index, there in ((me - groups, w > 0), (me + groups, w < sizes[0] - 1), (me - 1, d > 0), (me + 1, d < groups - 1)):
        picked.append(jnp.sum(jnp.where((rows == index) & there, z, 0.0), axis=0, keepdims=True))
    wide = expand_rows(jnp.concatenate(picked, axis=0)) * (1.0 / 16.0)
    layers = []
    for i in range(2):
        low = jnp.broadcast_to(wide[i : i + 1, 0:BZ], (8, BZ))
        high = jnp.broadcast_to(wide[i : i + 1, BZ:], (8, BZ))
        layers.append(jnp.concatenate([low, high], axis=0)[None])
    shape = (BX, BY, BZ)
    x, y = iota(shape, 0), iota(shape, 1)
    missing = jnp.where(x == 0, layers[0], 0.0) + jnp.where(x == BX - 1, layers[1], 0.0)
    missing = missing + jnp.where(y == 0, wide[2:3, BZ:][None], 0.0) + jnp.where(y == BY - 1, wide[3:4, 0:BZ][None], 0.0)
    ratio = next_product / product
    curvature = quadratic + 2.0 * ratio * cross + ratio * ratio * bottom
    step_next = next_product / curvature
    own_search = search[:, 0:BY, :]
    own_image = image[1 : BX + 1, 0:BY, :]
    direction = next_search[...] + ratio * own_search
    total_image = next_image[...] + step * missing + ratio * own_image
    x_out[...] = step * own_search + step_next * direction
    r_out[...] = (right.here()[...] - step * own_image) - step_next * total_image


class Loaded:
    def __init__(self, copy, ref):
        self.copy, self.ref, self.ready = copy, ref, False

    def wait(self):
        if not self.ready:
            self.copy.wait()
            self.ready = True

    def here(self):
        self.wait()
        return self.ref


class Copies:
    def __init__(self, semaphores):
        self.semaphores, self.all = semaphores, []

    def start(self, source, target):
        copy = pltpu.make_async_copy(source, target, self.semaphores.at[len(self.all)])
        copy.start()
        self.all.append(Loaded(copy, target))
        return self.all[-1]

    def finish(self):
        for loaded in self.all:
            loaded.wait()


def call(kernel, outs, far=(), late=(), near=(), final=False):
    first, second = len(far), len(far) + len(late)

    def run(*refs):
        end = len(refs) - 1 - len(late)
        copies = Copies(refs[-1])
        loaded = [copies.start(source, target) for source, target in zip(refs[first:second], refs[end:-1])]
        kernel(copies, *refs[:first], *loaded, *refs[second:end])
        copies.finish()

    shape_of = jax.ShapeDtypeStruct if final else pltpu.VMEM
    spaces = [pltpu.HBM] * second + [pltpu.VMEM] * len(near)
    return pl.pallas_call(
        run,
        out_shape=[shape_of(getattr(out, "shape", out), getattr(out, "dtype", F32)) for out in outs],
        in_specs=[pl.BlockSpec(memory_space=space) for space in spaces],
        out_specs=[pl.BlockSpec(memory_space=pltpu.VMEM)] * len(outs),
        scratch_shapes=[*(pltpu.VMEM(array.shape, array.dtype) for array in late), pltpu.SemaphoreType.DMA((second + 2,))],
        compiler_params=pltpu.CompilerParams(vmem_limit_bytes=16 * 1024 * 1024),
    )(*(pltpu.with_memory_space_constraint(array, pltpu.HBM) for array in (*far, *late)), *near)


def pair_swap(first, second, axis):
    size = lax.axis_size(axis)
    received = []
    for value, begin in ((first, 0), (second, 1)):
        perm = []
        for i in range(begin, size - 1, 2):
            perm += [(i, i + 1), (i + 1, i)]
        received.append(lax.ppermute(value, axis, perm) if perm else jnp.zeros_like(value))
    return received


def everywhere(rows):
    return lax.all_to_all(rows, AXES, split_axis=0, concat_axis=0, tiled=True)


def body(right, diagonal, coarse_slot, factor):
    sizes = (lax.axis_size("wide"), lax.axis_size("narrow"))
    groups = sizes[1]
    count = sizes[0] * groups
    fine = [jnp.asarray(c) for c in tables()]
    slots = coarse_slot.reshape(EY, EZ)
    swapped = groups == 2
    if not swapped:
        factor = factor.reshape(groups, ELEMS // groups, KCOL)
        factor = lax.all_to_all(factor, "narrow", split_axis=0, concat_axis=0, tiled=True).reshape(ELEMS, KCOL)
    part = functools.partial

    block, layer, extended = (BX, BY, BZ), (YR, BZ), (BX, YR, BZ)
    y_shape, x_shape, half = (3, BX, BZ), (2, YR, BZ), (ELEMS // 2, KCOL)
    right_far, diagonal_far = right, diagonal
    c, ya, yb, right, diagonal, slots = call(
        start_kernel, [(1, ELEMS), y_shape, y_shape, block, block, (1, ELEMS)], far=[right, diagonal], late=[slots]
    )
    ya, yb = pair_swap(ya, yb, "narrow")
    sent, kept, c, *near = call(
        part(stage_kernel, swapped), [half, half, (1, ELEMS), *fine[:STAGED]], far=[factor, *fine[:STAGED]], near=[c]
    )
    sums, xa, xb = call(
        part(project_kernel, swapped), [(count, 1, WIDTH), x_shape, x_shape], near=[c, ya, yb, right, diagonal, kept, sent]
    )
    sums = everywhere(sums)
    xa, xb = pair_swap(xa, xb, "wide")
    solved, sigma = call(first_fine_kernel, [block, (1, ELEMS)], late=fine[STAGED:], near=[*near, right, diagonal, ya, yb, xa, xb])
    ta, tb = call(part(first_coarse_kernel, swapped), [y_shape, y_shape], near=[sums, solved, slots, kept, sent])
    ra, rb = pair_swap(ta, tb, "narrow")
    received = lax.ppermute(sent, "narrow", [(0, 1), (1, 0)]) if swapped else sent
    search, sa, sb = call(
        part(extend_kernel, swapped),
        [extended, (2,) + layer, (2,) + layer],
        near=[solved, slots, ya, ta, ra, rb],
    )
    sa, sb = pair_swap(sa, sb, "wide")
    sums, image, halo = call(
        part(operator_kernel, swapped, sizes),
        [(count, 1, WIDTH), (BX + 2, YR, BZ), (3 * BY, BZ)],
        near=[right, diagonal, kept, received, search, sa, sb, ya, yb, xa, xb, slots],
    )
    sums = everywhere(sums)
    solved, ya, yb, fa, fb = call(
        second_fine_kernel, [block, (BX, BZ), (BX, BZ), (BY, BZ), (BY, BZ)], late=fine, near=[image, sigma]
    )
    ya, yb = pair_swap(ya, yb, "narrow")
    fa, fb = pair_swap(fa, fb, "wide")
    next_search, next_image, last, products = call(
        part(second_coarse_kernel, swapped),
        [block, block, (count, 1, 2 * ELEMS), (1, 128)],
        late=[right_far, diagonal_far],
        near=[kept, received, sums, solved, ya, yb, fa, fb, search, halo, image, slots],
    )
    last = everywhere(last)
    return tuple(
        call(
            part(last_kernel, sizes),
            [block, block],
            late=[right_far],
            near=[products, last, search, image, next_search, next_image],
            final=True,
        )
    )


def solution(mesh):
    in_specs = (
        P("wide", "narrow", None),
        P("wide", "narrow", None),
        P("wide", "narrow", None),
        P(("wide", "narrow"), None),
    )
    out_specs = (P("wide", "narrow", None), P("wide", "narrow", None))
    return jax.shard_map(body, mesh=mesh, in_specs=in_specs, out_specs=out_specs, check_vma=False)
```

```python
import functools

import jax
import jax.numpy as jnp
import numpy as np
from jax import lax
from jax.experimental import pallas as pl
from jax.experimental.pallas import tpu as pltpu
from jax.sharding import PartitionSpec as P

F32 = jnp.float32
BF16 = jnp.bfloat16
BX, BY, BZ = 8, 16, 512
EY, EZ = 2, 64
ELEMS = EY * EZ
YR = 24
YW = YR * (BX + 2)
AB = 208
HZ = 256
HW = 384
STAGED = 3
TABLES = 10
KCOL = 2048
WIDTH = KCOL + 128
AXES = ("wide", "narrow")


def split_const(values):
    high = values.astype(jnp.bfloat16)
    low = (values - high.astype(np.float64)).astype(jnp.bfloat16)
    return high, low


@functools.lru_cache(maxsize=None)
def tables():
    index = np.arange(10, dtype=np.float64)
    basis = np.sqrt(2.0 / 11.0) * np.sin(np.pi * (index[:, None] + 1.0) * (index[None, :] + 1.0) / 11.0)
    values = 2.0 - 2.0 * np.cos(np.pi * (index + 1.0) / 11.0)
    to_z = np.zeros((HZ, HW))
    from_z = np.zeros((HW, HZ))
    beyond = np.zeros((8, HW), np.float32)
    last = HZ // 8 - 1
    for e in range(last + 1):
        at = slice(e, 10 * (last + 1), last + 1)
        for k in range(10):
            z = 8 * e + k - 1
            if 0 <= z < HZ:
                to_z[z, at] = basis[k]
            if 1 <= k <= 8:
                from_z[at, z] = basis[k]
    beyond[0, last : 10 * (last + 1) : last + 1] = basis[9]
    beyond[1, 0 : 10 * (last + 1) : last + 1] = basis[0]
    beyond[2] = 1.0
    beyond[2, : 10 * (last + 1)] = np.repeat(values, last + 1)
    to_xy = np.zeros((10, EY, 10, 10, YR))
    from_xy = np.zeros((BX, BY, 10, EY, 10))
    for e in range(EY):
        for j in range(10):
            y = 8 * e + j - 1
            to_xy[:, e, :, :, y % YR] += basis.T[:, None, :] * basis[j][None, :, None]
            if 1 <= j <= 8:
                from_xy[:, y, :, e, :] = basis[1:9, :, None] * basis[j][None, None, :]
    to_xy = np.pad(to_xy.reshape(200, YW), ((0, AB - 200), (0, 0)))
    from_xy = np.pad(from_xy.reshape(BX * BY, 200), ((0, 0), (0, AB - 200)))
    column = np.zeros((AB, 128), np.float32)
    grid = np.zeros((10, EY, 10, 2))
    grid[..., 0] = values[:, None, None] + values[None, None, :]
    grid[..., 1] = np.arange(EY)[None, :, None]
    column[:200, :2] = grid.reshape(200, 2)
    column[200:, 0] = 1.0
    return split_const(to_xy) + split_const(to_z) + split_const(from_xy) + split_const(from_z) + (column, beyond)


def dot(a, b):
    return jnp.dot(a, b, preferred_element_type=F32)


def split2(x):
    high = x.astype(BF16)
    return high, (x - high.astype(F32)).astype(BF16)


def split3(x):
    high = x.astype(BF16)
    rest = x - high.astype(F32)
    middle = rest.astype(BF16)
    return high, middle, (rest - middle.astype(F32)).astype(BF16)


def dot3(a, b):
    return dot(a[0], b[0]) + dot(a[0], b[1]) + dot(a[1], b[0])


def iota(shape, axis):
    return lax.broadcasted_iota(jnp.int32, shape, axis)


def total(x):
    while x.ndim > 2:
        x = jnp.sum(x, axis=0)
    return jnp.sum(jnp.sum(x, axis=0, keepdims=True), axis=1, keepdims=True)


def gather_table():
    shape = (BZ, EY * ELEMS)
    node, at = iota(shape, 0), iota(shape, 1)
    return jnp.where(at == node // 8 + (at // ELEMS) * (ELEMS + EZ), 1.0, 0.0).astype(BF16)


def spread_table():
    shape = (ELEMS, EY * BZ)
    element, at = iota(shape, 0), iota(shape, 1)
    return jnp.where(at // 8 == element, 1.0, 0.0).astype(BF16)


def element_row(field, table):
    parts = jnp.concatenate(split3(jnp.sum(field, axis=0)), axis=0)
    sums = dot(parts, table)
    sums = sums[0:16] + sums[16:32] + sums[32:48]
    return jnp.sum(sums[0:8, 0:ELEMS], axis=0, keepdims=True) + jnp.sum(sums[8:16, ELEMS:], axis=0, keepdims=True)


def expand_rows(rows):
    count = rows.shape[0]
    tall = jnp.broadcast_to(rows, (16, ELEMS)) if count == 1 else jnp.concatenate([rows, jnp.zeros((16 - count, ELEMS), F32)], axis=0)
    wide = dot(jnp.concatenate(split3(tall), axis=0), spread_table())
    return (wide[0:16] + wide[16:32] + wide[32:48])[0:count]


def expand_block(row):
    wide = expand_rows(row)
    low = jnp.broadcast_to(wide[:, 0:BZ], (8, BZ))
    high = jnp.broadcast_to(wide[:, BZ:], (8, BZ))
    return jnp.concatenate([low, high], axis=0)


def slot_mask(slots, offset):
    slot_of_row = lax.rem(iota((ELEMS, ELEMS), 0) + offset, ELEMS)
    return slot_of_row.astype(F32) == slots


def to_rows(element_values, slots, offset):
    return jnp.sum(jnp.where(slot_mask(slots, offset), element_values, 0.0), axis=1, keepdims=True)


def to_elements(row_values, slots, offset):
    return jnp.sum(jnp.where(slot_mask(slots, offset), row_values, 0.0), axis=0, keepdims=True)


def project(column, parts):
    out = 0.0
    at = 0
    for part in parts:
        size = part.shape[0]
        out = out + jnp.sum(column[at : at + size] * part[...], axis=0, keepdims=True)
        at += size
    return out


def correct(row, parts):
    out = []
    for part in parts:
        products = part[...] * row
        folded = products[:, 0:128]
        for at in range(128, KCOL, 128):
            folded = folded + products[:, at : at + 128]
        out.append(jnp.sum(folded, axis=1, keepdims=True))
    return jnp.concatenate(out, axis=0)


def store_sum(out_ref, first, second):
    count, _, width = out_ref.shape
    cut = width - 128
    out_ref[:, :, 0:cut] = jnp.broadcast_to(first[None], (count, 1, cut))
    out_ref[:, :, cut:width] = jnp.broadcast_to(second[None], (count, 1, 128))


def lanes(values):
    at = iota((1, 128), 1)
    row = jnp.zeros((1, 128), F32)
    for i, value in enumerate(values):
        row = jnp.where(at == i, value, row)
    return row


def lane(row, i):
    return jnp.sum(jnp.where(iota(row.shape, 1) == i, row, 0.0), axis=1, keepdims=True)


def odd(index):
    return lax.rem(index, 2) == 1


def pair_out(index, low, high):
    return jnp.where(odd(index), low, high), jnp.where(odd(index), high, low)


def pair_in(index, first, second):
    return jnp.where(odd(index), first, second), jnp.where(odd(index), second, first)


def extend_y(block, low, high, depth):
    at = iota((8, BZ), 0)
    tails = []
    for x in range(block.shape[0]):
        tail = jnp.zeros((8, BZ), F32)
        for i in range(depth):
            tail = jnp.where(at == i, high[i][x : x + 1], tail)
            tail = jnp.where(at == 8 - depth + i, low[i][x : x + 1], tail)
        tails.append(tail)
    return jnp.concatenate([block, jnp.stack(tails)], axis=1)


def roll_sum(x):
    count, rows, _ = x.shape
    beside = pltpu.roll(x, 1, 1) + pltpu.roll(x, rows - 1, 1)
    flat = x.reshape(count * rows, BZ)
    at = iota(flat.shape, 1)
    beside_z = jnp.where(at == 0, 0.0, pltpu.roll(flat, 1, 1)) + jnp.where(at == BZ - 1, 0.0, pltpu.roll(flat, BZ - 1, 1))
    return beside + beside_z.reshape(x.shape)


def fine_solve(rows, sigma, tables):
    wh, wl, th, tl, vh, vl, uh, ul, column, beyond = tables
    spectra = dot3((value(wh), value(wl)), split2(rows))
    th, tl, vh, vl, uh, ul, column, beyond = [value(table) for table in (th, tl, vh, vl, uh, ul, column, beyond)]
    nodal = []
    for half in range(2):
        part = spectra[:, half * HZ : (half + 1) * HZ]
        edge = spectra[:, HZ : HZ + 1] if half == 0 else spectra[:, HZ - 1 : HZ]
        part = dot3(split2(part), (th, tl)) + edge * beyond[half : half + 1]
        sig = jnp.where(column[:, 1:2] == 0.0, repeat_lanes(sigma, half), repeat_lanes(sigma, 2 + half))
        part = part / (column[:, 0:1] + beyond[2:3] + sig)
        part = dot3((vh, vl), split2(part))
        nodal.append(dot3(split2(part), (uh, ul)).reshape(BX, BY, HZ))
    return jnp.concatenate(nodal, axis=2)


def value(table):
    return (table.here() if isinstance(table, Loaded) else table)[...]


def repeat_lanes(row, group):
    only = jnp.where(iota((1, ELEMS), 1) // 32 == group, row, 0.0)
    only = only + pltpu.roll(only, 64, 1)
    only = only + pltpu.roll(only, 32, 1)
    return jnp.concatenate([only] * 3, axis=1)


def eye_mask():
    return iota((ELEMS, ELEMS), 0) == iota((ELEMS, ELEMS), 1)


def row_to_column(row):
    return jnp.sum(jnp.where(eye_mask(), row, 0.0), axis=1, keepdims=True)


def column_to_row(column):
    return jnp.sum(jnp.where(eye_mask(), column, 0.0), axis=0, keepdims=True)


def pad_tile(rows):
    at = iota((8, ELEMS), 0)
    tile = jnp.zeros((8, ELEMS), F32)
    for i, row in enumerate(rows):
        tile = jnp.where(at == i, row, tile)
    return jnp.concatenate([tile, jnp.zeros((8, BZ - ELEMS), F32)], axis=1)


def start_kernel(
    late, right_far, diagonal_far, slots_far, c, ya, yb, right, diagonal, slots_out, table_out
):
    d = lax.axis_index("narrow")
    right_load = late.start(right_far, right)
    diagonal_load = late.start(diagonal_far, diagonal)
    slots_in = slots_far.here()
    slots = jnp.concatenate([slots_in[0:1], slots_in[1:2]], axis=1).astype(F32)
    slots_out[...] = slots
    table = gather_table()
    table_out[...] = table
    right_load.wait()
    row = column_to_row(to_rows(element_row(right[...], table) * (1.0 / 16.0), slots, 0))
    c[...] = row
    diagonal_load.wait()
    for i, ref in enumerate((right, diagonal)):
        ya[i], yb[i] = pair_out(d, ref[:, 0, :], ref[:, BY - 1, :])
    ya[2] = pad_tile([row, slots])
    yb[2] = jnp.zeros((8, BZ), F32)


def stage_kernel(swapped, late, factor, *refs):
    d = lax.axis_index("narrow")
    half = ELEMS // 2
    at = pl.multiple_of(d * half, half) if swapped else 0
    there = pl.multiple_of((1 - d) * half, half) if swapped else half
    after, diagonal, table, sent, kept, done, sigma = refs[STAGED : STAGED + 7]
    late.start(factor.at[pl.ds(at, half)], kept)
    late.start(factor.at[pl.ds(there, half)], sent)
    for source, target in zip(refs[:STAGED], refs[STAGED + 7 :]):
        late.start(source, target)
    done[...] = after[...]
    sigma[...] = element_row(diagonal[...], table[...]) * (1.0 / 512.0)


def project_kernel(swapped, late, c, ra, rb, right, diagonal, kept, sent, sums, xa, xb):
    w, d = lax.axis_index("wide"), lax.axis_index("narrow")
    row = c[...]
    if swapped:
        half = ELEMS // 2
        other = ra[2, 0:1, 0:ELEMS]
        row = jnp.where(d == 0, row, pltpu.roll(row, half, 1))
        other = jnp.where(d == 0, pltpu.roll(other, half, 1), other)
        row = jnp.where(iota((1, ELEMS), 1) < half, row, other)
    store_sum(sums, project(row_to_column(row), (kept, sent)), jnp.zeros((1, 128), F32))
    for i, ref in enumerate((right, diagonal)):
        low, high = pair_in(d, ra[i], rb[i])
        layers = [extend_y(ref[x : x + 1], [low[x : x + 1]], [high[x : x + 1]], 1)[0] for x in (0, BX - 1)]
        xa[i], xb[i] = pair_out(w, *layers)


def widened(block, ya, yb, xa, xb, i):
    w, d = lax.axis_index("wide"), lax.axis_index("narrow")
    low, high = pair_in(d, ya[i], yb[i])
    x_low, x_high = pair_in(w, xa[i], xb[i])
    return jnp.concatenate([x_low[None], extend_y(block, [low], [high], 1), x_high[None]], axis=0)


def first_fine_kernel(late, *rest):
    right, ya, yb, xa, xb, sigma, solved = rest[TABLES:]
    rows = widened(right[...], ya, yb, xa, xb, 0)
    tables = rest[TABLES - STAGED : TABLES] + rest[: TABLES - STAGED]
    solved[...] = fine_solve(rows.reshape(YW, BZ), sigma[...], tables)


def first_coarse_kernel(swapped, late, sums, solved, slots, kept, sent, ya, yb):
    d = lax.axis_index("narrow")
    row = jnp.sum(sums[...], axis=0)[:, 0:KCOL]
    column = correct(row, (kept, sent))
    for i in range(2):
        ya[i], yb[i] = pair_out(d, solved[:, i, :], solved[:, BY - 2 + i, :])
    if swapped:
        values = column_to_row(column)
        values = jnp.where(d == 0, values, pltpu.roll(values, ELEMS // 2, 1))
    else:
        values = to_elements(column, slots[...], 0)
    ya[2] = pad_tile([values])
    yb[2] = ya[2]


def extend_kernel(swapped, late, solved, slots, ra_first, own_ref, ra, rb, search, xa, xb):
    w, d = lax.axis_index("wide"), lax.axis_index("narrow")
    groups = lax.axis_size("narrow")
    own = own_ref[2, 0:1, 0:ELEMS]
    theirs = ra[2, 0:1, 0:ELEMS]
    if swapped:
        half = ELEMS // 2
        at = iota((1, ELEMS), 1) // half
        other = jnp.where(at == d, pltpu.roll(own, half, 1), theirs)
        own = jnp.where(at == d, own, pltpu.roll(theirs, half, 1))
        own = to_elements(row_to_column(own), slots[...], 0)
        other = to_elements(row_to_column(other), ra_first[2, 1:2, 0:ELEMS], 0)
        values_low, values_high = other, other
    else:
        values_low, values_high = pair_in(d, theirs, rb[2, 0:1, 0:ELEMS])
    values_low = jnp.where(d > 0, values_low, 0.0)
    values_high = jnp.where(d < groups - 1, values_high, 0.0)
    wide = expand_rows(jnp.concatenate([own, values_low, values_high], axis=0)) * (1.0 / 16.0)
    coarse = jnp.concatenate(
        [jnp.broadcast_to(wide[0:1, 0:BZ], (8, BZ)), jnp.broadcast_to(wide[0:1, BZ:], (8, BZ))], axis=0
    )
    low, high = [], []
    for i in range(2):
        one, two = pair_in(d, ra[i], rb[i])
        low.append(one + wide[1:2, BZ:])
        high.append(two + wide[2:3, 0:BZ])
    block = extend_y(solved[...] + coarse[None], low, high, 2)
    search[...] = block
    xa[...], xb[...] = pair_out(w, block[0:2], block[BX - 2 : BX])


def interior_kernel(late, right, diagonal, search, ya, yb, image, product, table):
    d = lax.axis_index("narrow")
    low, high = pair_in(d, ya[1], yb[1])
    centre = search[...]
    part = (6.0 + extend_y(diagonal[...], [low], [high], 1)) * centre - roll_sum(centre)
    zero = jnp.zeros((1, YR, BZ), F32)
    part = part - jnp.concatenate([zero, centre[0 : BX - 1]], axis=0) - jnp.concatenate([centre[1:BX], zero], axis=0)
    image[...] = part
    product[...] = lanes([total(right[...] * centre[:, 0:BY])])
    table[...] = gather_table()


def operator_kernel(
    swapped, sizes, late, kept, received, search, inner, product, table, sa, sb, xa, xb, slots, sums, image_out, halo
):
    w, d = lax.axis_index("wide"), lax.axis_index("narrow")
    owned, offset = (kept, received), d * (ELEMS // 2) if swapped else 0
    s_low, s_high = pair_in(w, sa[...], sb[...])
    d_low, d_high = pair_in(w, xa[1], xb[1])
    low = (6.0 + d_low) * s_low[1] - s_low[0] - search[0] - roll_sum(s_low[1:2])[0]
    high = (6.0 + d_high) * s_high[0] - s_high[1] - search[BX - 1] - roll_sum(s_high[0:1])[0]
    y = iota((YR, BZ), 0)
    inside = (y < BY) | ((y == BY) & (d < sizes[1] - 1)) | ((y == YR - 1) & (d > 0))
    image_out[0] = jnp.where(inside & (w > 0), low, 0.0)
    image_out[1] = jnp.where(inside, inner[0] - s_low[1], 0.0)
    image_out[2:BX] = jnp.where(inside[None], inner[1 : BX - 1], 0.0)
    image_out[BX] = jnp.where(inside, inner[BX - 1] - s_high[0], 0.0)
    image_out[BX + 1] = jnp.where(inside & (w < sizes[0] - 1), high, 0.0)
    halo[0:BY] = s_low[1, 0:BY]
    halo[BY : 2 * BY] = s_high[0, 0:BY]
    halo[2 * BY : 2 * BY + 8] = search[:, YR - 1, :]
    halo[2 * BY + 8 : 3 * BY] = search[:, BY, :]
    own = image_out[1 : BX + 1, 0:BY, :]
    column = to_rows(element_row(own, table[...]) * (1.0 / 16.0), slots[...], offset)
    extra = lanes([lane(product[...], 0), total(search[:, 0:BY, :] * own)])
    store_sum(sums, project(column, owned), extra)


def second_fine_kernel(late, *rest):
    w, d = lax.axis_index("wide"), lax.axis_index("narrow")
    image, sigma, solved, ya, yb, xa, xb = rest[TABLES:]
    out = fine_solve(image[...].reshape(YW, BZ), sigma[...], rest[:TABLES])
    solved[...] = out
    ya[...], yb[...] = pair_out(d, solved[:, 0, :], solved[:, BY - 1, :])
    xa[...], xb[...] = pair_out(w, out[0], out[BX - 1])


def second_coarse_kernel(
    swapped, late, right, diagonal, kept, received, sums, solved, fya, fyb, fxa, fxb, search, halo, image, slots,
    search_out, image_out, last, products,
):
    w, d = lax.axis_index("wide"), lax.axis_index("narrow")
    owned, offset = (kept, received), d * (ELEMS // 2) if swapped else 0
    row = jnp.sum(sums[...], axis=0)
    products[...] = row[:, KCOL:WIDTH]
    step = lane(row[:, KCOL:WIDTH], 0) / lane(row[:, KCOL:WIDTH], 1)
    values = to_elements(correct(row[:, 0:KCOL], owned), slots[...], offset)
    coarse = expand_block(values * (1.0 / 16.0))
    own_search = search[:, 0:BY, :]
    own_image = image[1 : BX + 1, 0:BY, :]
    vector = own_search - step * (solved[...] + coarse[None])
    f_low, f_high = pair_in(w, fxa[...], fxb[...])
    x_low = halo[0:BY] - step * f_low
    x_high = halo[BY : 2 * BY] - step * f_high
    g_low, g_high = pair_in(d, fya[...], fyb[...])
    y_low = halo[2 * BY : 2 * BY + 8] - step * g_low
    y_high = halo[2 * BY + 8 : 3 * BY] - step * g_high
    beside = roll_sum(extend_y(vector, [y_low], [y_high], 1))[:, 0:BY]
    beside = beside + jnp.concatenate([x_low[None], vector[0 : BX - 1]], axis=0)
    beside = beside + jnp.concatenate([vector[1:BX], x_high[None]], axis=0)
    next_image = (6.0 + diagonal[...]) * vector - beside
    search_out[...] = vector
    image_out[...] = next_image
    residual = right[...] - step * own_image
    edges = total(coarse * (x_low + x_high)) + total(y_low * coarse[0:1]) + total(y_high * coarse[BY - 1 : BY])
    store_sum(
        last,
        values,
        lanes([total(residual * vector), total(vector * next_image) + step * edges, total(vector * own_image)]),
    )


def last_kernel(sizes, late, right, products, last, search, image, next_search, next_image, x_out, r_out):
    w, d = lax.axis_index("wide"), lax.axis_index("narrow")
    groups = sizes[1]
    count = sizes[0] * groups
    product, bottom = lane(products[...], 0), lane(products[...], 1)
    step = product / bottom
    z = last[:, 0, 0:ELEMS]
    rows = iota((count, ELEMS), 0)
    at = iota((count, ELEMS), 1)
    faces = jnp.where(rows < count - groups, z * pltpu.roll(z, count - groups, 0), 0.0)
    across = pltpu.roll(pltpu.roll(z, count - 1, 0), EZ, 1)
    faces = faces + jnp.where((lax.rem(rows, groups) < groups - 1) & (at >= EZ), z * across, 0.0)
    sums = jnp.sum(last[:, :, ELEMS:], axis=0)
    next_product = lane(sums, 0)
    quadratic = lane(sums, 1) - step * step * 0.5 * total(faces)
    cross = lane(sums, 2)
    me = w * groups + d
    picked = []
    for index, there in ((me - groups, w > 0), (me + groups, w < sizes[0] - 1), (me - 1, d > 0), (me + 1, d < groups - 1)):
        picked.append(jnp.sum(jnp.where((rows == index) & there, z, 0.0), axis=0, keepdims=True))
    wide = expand_rows(jnp.concatenate(picked, axis=0)) * (1.0 / 16.0)
    layers = []
    for i in range(2):
        low = jnp.broadcast_to(wide[i : i + 1, 0:BZ], (8, BZ))
        high = jnp.broadcast_to(wide[i : i + 1, BZ:], (8, BZ))
        layers.append(jnp.concatenate([low, high], axis=0)[None])
    shape = (BX, BY, BZ)
    x, y = iota(shape, 0), iota(shape, 1)
    missing = jnp.where(x == 0, layers[0], 0.0) + jnp.where(x == BX - 1, layers[1], 0.0)
    missing = missing + jnp.where(y == 0, wide[2:3, BZ:][None], 0.0) + jnp.where(y == BY - 1, wide[3:4, 0:BZ][None], 0.0)
    ratio = next_product / product
    curvature = quadratic + 2.0 * ratio * cross + ratio * ratio * bottom
    step_next = next_product / curvature
    own_search = search[:, 0:BY, :]
    own_image = image[1 : BX + 1, 0:BY, :]
    direction = next_search[...] + ratio * own_search
    total_image = next_image[...] + step * missing + ratio * own_image
    x_out[...] = step * own_search + step_next * direction
    r_out[...] = (right[...] - step * own_image) - step_next * total_image


class Loaded:
    def __init__(self, copy, ref):
        self.copy, self.ref, self.ready = copy, ref, False

    def wait(self):
        if not self.ready:
            self.copy.wait()
            self.ready = True

    def here(self):
        self.wait()
        return self.ref


class Copies:
    def __init__(self, semaphores):
        self.semaphores, self.all = semaphores, []

    def start(self, source, target):
        copy = pltpu.make_async_copy(source, target, self.semaphores.at[len(self.all)])
        copy.start()
        self.all.append(Loaded(copy, target))
        return self.all[-1]

    def finish(self):
        for loaded in self.all:
            loaded.wait()


def call(kernel, outs, far=(), late=(), near=(), final=False):
    first, second = len(far), len(far) + len(late)

    def run(*refs):
        end = len(refs) - 1 - len(late)
        copies = Copies(refs[-1])
        loaded = [copies.start(source, target) for source, target in zip(refs[first:second], refs[end:-1])]
        kernel(copies, *refs[:first], *loaded, *refs[second:end])
        copies.finish()

    shape_of = jax.ShapeDtypeStruct if final else pltpu.VMEM
    spaces = [pltpu.HBM] * second + [pltpu.VMEM] * len(near)
    return pl.pallas_call(
        run,
        out_shape=[shape_of(getattr(out, "shape", out), getattr(out, "dtype", F32)) for out in outs],
        in_specs=[pl.BlockSpec(memory_space=space) for space in spaces],
        out_specs=[pl.BlockSpec(memory_space=pltpu.VMEM)] * len(outs),
        scratch_shapes=[*(pltpu.VMEM(array.shape, array.dtype) for array in late), pltpu.SemaphoreType.DMA((second + 2,))],
        compiler_params=pltpu.CompilerParams(vmem_limit_bytes=16 * 1024 * 1024),
    )(*(pltpu.with_memory_space_constraint(array, pltpu.HBM) for array in (*far, *late)), *near)


def pair_swap(first, second, axis):
    size = lax.axis_size(axis)
    received = []
    for value, begin in ((first, 0), (second, 1)):
        perm = []
        for i in range(begin, size - 1, 2):
            perm += [(i, i + 1), (i + 1, i)]
        received.append(lax.ppermute(value, axis, perm) if perm else jnp.zeros_like(value))
    return received


def everywhere(rows):
    return lax.all_to_all(rows, AXES, split_axis=0, concat_axis=0, tiled=True)


def body(right, diagonal, coarse_slot, factor):
    sizes = (lax.axis_size("wide"), lax.axis_size("narrow"))
    groups = sizes[1]
    count = sizes[0] * groups
    fine = [jnp.asarray(c) for c in tables()]
    slots = coarse_slot.reshape(EY, EZ)
    swapped = groups == 2
    if not swapped:
        factor = factor.reshape(groups, ELEMS // groups, KCOL)
        factor = lax.all_to_all(factor, "narrow", split_axis=0, concat_axis=0, tiled=True).reshape(ELEMS, KCOL)
    part = functools.partial

    block, layer, extended = (BX, BY, BZ), (YR, BZ), (BX, YR, BZ)
    y_shape, x_shape, half = (3, BX, BZ), (2, YR, BZ), (ELEMS // 2, KCOL)
    gather = jax.ShapeDtypeStruct((BZ, EY * ELEMS), BF16)
    c, ya, yb, right, diagonal, slots, table = call(
        start_kernel,
        [(1, ELEMS), y_shape, y_shape, block, block, (1, ELEMS), gather],
        far=[right, diagonal],
        late=[slots],
    )
    ya, yb = pair_swap(ya, yb, "narrow")
    sent, kept, c, sigma, *near = call(
        part(stage_kernel, swapped),
        [half, half, (1, ELEMS), (1, ELEMS), *fine[:STAGED]],
        far=[factor, *fine[:STAGED]],
        near=[c, diagonal, table],
    )
    sums, xa, xb = call(
        part(project_kernel, swapped), [(count, 1, WIDTH), x_shape, x_shape], near=[c, ya, yb, right, diagonal, kept, sent]
    )
    sums = everywhere(sums)
    xa, xb = pair_swap(xa, xb, "wide")
    (solved,) = call(first_fine_kernel, [block], late=fine[STAGED:], near=[*near, right, ya, yb, xa, xb, sigma])
    ta, tb = call(part(first_coarse_kernel, swapped), [y_shape, y_shape], near=[sums, solved, slots, kept, sent])
    ra, rb = pair_swap(ta, tb, "narrow")
    received = lax.ppermute(sent, "narrow", [(0, 1), (1, 0)]) if swapped else sent
    search, sa, sb = call(
        part(extend_kernel, swapped),
        [extended, (2,) + layer, (2,) + layer],
        near=[solved, slots, ya, ta, ra, rb],
    )
    sa, sb = pair_swap(sa, sb, "wide")
    inner, product, table = call(
        interior_kernel, [extended, (1, 128), gather], near=[right, diagonal, search, ya, yb]
    )
    sums, image, halo = call(
        part(operator_kernel, swapped, sizes),
        [(count, 1, WIDTH), (BX + 2, YR, BZ), (3 * BY, BZ)],
        near=[kept, received, search, inner, product, table, sa, sb, xa, xb, slots],
    )
    sums = everywhere(sums)
    solved, ya, yb, fa, fb = call(
        second_fine_kernel, [block, (BX, BZ), (BX, BZ), (BY, BZ), (BY, BZ)], late=fine, near=[image, sigma]
    )
    ya, yb = pair_swap(ya, yb, "narrow")
    fa, fb = pair_swap(fa, fb, "wide")
    next_search, next_image, last, products = call(
        part(second_coarse_kernel, swapped),
        [block, block, (count, 1, 2 * ELEMS), (1, 128)],
        near=[right, diagonal, kept, received, sums, solved, ya, yb, fa, fb, search, halo, image, slots],
    )
    last = everywhere(last)
    return tuple(
        call(
            part(last_kernel, sizes),
            [block, block],
            near=[right, products, last, search, image, next_search, next_image],
            final=True,
        )
    )


def solution(mesh):
    in_specs = (
        P("wide", "narrow", None),
        P("wide", "narrow", None),
        P("wide", "narrow", None),
        P(("wide", "narrow"), None),
    )
    out_specs = (P("wide", "narrow", None), P("wide", "narrow", None))
    return jax.shard_map(body, mesh=mesh, in_specs=in_specs, out_specs=out_specs, check_vma=False)
```

```python
import functools

import jax
import jax.numpy as jnp
import numpy as np
from jax import lax
from jax.experimental import pallas as pl
from jax.experimental.pallas import tpu as pltpu
from jax.sharding import PartitionSpec as P

F32 = jnp.float32
BF16 = jnp.bfloat16
BX, BY, BZ = 8, 16, 512
EY, EZ = 2, 64
ELEMS = EY * EZ
YR = 24
YW = YR * (BX + 2)
AB = 208
HZ = 256
HW = 384
STAGED = 6
TABLES = 10
KCOL = 2048
WIDTH = KCOL + 128
AXES = ("wide", "narrow")


def split_const(values):
    high = values.astype(jnp.bfloat16)
    low = (values - high.astype(np.float64)).astype(jnp.bfloat16)
    return high, low


@functools.lru_cache(maxsize=None)
def tables():
    index = np.arange(10, dtype=np.float64)
    basis = np.sqrt(2.0 / 11.0) * np.sin(np.pi * (index[:, None] + 1.0) * (index[None, :] + 1.0) / 11.0)
    values = 2.0 - 2.0 * np.cos(np.pi * (index + 1.0) / 11.0)
    to_z = np.zeros((HZ, HW))
    from_z = np.zeros((HW, HZ))
    beyond = np.zeros((8, HW), np.float32)
    last = HZ // 8 - 1
    for e in range(last + 1):
        at = slice(e, 10 * (last + 1), last + 1)
        for k in range(10):
            z = 8 * e + k - 1
            if 0 <= z < HZ:
                to_z[z, at] = basis[k]
            if 1 <= k <= 8:
                from_z[at, z] = basis[k]
    beyond[0, last : 10 * (last + 1) : last + 1] = basis[9]
    beyond[1, 0 : 10 * (last + 1) : last + 1] = basis[0]
    beyond[2] = 1.0
    beyond[2, : 10 * (last + 1)] = np.repeat(values, last + 1)
    to_xy = np.zeros((10, EY, 10, 10, YR))
    from_xy = np.zeros((BX, BY, 10, EY, 10))
    for e in range(EY):
        for j in range(10):
            y = 8 * e + j - 1
            to_xy[:, e, :, :, y % YR] += basis.T[:, None, :] * basis[j][None, :, None]
            if 1 <= j <= 8:
                from_xy[:, y, :, e, :] = basis[1:9, :, None] * basis[j][None, None, :]
    to_xy = np.pad(to_xy.reshape(200, YW), ((0, AB - 200), (0, 0)))
    from_xy = np.pad(from_xy.reshape(BX * BY, 200), ((0, 0), (0, AB - 200)))
    column = np.zeros((AB, 128), np.float32)
    grid = np.zeros((10, EY, 10, 2))
    grid[..., 0] = values[:, None, None] + values[None, None, :]
    grid[..., 1] = np.arange(EY)[None, :, None]
    column[:200, :2] = grid.reshape(200, 2)
    column[200:, 0] = 1.0
    return split_const(to_xy) + split_const(to_z) + split_const(from_xy) + split_const(from_z) + (column, beyond)


def dot(a, b):
    return jnp.dot(a, b, preferred_element_type=F32)


def split2(x):
    high = x.astype(BF16)
    return high, (x - high.astype(F32)).astype(BF16)


def split3(x):
    high = x.astype(BF16)
    rest = x - high.astype(F32)
    middle = rest.astype(BF16)
    return high, middle, (rest - middle.astype(F32)).astype(BF16)


def dot3(a, b):
    return dot(a[0], b[0]) + dot(a[0], b[1]) + dot(a[1], b[0])


def iota(shape, axis):
    return lax.broadcasted_iota(jnp.int32, shape, axis)


def total(x):
    while x.ndim > 2:
        x = jnp.sum(x, axis=0)
    return jnp.sum(jnp.sum(x, axis=0, keepdims=True), axis=1, keepdims=True)


def gather_table():
    shape = (BZ, EY * ELEMS)
    node, at = iota(shape, 0), iota(shape, 1)
    return jnp.where(at == node // 8 + (at // ELEMS) * (ELEMS + EZ), 1.0, 0.0).astype(BF16)


def spread_table():
    shape = (ELEMS, EY * BZ)
    element, at = iota(shape, 0), iota(shape, 1)
    return jnp.where(at // 8 == element, 1.0, 0.0).astype(BF16)


def element_row(field, table):
    parts = jnp.concatenate(split3(jnp.sum(field, axis=0)), axis=0)
    sums = dot(parts, table)
    sums = sums[0:16] + sums[16:32] + sums[32:48]
    return jnp.sum(sums[0:8, 0:ELEMS], axis=0, keepdims=True) + jnp.sum(sums[8:16, ELEMS:], axis=0, keepdims=True)


def expand_rows(rows):
    count = rows.shape[0]
    tall = jnp.broadcast_to(rows, (16, ELEMS)) if count == 1 else jnp.concatenate([rows, jnp.zeros((16 - count, ELEMS), F32)], axis=0)
    wide = dot(jnp.concatenate(split3(tall), axis=0), spread_table())
    return (wide[0:16] + wide[16:32] + wide[32:48])[0:count]


def expand_block(row):
    wide = expand_rows(row)
    low = jnp.broadcast_to(wide[:, 0:BZ], (8, BZ))
    high = jnp.broadcast_to(wide[:, BZ:], (8, BZ))
    return jnp.concatenate([low, high], axis=0)


def slot_mask(slots, offset):
    slot_of_row = lax.rem(iota((ELEMS, ELEMS), 0) + offset, ELEMS)
    return slot_of_row.astype(F32) == slots


def to_rows(element_values, slots, offset):
    return jnp.sum(jnp.where(slot_mask(slots, offset), element_values, 0.0), axis=1, keepdims=True)


def to_elements(row_values, slots, offset):
    return jnp.sum(jnp.where(slot_mask(slots, offset), row_values, 0.0), axis=0, keepdims=True)


def project(column, parts):
    out = 0.0
    at = 0
    for part in parts:
        size = part.shape[0]
        out = out + jnp.sum(column[at : at + size] * part[...], axis=0, keepdims=True)
        at += size
    return out


def correct(row, parts):
    out = []
    for part in parts:
        products = part[...] * row
        folded = products[:, 0:128]
        for at in range(128, KCOL, 128):
            folded = folded + products[:, at : at + 128]
        out.append(jnp.sum(folded, axis=1, keepdims=True))
    return jnp.concatenate(out, axis=0)


def store_sum(out_ref, first, second):
    count, _, width = out_ref.shape
    cut = width - 128
    out_ref[:, :, 0:cut] = jnp.broadcast_to(first[None], (count, 1, cut))
    out_ref[:, :, cut:width] = jnp.broadcast_to(second[None], (count, 1, 128))


def lanes(values):
    at = iota((1, 128), 1)
    row = jnp.zeros((1, 128), F32)
    for i, value in enumerate(values):
        row = jnp.where(at == i, value, row)
    return row


def lane(row, i):
    return jnp.sum(jnp.where(iota(row.shape, 1) == i, row, 0.0), axis=1, keepdims=True)


def odd(index):
    return lax.rem(index, 2) == 1


def pair_out(index, low, high):
    return jnp.where(odd(index), low, high), jnp.where(odd(index), high, low)


def pair_in(index, first, second):
    return jnp.where(odd(index), first, second), jnp.where(odd(index), second, first)


def extend_y(block, low, high, depth):
    at = iota((8, BZ), 0)
    tails = []
    for x in range(block.shape[0]):
        tail = jnp.zeros((8, BZ), F32)
        for i in range(depth):
            tail = jnp.where(at == i, high[i][x : x + 1], tail)
            tail = jnp.where(at == 8 - depth + i, low[i][x : x + 1], tail)
        tails.append(tail)
    return jnp.concatenate([block, jnp.stack(tails)], axis=1)


def roll_sum(x):
    count, rows, _ = x.shape
    beside = pltpu.roll(x, 1, 1) + pltpu.roll(x, rows - 1, 1)
    flat = x.reshape(count * rows, BZ)
    at = iota(flat.shape, 1)
    beside_z = jnp.where(at == 0, 0.0, pltpu.roll(flat, 1, 1)) + jnp.where(at == BZ - 1, 0.0, pltpu.roll(flat, BZ - 1, 1))
    return beside + beside_z.reshape(x.shape)


def fine_solve(rows, sigma, tables):
    wh, wl, th, tl, vh, vl, uh, ul, column, beyond = tables
    high, low = value(wh), value(wl)
    for table in tables:
        if isinstance(table, Loaded):
            table.begin()
    spectra = dot3((high, low), split2(rows))
    th, tl, vh, vl, uh, ul, column, beyond = [value(table) for table in (th, tl, vh, vl, uh, ul, column, beyond)]
    nodal = []
    for half in range(2):
        part = spectra[:, half * HZ : (half + 1) * HZ]
        edge = spectra[:, HZ : HZ + 1] if half == 0 else spectra[:, HZ - 1 : HZ]
        part = dot3(split2(part), (th, tl)) + edge * beyond[half : half + 1]
        sig = jnp.where(column[:, 1:2] == 0.0, repeat_lanes(sigma, half), repeat_lanes(sigma, 2 + half))
        part = part / (column[:, 0:1] + beyond[2:3] + sig)
        part = dot3((vh, vl), split2(part))
        nodal.append(dot3(split2(part), (uh, ul)).reshape(BX, BY, HZ))
    return jnp.concatenate(nodal, axis=2)


def value(table):
    return (table.here() if isinstance(table, Loaded) else table)[...]


def repeat_lanes(row, group):
    only = jnp.where(iota((1, ELEMS), 1) // 32 == group, row, 0.0)
    only = only + pltpu.roll(only, 64, 1)
    only = only + pltpu.roll(only, 32, 1)
    return jnp.concatenate([only] * 3, axis=1)


def eye_mask():
    return iota((ELEMS, ELEMS), 0) == iota((ELEMS, ELEMS), 1)


def row_to_column(row):
    return jnp.sum(jnp.where(eye_mask(), row, 0.0), axis=1, keepdims=True)


def column_to_row(column):
    return jnp.sum(jnp.where(eye_mask(), column, 0.0), axis=0, keepdims=True)


def pad_tile(rows):
    at = iota((8, ELEMS), 0)
    tile = jnp.zeros((8, ELEMS), F32)
    for i, row in enumerate(rows):
        tile = jnp.where(at == i, row, tile)
    return jnp.concatenate([tile, jnp.zeros((8, BZ - ELEMS), F32)], axis=1)


def start_kernel(
    late, right_far, diagonal_far, slots_far, c, ya, yb, right, diagonal, slots_out, table_out
):
    d = lax.axis_index("narrow")
    right_load = late.start(right_far, right)
    diagonal_load = late.start(diagonal_far, diagonal)
    slots_in = slots_far.here()
    slots = jnp.concatenate([slots_in[0:1], slots_in[1:2]], axis=1).astype(F32)
    slots_out[...] = slots
    table = gather_table()
    table_out[...] = table
    right_load.wait()
    row = column_to_row(to_rows(element_row(right[...], table) * (1.0 / 16.0), slots, 0))
    c[...] = row
    diagonal_load.wait()
    for i, ref in enumerate((right, diagonal)):
        ya[i], yb[i] = pair_out(d, ref[:, 0, :], ref[:, BY - 1, :])
    ya[2] = pad_tile([row, slots])
    yb[2] = jnp.zeros((8, BZ), F32)


def stage_kernel(swapped, late, factor, *refs):
    d = lax.axis_index("narrow")
    half = ELEMS // 2
    at = pl.multiple_of(d * half, half) if swapped else 0
    there = pl.multiple_of((1 - d) * half, half) if swapped else half
    after, diagonal, table, sent, kept, done, sigma = refs[STAGED : STAGED + 7]
    late.start(factor.at[pl.ds(at, half)], kept)
    late.start(factor.at[pl.ds(there, half)], sent)
    for source, target in zip(refs[:STAGED], refs[STAGED + 7 :]):
        late.start(source, target)
    done[...] = after[...]
    sigma[...] = element_row(diagonal[...], table[...]) * (1.0 / 512.0)


def project_kernel(swapped, late, c, ra, rb, right, diagonal, kept, sent, sums, xa, xb):
    w, d = lax.axis_index("wide"), lax.axis_index("narrow")
    row = c[...]
    if swapped:
        half = ELEMS // 2
        other = ra[2, 0:1, 0:ELEMS]
        row = jnp.where(d == 0, row, pltpu.roll(row, half, 1))
        other = jnp.where(d == 0, pltpu.roll(other, half, 1), other)
        row = jnp.where(iota((1, ELEMS), 1) < half, row, other)
    store_sum(sums, project(row_to_column(row), (kept, sent)), jnp.zeros((1, 128), F32))
    for i, ref in enumerate((right, diagonal)):
        low, high = pair_in(d, ra[i], rb[i])
        layers = [extend_y(ref[x : x + 1], [low[x : x + 1]], [high[x : x + 1]], 1)[0] for x in (0, BX - 1)]
        xa[i], xb[i] = pair_out(w, *layers)


def widened(block, ya, yb, xa, xb, i):
    w, d = lax.axis_index("wide"), lax.axis_index("narrow")
    low, high = pair_in(d, ya[i], yb[i])
    x_low, x_high = pair_in(w, xa[i], xb[i])
    return jnp.concatenate([x_low[None], extend_y(block, [low], [high], 1), x_high[None]], axis=0)


def first_fine_kernel(late, *rest):
    right, ya, yb, xa, xb, sigma, solved = rest[TABLES:]
    rows = widened(right[...], ya, yb, xa, xb, 0)
    tables = rest[TABLES - STAGED : TABLES] + rest[: TABLES - STAGED]
    solved[...] = fine_solve(rows.reshape(YW, BZ), sigma[...], tables)


def first_coarse_kernel(swapped, late, sums, solved, slots, kept, sent, ya, yb):
    d = lax.axis_index("narrow")
    row = jnp.sum(sums[...], axis=0)[:, 0:KCOL]
    column = correct(row, (kept, sent))
    for i in range(2):
        ya[i], yb[i] = pair_out(d, solved[:, i, :], solved[:, BY - 2 + i, :])
    if swapped:
        values = column_to_row(column)
        values = jnp.where(d == 0, values, pltpu.roll(values, ELEMS // 2, 1))
    else:
        values = to_elements(column, slots[...], 0)
    ya[2] = pad_tile([values])
    yb[2] = ya[2]


def extend_kernel(swapped, late, solved, slots, ra_first, own_ref, ra, rb, search, xa, xb):
    w, d = lax.axis_index("wide"), lax.axis_index("narrow")
    groups = lax.axis_size("narrow")
    own = own_ref[2, 0:1, 0:ELEMS]
    theirs = ra[2, 0:1, 0:ELEMS]
    if swapped:
        half = ELEMS // 2
        at = iota((1, ELEMS), 1) // half
        other = jnp.where(at == d, pltpu.roll(own, half, 1), theirs)
        own = jnp.where(at == d, own, pltpu.roll(theirs, half, 1))
        own = to_elements(row_to_column(own), slots[...], 0)
        other = to_elements(row_to_column(other), ra_first[2, 1:2, 0:ELEMS], 0)
        values_low, values_high = other, other
    else:
        values_low, values_high = pair_in(d, theirs, rb[2, 0:1, 0:ELEMS])
    values_low = jnp.where(d > 0, values_low, 0.0)
    values_high = jnp.where(d < groups - 1, values_high, 0.0)
    wide = expand_rows(jnp.concatenate([own, values_low, values_high], axis=0)) * (1.0 / 16.0)
    coarse = jnp.concatenate(
        [jnp.broadcast_to(wide[0:1, 0:BZ], (8, BZ)), jnp.broadcast_to(wide[0:1, BZ:], (8, BZ))], axis=0
    )
    low, high = [], []
    for i in range(2):
        one, two = pair_in(d, ra[i], rb[i])
        low.append(one + wide[1:2, BZ:])
        high.append(two + wide[2:3, 0:BZ])
    block = extend_y(solved[...] + coarse[None], low, high, 2)
    search[...] = block
    xa[...], xb[...] = pair_out(w, block[0:2], block[BX - 2 : BX])


def interior_kernel(late, diagonal_late, right, search, ya, yb, image, product, table, diagonal):
    d = lax.axis_index("narrow")
    low, high = pair_in(d, ya[1], yb[1])
    centre = search[...]
    diagonal[...] = diagonal_late.here()[...]
    part = (6.0 + extend_y(diagonal[...], [low], [high], 1)) * centre - roll_sum(centre)
    zero = jnp.zeros((1, YR, BZ), F32)
    part = part - jnp.concatenate([zero, centre[0 : BX - 1]], axis=0) - jnp.concatenate([centre[1:BX], zero], axis=0)
    image[...] = part
    product[...] = lanes([total(right[...] * centre[:, 0:BY])])
    table[...] = gather_table()


def operator_kernel(
    swapped, sizes, late, kept, received, search, inner, product, table, sa, sb, xa, xb, slots, sums, image_out, halo
):
    w, d = lax.axis_index("wide"), lax.axis_index("narrow")
    owned, offset = (kept, received), d * (ELEMS // 2) if swapped else 0
    s_low, s_high = pair_in(w, sa[...], sb[...])
    d_low, d_high = pair_in(w, xa[1], xb[1])
    low = (6.0 + d_low) * s_low[1] - s_low[0] - search[0] - roll_sum(s_low[1:2])[0]
    high = (6.0 + d_high) * s_high[0] - s_high[1] - search[BX - 1] - roll_sum(s_high[0:1])[0]
    y = iota((YR, BZ), 0)
    inside = (y < BY) | ((y == BY) & (d < sizes[1] - 1)) | ((y == YR - 1) & (d > 0))
    image_out[0] = jnp.where(inside & (w > 0), low, 0.0)
    image_out[1] = jnp.where(inside, inner[0] - s_low[1], 0.0)
    image_out[2:BX] = jnp.where(inside[None], inner[1 : BX - 1], 0.0)
    image_out[BX] = jnp.where(inside, inner[BX - 1] - s_high[0], 0.0)
    image_out[BX + 1] = jnp.where(inside & (w < sizes[0] - 1), high, 0.0)
    halo[0:BY] = s_low[1, 0:BY]
    halo[BY : 2 * BY] = s_high[0, 0:BY]
    halo[2 * BY : 2 * BY + 8] = search[:, YR - 1, :]
    halo[2 * BY + 8 : 3 * BY] = search[:, BY, :]
    own = image_out[1 : BX + 1, 0:BY, :]
    column = to_rows(element_row(own, table[...]) * (1.0 / 16.0), slots[...], offset)
    extra = lanes([lane(product[...], 0), total(search[:, 0:BY, :] * own)])
    store_sum(sums, project(column, owned), extra)


def second_fine_kernel(late, *rest):
    w, d = lax.axis_index("wide"), lax.axis_index("narrow")
    image, sigma, solved, ya, yb, xa, xb = rest[TABLES:]
    out = fine_solve(image[...].reshape(YW, BZ), sigma[...], rest[:TABLES])
    solved[...] = out
    ya[...], yb[...] = pair_out(d, solved[:, 0, :], solved[:, BY - 1, :])
    xa[...], xb[...] = pair_out(w, out[0], out[BX - 1])


def second_coarse_kernel(
    swapped, late, right, diagonal, kept, received, sums, solved, fya, fyb, fxa, fxb, search, halo, image, slots,
    search_out, image_out, last, products,
):
    w, d = lax.axis_index("wide"), lax.axis_index("narrow")
    owned, offset = (kept, received), d * (ELEMS // 2) if swapped else 0
    row = jnp.sum(sums[...], axis=0)
    products[...] = row[:, KCOL:WIDTH]
    step = lane(row[:, KCOL:WIDTH], 0) / lane(row[:, KCOL:WIDTH], 1)
    values = to_elements(correct(row[:, 0:KCOL], owned), slots[...], offset)
    coarse = expand_block(values * (1.0 / 16.0))
    own_search = search[:, 0:BY, :]
    own_image = image[1 : BX + 1, 0:BY, :]
    vector = own_search - step * (solved[...] + coarse[None])
    f_low, f_high = pair_in(w, fxa[...], fxb[...])
    x_low = halo[0:BY] - step * f_low
    x_high = halo[BY : 2 * BY] - step * f_high
    g_low, g_high = pair_in(d, fya[...], fyb[...])
    y_low = halo[2 * BY : 2 * BY + 8] - step * g_low
    y_high = halo[2 * BY + 8 : 3 * BY] - step * g_high
    beside = roll_sum(extend_y(vector, [y_low], [y_high], 1))[:, 0:BY]
    beside = beside + jnp.concatenate([x_low[None], vector[0 : BX - 1]], axis=0)
    beside = beside + jnp.concatenate([vector[1:BX], x_high[None]], axis=0)
    next_image = (6.0 + diagonal[...]) * vector - beside
    search_out[...] = vector
    image_out[...] = next_image
    residual = right[...] - step * own_image
    edges = total(coarse * (x_low + x_high)) + total(y_low * coarse[0:1]) + total(y_high * coarse[BY - 1 : BY])
    store_sum(
        last,
        values,
        lanes([total(residual * vector), total(vector * next_image) + step * edges, total(vector * own_image)]),
    )


def last_kernel(sizes, late, right, products, last, search, image, next_search, next_image, x_out, r_out):
    w, d = lax.axis_index("wide"), lax.axis_index("narrow")
    groups = sizes[1]
    count = sizes[0] * groups
    product, bottom = lane(products[...], 0), lane(products[...], 1)
    step = product / bottom
    z = last[:, 0, 0:ELEMS]
    rows = iota((count, ELEMS), 0)
    at = iota((count, ELEMS), 1)
    faces = jnp.where(rows < count - groups, z * pltpu.roll(z, count - groups, 0), 0.0)
    across = pltpu.roll(pltpu.roll(z, count - 1, 0), EZ, 1)
    faces = faces + jnp.where((lax.rem(rows, groups) < groups - 1) & (at >= EZ), z * across, 0.0)
    sums = jnp.sum(last[:, :, ELEMS:], axis=0)
    next_product = lane(sums, 0)
    quadratic = lane(sums, 1) - step * step * 0.5 * total(faces)
    cross = lane(sums, 2)
    me = w * groups + d
    picked = []
    for index, there in ((me - groups, w > 0), (me + groups, w < sizes[0] - 1), (me - 1, d > 0), (me + 1, d < groups - 1)):
        picked.append(jnp.sum(jnp.where((rows == index) & there, z, 0.0), axis=0, keepdims=True))
    wide = expand_rows(jnp.concatenate(picked, axis=0)) * (1.0 / 16.0)
    layers = []
    for i in range(2):
        low = jnp.broadcast_to(wide[i : i + 1, 0:BZ], (8, BZ))
        high = jnp.broadcast_to(wide[i : i + 1, BZ:], (8, BZ))
        layers.append(jnp.concatenate([low, high], axis=0)[None])
    shape = (BX, BY, BZ)
    x, y = iota(shape, 0), iota(shape, 1)
    missing = jnp.where(x == 0, layers[0], 0.0) + jnp.where(x == BX - 1, layers[1], 0.0)
    missing = missing + jnp.where(y == 0, wide[2:3, BZ:][None], 0.0) + jnp.where(y == BY - 1, wide[3:4, 0:BZ][None], 0.0)
    ratio = next_product / product
    curvature = quadratic + 2.0 * ratio * cross + ratio * ratio * bottom
    step_next = next_product / curvature
    own_search = search[:, 0:BY, :]
    own_image = image[1 : BX + 1, 0:BY, :]
    direction = next_search[...] + ratio * own_search
    total_image = next_image[...] + step * missing + ratio * own_image
    x_out[...] = step * own_search + step_next * direction
    r_out[...] = (right[...] - step * own_image) - step_next * total_image


class Loaded:
    def __init__(self, copy, ref):
        self.copy, self.ref, self.begun, self.ready = copy, ref, False, False

    def begin(self):
        if not self.begun:
            self.copy.start()
            self.begun = True

    def wait(self):
        self.begin()
        if not self.ready:
            self.copy.wait()
            self.ready = True

    def here(self):
        self.wait()
        return self.ref


class Copies:
    def __init__(self, semaphores):
        self.semaphores, self.all = semaphores, []

    def start(self, source, target, begin=True):
        self.all.append(Loaded(pltpu.make_async_copy(source, target, self.semaphores.at[len(self.all)]), target))
        if begin:
            self.all[-1].begin()
        return self.all[-1]

    def finish(self):
        for loaded in self.all:
            loaded.wait()


def call(kernel, outs, far=(), late=(), near=(), final=False, first_wave=99):
    first, second = len(far), len(far) + len(late)

    def run(*refs):
        end = len(refs) - 1 - len(late)
        copies = Copies(refs[-1])
        loaded = [
            copies.start(source, target, i < first_wave)
            for i, (source, target) in enumerate(zip(refs[first:second], refs[end:-1]))
        ]
        kernel(copies, *refs[:first], *loaded, *refs[second:end])
        copies.finish()

    shape_of = jax.ShapeDtypeStruct if final else pltpu.VMEM
    spaces = [pltpu.HBM] * second + [pltpu.VMEM] * len(near)
    return pl.pallas_call(
        run,
        out_shape=[shape_of(getattr(out, "shape", out), getattr(out, "dtype", F32)) for out in outs],
        in_specs=[pl.BlockSpec(memory_space=space) for space in spaces],
        out_specs=[pl.BlockSpec(memory_space=pltpu.VMEM)] * len(outs),
        scratch_shapes=[*(pltpu.VMEM(array.shape, array.dtype) for array in late), pltpu.SemaphoreType.DMA((second + 2,))],
        compiler_params=pltpu.CompilerParams(vmem_limit_bytes=16 * 1024 * 1024),
    )(*(pltpu.with_memory_space_constraint(array, pltpu.HBM) for array in (*far, *late)), *near)


def pair_swap(first, second, axis):
    size = lax.axis_size(axis)
    received = []
    for value, begin in ((first, 0), (second, 1)):
        perm = []
        for i in range(begin, size - 1, 2):
            perm += [(i, i + 1), (i + 1, i)]
        received.append(lax.ppermute(value, axis, perm) if perm else jnp.zeros_like(value))
    return received


def everywhere(rows):
    return lax.all_to_all(rows, AXES, split_axis=0, concat_axis=0, tiled=True)


def body(right, diagonal, coarse_slot, factor):
    sizes = (lax.axis_size("wide"), lax.axis_size("narrow"))
    groups = sizes[1]
    count = sizes[0] * groups
    fine = [jnp.asarray(c) for c in tables()]
    slots = coarse_slot.reshape(EY, EZ)
    swapped = groups == 2
    if not swapped:
        factor = factor.reshape(groups, ELEMS // groups, KCOL)
        factor = lax.all_to_all(factor, "narrow", split_axis=0, concat_axis=0, tiled=True).reshape(ELEMS, KCOL)
    part = functools.partial

    block, layer, extended = (BX, BY, BZ), (YR, BZ), (BX, YR, BZ)
    y_shape, x_shape, half = (3, BX, BZ), (2, YR, BZ), (ELEMS // 2, KCOL)
    gather = jax.ShapeDtypeStruct((BZ, EY * ELEMS), BF16)
    diagonal_far = diagonal
    c, ya, yb, right, diagonal, slots, table = call(
        start_kernel,
        [(1, ELEMS), y_shape, y_shape, block, block, (1, ELEMS), gather],
        far=[right, diagonal],
        late=[slots],
    )
    ya, yb = pair_swap(ya, yb, "narrow")
    sent, kept, c, sigma, *near = call(
        part(stage_kernel, swapped),
        [half, half, (1, ELEMS), (1, ELEMS), *fine[:STAGED]],
        far=[factor, *fine[:STAGED]],
        near=[c, diagonal, table],
    )
    sums, xa, xb = call(
        part(project_kernel, swapped), [(count, 1, WIDTH), x_shape, x_shape], near=[c, ya, yb, right, diagonal, kept, sent]
    )
    sums = everywhere(sums)
    xa, xb = pair_swap(xa, xb, "wide")
    (solved,) = call(first_fine_kernel, [block], late=fine[STAGED:], near=[*near, right, ya, yb, xa, xb, sigma])
    ta, tb = call(part(first_coarse_kernel, swapped), [y_shape, y_shape], near=[sums, solved, slots, kept, sent])
    ra, rb = pair_swap(ta, tb, "narrow")
    received = lax.ppermute(sent, "narrow", [(0, 1), (1, 0)]) if swapped else sent
    search, sa, sb = call(
        part(extend_kernel, swapped),
        [extended, (2,) + layer, (2,) + layer],
        near=[solved, slots, ya, ta, ra, rb],
    )
    sa, sb = pair_swap(sa, sb, "wide")
    inner, product, table, diagonal = call(
        interior_kernel, [extended, (1, 128), gather, block], late=[diagonal_far], near=[right, search, ya, yb]
    )
    sums, image, halo = call(
        part(operator_kernel, swapped, sizes),
        [(count, 1, WIDTH), (BX + 2, YR, BZ), (3 * BY, BZ)],
        near=[kept, received, search, inner, product, table, sa, sb, xa, xb, slots],
    )
    sums = everywhere(sums)
    solved, ya, yb, fa, fb = call(
        second_fine_kernel, [block, (BX, BZ), (BX, BZ), (BY, BZ), (BY, BZ)], late=fine, near=[image, sigma], first_wave=4
    )
    ya, yb = pair_swap(ya, yb, "narrow")
    fa, fb = pair_swap(fa, fb, "wide")
    next_search, next_image, last, products = call(
        part(second_coarse_kernel, swapped),
        [block, block, (count, 1, 2 * ELEMS), (1, 128)],
        near=[right, diagonal, kept, received, sums, solved, ya, yb, fa, fb, search, halo, image, slots],
    )
    last = everywhere(last)
    return tuple(
        call(
            part(last_kernel, sizes),
            [block, block],
            near=[right, products, last, search, image, next_search, next_image],
            final=True,
        )
    )


def solution(mesh):
    in_specs = (
        P("wide", "narrow", None),
        P("wide", "narrow", None),
        P("wide", "narrow", None),
        P(("wide", "narrow"), None),
    )
    out_specs = (P("wide", "narrow", None), P("wide", "narrow", None))
    return jax.shard_map(body, mesh=mesh, in_specs=in_specs, out_specs=out_specs, check_vma=False)
```

```python
import functools

import jax
import jax.numpy as jnp
import numpy as np
from jax import lax
from jax.experimental import pallas as pl
from jax.experimental.pallas import tpu as pltpu
from jax.sharding import PartitionSpec as P

F32 = jnp.float32
BF16 = jnp.bfloat16
BX, BY, BZ = 8, 16, 512
EY, EZ = 2, 64
ELEMS = EY * EZ
YR = 24
YW = YR * (BX + 2)
AB = 208
HZ = 256
HW = 384
STAGED = 6
TABLES = 10
KCOL = 2048
WIDTH = KCOL + 128
AXES = ("wide", "narrow")


def split_const(values):
    high = values.astype(jnp.bfloat16)
    low = (values - high.astype(np.float64)).astype(jnp.bfloat16)
    return high, low


@functools.lru_cache(maxsize=None)
def tables():
    index = np.arange(10, dtype=np.float64)
    basis = np.sqrt(2.0 / 11.0) * np.sin(np.pi * (index[:, None] + 1.0) * (index[None, :] + 1.0) / 11.0)
    values = 2.0 - 2.0 * np.cos(np.pi * (index + 1.0) / 11.0)
    to_z = np.zeros((HZ, HW))
    from_z = np.zeros((HW, HZ))
    beyond = np.zeros((8, HW), np.float32)
    last = HZ // 8 - 1
    for e in range(last + 1):
        at = slice(e, 10 * (last + 1), last + 1)
        for k in range(10):
            z = 8 * e + k - 1
            if 0 <= z < HZ:
                to_z[z, at] = basis[k]
            if 1 <= k <= 8:
                from_z[at, z] = basis[k]
    beyond[0, last : 10 * (last + 1) : last + 1] = basis[9]
    beyond[1, 0 : 10 * (last + 1) : last + 1] = basis[0]
    beyond[2] = 1.0
    beyond[2, : 10 * (last + 1)] = np.repeat(values, last + 1)
    to_xy = np.zeros((10, EY, 10, 10, YR))
    from_xy = np.zeros((BX, BY, 10, EY, 10))
    for e in range(EY):
        for j in range(10):
            y = 8 * e + j - 1
            to_xy[:, e, :, :, y % YR] += basis.T[:, None, :] * basis[j][None, :, None]
            if 1 <= j <= 8:
                from_xy[:, y, :, e, :] = basis[1:9, :, None] * basis[j][None, None, :]
    to_xy = np.pad(to_xy.reshape(200, YW), ((0, AB - 200), (0, 256 - YW)))
    from_xy = np.pad(from_xy.reshape(BX * BY, 200), ((0, 0), (0, 256 - 200)))
    column = np.zeros((AB, 128), np.float32)
    grid = np.zeros((10, EY, 10, 2))
    grid[..., 0] = values[:, None, None] + values[None, None, :]
    grid[..., 1] = np.arange(EY)[None, :, None]
    column[:200, :2] = grid.reshape(200, 2)
    column[200:, 0] = 1.0
    return split_const(to_xy) + split_const(to_z) + split_const(from_xy) + split_const(from_z) + (column, beyond)


def dot(a, b):
    return jnp.dot(a, b, preferred_element_type=F32)


def split2(x):
    high = x.astype(BF16)
    return high, (x - high.astype(F32)).astype(BF16)


def split3(x):
    high = x.astype(BF16)
    rest = x - high.astype(F32)
    middle = rest.astype(BF16)
    return high, middle, (rest - middle.astype(F32)).astype(BF16)


def dot3(a, b):
    return dot(a[0], b[0]) + dot(a[0], b[1]) + dot(a[1], b[0])


def iota(shape, axis):
    return lax.broadcasted_iota(jnp.int32, shape, axis)


def total(x):
    while x.ndim > 2:
        x = jnp.sum(x, axis=0)
    return jnp.sum(jnp.sum(x, axis=0, keepdims=True), axis=1, keepdims=True)


def gather_table():
    shape = (BZ, EY * ELEMS)
    node, at = iota(shape, 0), iota(shape, 1)
    return jnp.where(at == node // 8 + (at // ELEMS) * (ELEMS + EZ), 1.0, 0.0).astype(BF16)


def spread_table():
    shape = (ELEMS, EY * BZ)
    element, at = iota(shape, 0), iota(shape, 1)
    return jnp.where(at // 8 == element, 1.0, 0.0).astype(BF16)


def element_row(field, table):
    parts = jnp.concatenate(split3(jnp.sum(field, axis=0)), axis=0)
    sums = dot(parts, table)
    sums = sums[0:16] + sums[16:32] + sums[32:48]
    return jnp.sum(sums[0:8, 0:ELEMS], axis=0, keepdims=True) + jnp.sum(sums[8:16, ELEMS:], axis=0, keepdims=True)


def expand_rows(rows):
    count = rows.shape[0]
    tall = jnp.broadcast_to(rows, (16, ELEMS)) if count == 1 else jnp.concatenate([rows, jnp.zeros((16 - count, ELEMS), F32)], axis=0)
    wide = dot(jnp.concatenate(split3(tall), axis=0), spread_table())
    return (wide[0:16] + wide[16:32] + wide[32:48])[0:count]


def expand_block(row):
    wide = expand_rows(row)
    low = jnp.broadcast_to(wide[:, 0:BZ], (8, BZ))
    high = jnp.broadcast_to(wide[:, BZ:], (8, BZ))
    return jnp.concatenate([low, high], axis=0)


def slot_mask(slots, offset):
    slot_of_row = lax.rem(iota((ELEMS, ELEMS), 0) + offset, ELEMS)
    return slot_of_row.astype(F32) == slots


def to_rows(element_values, slots, offset):
    return jnp.sum(jnp.where(slot_mask(slots, offset), element_values, 0.0), axis=1, keepdims=True)


def to_elements(row_values, slots, offset):
    return jnp.sum(jnp.where(slot_mask(slots, offset), row_values, 0.0), axis=0, keepdims=True)


def project(column, parts):
    out = 0.0
    at = 0
    for part in parts:
        size = part.shape[0]
        out = out + jnp.sum(column[at : at + size] * part[...], axis=0, keepdims=True)
        at += size
    return out


def correct(row, parts):
    out = []
    for part in parts:
        products = part[...] * row
        folded = products[:, 0:128]
        for at in range(128, KCOL, 128):
            folded = folded + products[:, at : at + 128]
        out.append(jnp.sum(folded, axis=1, keepdims=True))
    return jnp.concatenate(out, axis=0)


def store_sum(out_ref, first, second):
    count, _, width = out_ref.shape
    cut = width - 128
    out_ref[:, :, 0:cut] = jnp.broadcast_to(first[None], (count, 1, cut))
    out_ref[:, :, cut:width] = jnp.broadcast_to(second[None], (count, 1, 128))


def lanes(values):
    at = iota((1, 128), 1)
    row = jnp.zeros((1, 128), F32)
    for i, value in enumerate(values):
        row = jnp.where(at == i, value, row)
    return row


def lane(row, i):
    return jnp.sum(jnp.where(iota(row.shape, 1) == i, row, 0.0), axis=1, keepdims=True)


def odd(index):
    return lax.rem(index, 2) == 1


def pair_out(index, low, high):
    return jnp.where(odd(index), low, high), jnp.where(odd(index), high, low)


def pair_in(index, first, second):
    return jnp.where(odd(index), first, second), jnp.where(odd(index), second, first)


def extend_y(block, low, high, depth):
    at = iota((8, BZ), 0)
    tails = []
    for x in range(block.shape[0]):
        tail = jnp.zeros((8, BZ), F32)
        for i in range(depth):
            tail = jnp.where(at == i, high[i][x : x + 1], tail)
            tail = jnp.where(at == 8 - depth + i, low[i][x : x + 1], tail)
        tails.append(tail)
    return jnp.concatenate([block, jnp.stack(tails)], axis=1)


def roll_sum(x):
    count, rows, _ = x.shape
    beside = pltpu.roll(x, 1, 1) + pltpu.roll(x, rows - 1, 1)
    flat = x.reshape(count * rows, BZ)
    at = iota(flat.shape, 1)
    beside_z = jnp.where(at == 0, 0.0, pltpu.roll(flat, 1, 1)) + jnp.where(at == BZ - 1, 0.0, pltpu.roll(flat, BZ - 1, 1))
    return beside + beside_z.reshape(x.shape)


def fine_solve(rows, sigma, tables):
    wh, wl, th, tl, vh, vl, uh, ul, column, beyond = tables
    high, low = value(wh), value(wl)
    for table in tables:
        if isinstance(table, Loaded):
            table.begin()
    rows = jnp.concatenate([rows, jnp.zeros((256 - YW, BZ), F32)], axis=0)
    spectra = dot3((high, low), split2(rows))
    th, tl, vh, vl, uh, ul, column, beyond = [value(table) for table in (th, tl, vh, vl, uh, ul, column, beyond)]
    nodal = []
    for half in range(2):
        part = spectra[:, half * HZ : (half + 1) * HZ]
        edge = spectra[:, HZ : HZ + 1] if half == 0 else spectra[:, HZ - 1 : HZ]
        part = dot3(split2(part), (th, tl)) + edge * beyond[half : half + 1]
        sig = jnp.where(column[:, 1:2] == 0.0, repeat_lanes(sigma, half), repeat_lanes(sigma, 2 + half))
        part = part / (column[:, 0:1] + beyond[2:3] + sig)
        part = jnp.concatenate([part, jnp.zeros((256 - AB, HW), F32)], axis=0)
        part = dot3((vh, vl), split2(part))
        nodal.append(dot3(split2(part), (uh, ul)).reshape(BX, BY, HZ))
    return jnp.concatenate(nodal, axis=2)


def value(table):
    return (table.here() if isinstance(table, Loaded) else table)[...]


def repeat_lanes(row, group):
    only = jnp.where(iota((1, ELEMS), 1) // 32 == group, row, 0.0)
    only = only + pltpu.roll(only, 64, 1)
    only = only + pltpu.roll(only, 32, 1)
    return jnp.concatenate([only] * 3, axis=1)


def eye_mask():
    return iota((ELEMS, ELEMS), 0) == iota((ELEMS, ELEMS), 1)


def row_to_column(row):
    return jnp.sum(jnp.where(eye_mask(), row, 0.0), axis=1, keepdims=True)


def column_to_row(column):
    return jnp.sum(jnp.where(eye_mask(), column, 0.0), axis=0, keepdims=True)


def pad_tile(rows):
    at = iota((8, ELEMS), 0)
    tile = jnp.zeros((8, ELEMS), F32)
    for i, row in enumerate(rows):
        tile = jnp.where(at == i, row, tile)
    return jnp.concatenate([tile, jnp.zeros((8, BZ - ELEMS), F32)], axis=1)


def start_kernel(
    late, right_far, diagonal_far, slots_far, c, ya, yb, right, diagonal, slots_out, table_out
):
    d = lax.axis_index("narrow")
    right_load = late.start(right_far, right)
    diagonal_load = late.start(diagonal_far, diagonal)
    slots_in = slots_far.here()
    slots = jnp.concatenate([slots_in[0:1], slots_in[1:2]], axis=1).astype(F32)
    slots_out[...] = slots
    table = gather_table()
    table_out[...] = table
    right_load.wait()
    row = column_to_row(to_rows(element_row(right[...], table) * (1.0 / 16.0), slots, 0))
    c[...] = row
    diagonal_load.wait()
    for i, ref in enumerate((right, diagonal)):
        ya[i], yb[i] = pair_out(d, ref[:, 0, :], ref[:, BY - 1, :])
    ya[2] = pad_tile([row, slots])
    yb[2] = jnp.zeros((8, BZ), F32)


def stage_kernel(swapped, late, factor, *refs):
    d = lax.axis_index("narrow")
    half = ELEMS // 2
    at = pl.multiple_of(d * half, half) if swapped else 0
    there = pl.multiple_of((1 - d) * half, half) if swapped else half
    after, diagonal, table, sent, kept, done, sigma = refs[STAGED : STAGED + 7]
    late.start(factor.at[pl.ds(at, half)], kept)
    late.start(factor.at[pl.ds(there, half)], sent)
    for source, target in zip(refs[:STAGED], refs[STAGED + 7 :]):
        late.start(source, target)
    done[...] = after[...]
    sigma[...] = element_row(diagonal[...], table[...]) * (1.0 / 512.0)


def project_kernel(swapped, late, c, ra, rb, right, diagonal, kept, sent, sums, xa, xb):
    w, d = lax.axis_index("wide"), lax.axis_index("narrow")
    row = c[...]
    if swapped:
        half = ELEMS // 2
        other = ra[2, 0:1, 0:ELEMS]
        row = jnp.where(d == 0, row, pltpu.roll(row, half, 1))
        other = jnp.where(d == 0, pltpu.roll(other, half, 1), other)
        row = jnp.where(iota((1, ELEMS), 1) < half, row, other)
    store_sum(sums, project(row_to_column(row), (kept, sent)), jnp.zeros((1, 128), F32))
    for i, ref in enumerate((right, diagonal)):
        low, high = pair_in(d, ra[i], rb[i])
        layers = [extend_y(ref[x : x + 1], [low[x : x + 1]], [high[x : x + 1]], 1)[0] for x in (0, BX - 1)]
        xa[i], xb[i] = pair_out(w, *layers)


def widened(block, ya, yb, xa, xb, i):
    w, d = lax.axis_index("wide"), lax.axis_index("narrow")
    low, high = pair_in(d, ya[i], yb[i])
    x_low, x_high = pair_in(w, xa[i], xb[i])
    return jnp.concatenate([x_low[None], extend_y(block, [low], [high], 1), x_high[None]], axis=0)


def first_fine_kernel(late, *rest):
    right, ya, yb, xa, xb, sigma, solved = rest[TABLES:]
    rows = widened(right[...], ya, yb, xa, xb, 0)
    tables = rest[TABLES - STAGED : TABLES] + rest[: TABLES - STAGED]
    solved[...] = fine_solve(rows.reshape(YW, BZ), sigma[...], tables)


def first_coarse_kernel(swapped, late, sums, solved, slots, kept, sent, ya, yb):
    d = lax.axis_index("narrow")
    row = jnp.sum(sums[...], axis=0)[:, 0:KCOL]
    column = correct(row, (kept, sent))
    for i in range(2):
        ya[i], yb[i] = pair_out(d, solved[:, i, :], solved[:, BY - 2 + i, :])
    if swapped:
        values = column_to_row(column)
        values = jnp.where(d == 0, values, pltpu.roll(values, ELEMS // 2, 1))
    else:
        values = to_elements(column, slots[...], 0)
    ya[2] = pad_tile([values])
    yb[2] = ya[2]


def extend_kernel(swapped, late, solved, slots, ra_first, own_ref, ra, rb, search, xa, xb):
    w, d = lax.axis_index("wide"), lax.axis_index("narrow")
    groups = lax.axis_size("narrow")
    own = own_ref[2, 0:1, 0:ELEMS]
    theirs = ra[2, 0:1, 0:ELEMS]
    if swapped:
        half = ELEMS // 2
        at = iota((1, ELEMS), 1) // half
        other = jnp.where(at == d, pltpu.roll(own, half, 1), theirs)
        own = jnp.where(at == d, own, pltpu.roll(theirs, half, 1))
        own = to_elements(row_to_column(own), slots[...], 0)
        other = to_elements(row_to_column(other), ra_first[2, 1:2, 0:ELEMS], 0)
        values_low, values_high = other, other
    else:
        values_low, values_high = pair_in(d, theirs, rb[2, 0:1, 0:ELEMS])
    values_low = jnp.where(d > 0, values_low, 0.0)
    values_high = jnp.where(d < groups - 1, values_high, 0.0)
    wide = expand_rows(jnp.concatenate([own, values_low, values_high], axis=0)) * (1.0 / 16.0)
    coarse = jnp.concatenate(
        [jnp.broadcast_to(wide[0:1, 0:BZ], (8, BZ)), jnp.broadcast_to(wide[0:1, BZ:], (8, BZ))], axis=0
    )
    low, high = [], []
    for i in range(2):
        one, two = pair_in(d, ra[i], rb[i])
        low.append(one + wide[1:2, BZ:])
        high.append(two + wide[2:3, 0:BZ])
    block = extend_y(solved[...] + coarse[None], low, high, 2)
    search[...] = block
    xa[...], xb[...] = pair_out(w, block[0:2], block[BX - 2 : BX])


def interior_kernel(late, diagonal_late, right, search, ya, yb, image, product, table, diagonal):
    d = lax.axis_index("narrow")
    low, high = pair_in(d, ya[1], yb[1])
    centre = search[...]
    diagonal[...] = diagonal_late.here()[...]
    part = (6.0 + extend_y(diagonal[...], [low], [high], 1)) * centre - roll_sum(centre)
    zero = jnp.zeros((1, YR, BZ), F32)
    part = part - jnp.concatenate([zero, centre[0 : BX - 1]], axis=0) - jnp.concatenate([centre[1:BX], zero], axis=0)
    image[...] = part
    product[...] = lanes([total(right[...] * centre[:, 0:BY])])
    table[...] = gather_table()


def operator_kernel(
    swapped, sizes, late, kept, received, search, inner, product, table, sa, sb, xa, xb, slots, sums, image_out, halo
):
    w, d = lax.axis_index("wide"), lax.axis_index("narrow")
    owned, offset = (kept, received), d * (ELEMS // 2) if swapped else 0
    s_low, s_high = pair_in(w, sa[...], sb[...])
    d_low, d_high = pair_in(w, xa[1], xb[1])
    low = (6.0 + d_low) * s_low[1] - s_low[0] - search[0] - roll_sum(s_low[1:2])[0]
    high = (6.0 + d_high) * s_high[0] - s_high[1] - search[BX - 1] - roll_sum(s_high[0:1])[0]
    y = iota((YR, BZ), 0)
    inside = (y < BY) | ((y == BY) & (d < sizes[1] - 1)) | ((y == YR - 1) & (d > 0))
    image_out[0] = jnp.where(inside & (w > 0), low, 0.0)
    image_out[1] = jnp.where(inside, inner[0] - s_low[1], 0.0)
    image_out[2:BX] = jnp.where(inside[None], inner[1 : BX - 1], 0.0)
    image_out[BX] = jnp.where(inside, inner[BX - 1] - s_high[0], 0.0)
    image_out[BX + 1] = jnp.where(inside & (w < sizes[0] - 1), high, 0.0)
    halo[0:BY] = s_low[1, 0:BY]
    halo[BY : 2 * BY] = s_high[0, 0:BY]
    halo[2 * BY : 2 * BY + 8] = search[:, YR - 1, :]
    halo[2 * BY + 8 : 3 * BY] = search[:, BY, :]
    own = image_out[1 : BX + 1, 0:BY, :]
    column = to_rows(element_row(own, table[...]) * (1.0 / 16.0), slots[...], offset)
    extra = lanes([lane(product[...], 0), total(search[:, 0:BY, :] * own)])
    store_sum(sums, project(column, owned), extra)


def second_fine_kernel(late, *rest):
    w, d = lax.axis_index("wide"), lax.axis_index("narrow")
    image, sigma, solved, ya, yb, xa, xb = rest[TABLES:]
    out = fine_solve(image[...].reshape(YW, BZ), sigma[...], rest[:TABLES])
    solved[...] = out
    ya[...], yb[...] = pair_out(d, solved[:, 0, :], solved[:, BY - 1, :])
    xa[...], xb[...] = pair_out(w, out[0], out[BX - 1])


def second_coarse_kernel(
    swapped, late, right, diagonal, kept, received, sums, solved, fya, fyb, fxa, fxb, search, halo, image, slots,
    search_out, image_out, last, products,
):
    w, d = lax.axis_index("wide"), lax.axis_index("narrow")
    owned, offset = (kept, received), d * (ELEMS // 2) if swapped else 0
    row = jnp.sum(sums[...], axis=0)
    products[...] = row[:, KCOL:WIDTH]
    step = lane(row[:, KCOL:WIDTH], 0) / lane(row[:, KCOL:WIDTH], 1)
    values = to_elements(correct(row[:, 0:KCOL], owned), slots[...], offset)
    coarse = expand_block(values * (1.0 / 16.0))
    own_search = search[:, 0:BY, :]
    own_image = image[1 : BX + 1, 0:BY, :]
    vector = own_search - step * (solved[...] + coarse[None])
    f_low, f_high = pair_in(w, fxa[...], fxb[...])
    x_low = halo[0:BY] - step * f_low
    x_high = halo[BY : 2 * BY] - step * f_high
    g_low, g_high = pair_in(d, fya[...], fyb[...])
    y_low = halo[2 * BY : 2 * BY + 8] - step * g_low
    y_high = halo[2 * BY + 8 : 3 * BY] - step * g_high
    beside = roll_sum(extend_y(vector, [y_low], [y_high], 1))[:, 0:BY]
    beside = beside + jnp.concatenate([x_low[None], vector[0 : BX - 1]], axis=0)
    beside = beside + jnp.concatenate([vector[1:BX], x_high[None]], axis=0)
    next_image = (6.0 + diagonal[...]) * vector - beside
    search_out[...] = vector
    image_out[...] = next_image
    residual = right[...] - step * own_image
    edges = total(coarse * (x_low + x_high)) + total(y_low * coarse[0:1]) + total(y_high * coarse[BY - 1 : BY])
    store_sum(
        last,
        values,
        lanes([total(residual * vector), total(vector * next_image) + step * edges, total(vector * own_image)]),
    )


def last_kernel(sizes, late, right, products, last, search, image, next_search, next_image, x_out, r_out):
    w, d = lax.axis_index("wide"), lax.axis_index("narrow")
    groups = sizes[1]
    count = sizes[0] * groups
    product, bottom = lane(products[...], 0), lane(products[...], 1)
    step = product / bottom
    z = last[:, 0, 0:ELEMS]
    rows = iota((count, ELEMS), 0)
    at = iota((count, ELEMS), 1)
    faces = jnp.where(rows < count - groups, z * pltpu.roll(z, count - groups, 0), 0.0)
    across = pltpu.roll(pltpu.roll(z, count - 1, 0), EZ, 1)
    faces = faces + jnp.where((lax.rem(rows, groups) < groups - 1) & (at >= EZ), z * across, 0.0)
    sums = jnp.sum(last[:, :, ELEMS:], axis=0)
    next_product = lane(sums, 0)
    quadratic = lane(sums, 1) - step * step * 0.5 * total(faces)
    cross = lane(sums, 2)
    me = w * groups + d
    picked = []
    for index, there in ((me - groups, w > 0), (me + groups, w < sizes[0] - 1), (me - 1, d > 0), (me + 1, d < groups - 1)):
        picked.append(jnp.sum(jnp.where((rows == index) & there, z, 0.0), axis=0, keepdims=True))
    wide = expand_rows(jnp.concatenate(picked, axis=0)) * (1.0 / 16.0)
    layers = []
    for i in range(2):
        low = jnp.broadcast_to(wide[i : i + 1, 0:BZ], (8, BZ))
        high = jnp.broadcast_to(wide[i : i + 1, BZ:], (8, BZ))
        layers.append(jnp.concatenate([low, high], axis=0)[None])
    shape = (BX, BY, BZ)
    x, y = iota(shape, 0), iota(shape, 1)
    missing = jnp.where(x == 0, layers[0], 0.0) + jnp.where(x == BX - 1, layers[1], 0.0)
    missing = missing + jnp.where(y == 0, wide[2:3, BZ:][None], 0.0) + jnp.where(y == BY - 1, wide[3:4, 0:BZ][None], 0.0)
    ratio = next_product / product
    curvature = quadratic + 2.0 * ratio * cross + ratio * ratio * bottom
    step_next = next_product / curvature
    own_search = search[:, 0:BY, :]
    own_image = image[1 : BX + 1, 0:BY, :]
    direction = next_search[...] + ratio * own_search
    total_image = next_image[...] + step * missing + ratio * own_image
    x_out[...] = step * own_search + step_next * direction
    r_out[...] = (right[...] - step * own_image) - step_next * total_image


class Loaded:
    def __init__(self, copy, ref):
        self.copy, self.ref, self.begun, self.ready = copy, ref, False, False

    def begin(self):
        if not self.begun:
            self.copy.start()
            self.begun = True

    def wait(self):
        self.begin()
        if not self.ready:
            self.copy.wait()
            self.ready = True

    def here(self):
        self.wait()
        return self.ref


class Copies:
    def __init__(self, semaphores):
        self.semaphores, self.all = semaphores, []

    def start(self, source, target, begin=True):
        self.all.append(Loaded(pltpu.make_async_copy(source, target, self.semaphores.at[len(self.all)]), target))
        if begin:
            self.all[-1].begin()
        return self.all[-1]

    def finish(self):
        for loaded in self.all:
            loaded.wait()


def call(kernel, outs, far=(), late=(), near=(), final=False, first_wave=99):
    first, second = len(far), len(far) + len(late)

    def run(*refs):
        end = len(refs) - 1 - len(late)
        copies = Copies(refs[-1])
        loaded = [
            copies.start(source, target, i < first_wave)
            for i, (source, target) in enumerate(zip(refs[first:second], refs[end:-1]))
        ]
        kernel(copies, *refs[:first], *loaded, *refs[second:end])
        copies.finish()

    shape_of = jax.ShapeDtypeStruct if final else pltpu.VMEM
    spaces = [pltpu.HBM] * second + [pltpu.VMEM] * len(near)
    return pl.pallas_call(
        run,
        out_shape=[shape_of(getattr(out, "shape", out), getattr(out, "dtype", F32)) for out in outs],
        in_specs=[pl.BlockSpec(memory_space=space) for space in spaces],
        out_specs=[pl.BlockSpec(memory_space=pltpu.VMEM)] * len(outs),
        scratch_shapes=[*(pltpu.VMEM(array.shape, array.dtype) for array in late), pltpu.SemaphoreType.DMA((second + 2,))],
        compiler_params=pltpu.CompilerParams(vmem_limit_bytes=16 * 1024 * 1024),
    )(*(pltpu.with_memory_space_constraint(array, pltpu.HBM) for array in (*far, *late)), *near)


def pair_swap(first, second, axis):
    size = lax.axis_size(axis)
    received = []
    for value, begin in ((first, 0), (second, 1)):
        perm = []
        for i in range(begin, size - 1, 2):
            perm += [(i, i + 1), (i + 1, i)]
        received.append(lax.ppermute(value, axis, perm) if perm else jnp.zeros_like(value))
    return received


def everywhere(rows):
    return lax.all_to_all(rows, AXES, split_axis=0, concat_axis=0, tiled=True)


def body(right, diagonal, coarse_slot, factor):
    sizes = (lax.axis_size("wide"), lax.axis_size("narrow"))
    groups = sizes[1]
    count = sizes[0] * groups
    fine = [jnp.asarray(c) for c in tables()]
    slots = coarse_slot.reshape(EY, EZ)
    swapped = groups == 2
    if not swapped:
        factor = factor.reshape(groups, ELEMS // groups, KCOL)
        factor = lax.all_to_all(factor, "narrow", split_axis=0, concat_axis=0, tiled=True).reshape(ELEMS, KCOL)
    part = functools.partial

    block, layer, extended = (BX, BY, BZ), (YR, BZ), (BX, YR, BZ)
    y_shape, x_shape, half = (3, BX, BZ), (2, YR, BZ), (ELEMS // 2, KCOL)
    gather = jax.ShapeDtypeStruct((BZ, EY * ELEMS), BF16)
    diagonal_far = diagonal
    c, ya, yb, right, diagonal, slots, table = call(
        start_kernel,
        [(1, ELEMS), y_shape, y_shape, block, block, (1, ELEMS), gather],
        far=[right, diagonal],
        late=[slots],
    )
    ya, yb = pair_swap(ya, yb, "narrow")
    sent, kept, c, sigma, *near = call(
        part(stage_kernel, swapped),
        [half, half, (1, ELEMS), (1, ELEMS), *fine[:STAGED]],
        far=[factor, *fine[:STAGED]],
        near=[c, diagonal, table],
    )
    sums, xa, xb = call(
        part(project_kernel, swapped), [(count, 1, WIDTH), x_shape, x_shape], near=[c, ya, yb, right, diagonal, kept, sent]
    )
    sums = everywhere(sums)
    xa, xb = pair_swap(xa, xb, "wide")
    (solved,) = call(first_fine_kernel, [block], late=fine[STAGED:], near=[*near, right, ya, yb, xa, xb, sigma])
    ta, tb = call(part(first_coarse_kernel, swapped), [y_shape, y_shape], near=[sums, solved, slots, kept, sent])
    ra, rb = pair_swap(ta, tb, "narrow")
    received = lax.ppermute(sent, "narrow", [(0, 1), (1, 0)]) if swapped else sent
    search, sa, sb = call(
        part(extend_kernel, swapped),
        [extended, (2,) + layer, (2,) + layer],
        near=[solved, slots, ya, ta, ra, rb],
    )
    sa, sb = pair_swap(sa, sb, "wide")
    inner, product, table, diagonal = call(
        interior_kernel, [extended, (1, 128), gather, block], late=[diagonal_far], near=[right, search, ya, yb]
    )
    sums, image, halo = call(
        part(operator_kernel, swapped, sizes),
        [(count, 1, WIDTH), (BX + 2, YR, BZ), (3 * BY, BZ)],
        near=[kept, received, search, inner, product, table, sa, sb, xa, xb, slots],
    )
    sums = everywhere(sums)
    solved, ya, yb, fa, fb = call(
        second_fine_kernel, [block, (BX, BZ), (BX, BZ), (BY, BZ), (BY, BZ)], late=fine, near=[image, sigma]
    )
    ya, yb = pair_swap(ya, yb, "narrow")
    fa, fb = pair_swap(fa, fb, "wide")
    next_search, next_image, last, products = call(
        part(second_coarse_kernel, swapped),
        [block, block, (count, 1, 2 * ELEMS), (1, 128)],
        near=[right, diagonal, kept, received, sums, solved, ya, yb, fa, fb, search, halo, image, slots],
    )
    last = everywhere(last)
    return tuple(
        call(
            part(last_kernel, sizes),
            [block, block],
            near=[right, products, last, search, image, next_search, next_image],
            final=True,
        )
    )


def solution(mesh):
    in_specs = (
        P("wide", "narrow", None),
        P("wide", "narrow", None),
        P("wide", "narrow", None),
        P(("wide", "narrow"), None),
    )
    out_specs = (P("wide", "narrow", None), P("wide", "narrow", None))
    return jax.shard_map(body, mesh=mesh, in_specs=in_specs, out_specs=out_specs, check_vma=False)
```

```python
import functools

import jax
import jax.numpy as jnp
import numpy as np
from jax import lax
from jax.experimental import pallas as pl
from jax.experimental.pallas import tpu as pltpu
from jax.sharding import PartitionSpec as P

F32 = jnp.float32
BF16 = jnp.bfloat16
BX, BY, BZ = 8, 16, 512
EY, EZ = 2, 64
ELEMS = EY * EZ
YR = 24
YW = YR * (BX + 2)
AB = 208
HZ = 256
HW = 384
STAGED = 6
AGAIN = 2
TABLES = 10
KCOL = 2048
WIDTH = KCOL + 128
AXES = ("wide", "narrow")


def split_const(values):
    high = values.astype(jnp.bfloat16)
    low = (values - high.astype(np.float64)).astype(jnp.bfloat16)
    return high, low


@functools.lru_cache(maxsize=None)
def tables():
    index = np.arange(10, dtype=np.float64)
    basis = np.sqrt(2.0 / 11.0) * np.sin(np.pi * (index[:, None] + 1.0) * (index[None, :] + 1.0) / 11.0)
    values = 2.0 - 2.0 * np.cos(np.pi * (index + 1.0) / 11.0)
    to_z = np.zeros((HZ, HW))
    from_z = np.zeros((HW, HZ))
    beyond = np.zeros((8, HW), np.float32)
    last = HZ // 8 - 1
    for e in range(last + 1):
        at = slice(e, 10 * (last + 1), last + 1)
        for k in range(10):
            z = 8 * e + k - 1
            if 0 <= z < HZ:
                to_z[z, at] = basis[k]
            if 1 <= k <= 8:
                from_z[at, z] = basis[k]
    beyond[0, last : 10 * (last + 1) : last + 1] = basis[9]
    beyond[1, 0 : 10 * (last + 1) : last + 1] = basis[0]
    beyond[2] = 1.0
    beyond[2, : 10 * (last + 1)] = np.repeat(values, last + 1)
    to_xy = np.zeros((10, EY, 10, 10, YR))
    from_xy = np.zeros((BX, BY, 10, EY, 10))
    for e in range(EY):
        for j in range(10):
            y = 8 * e + j - 1
            to_xy[:, e, :, :, y % YR] += basis.T[:, None, :] * basis[j][None, :, None]
            if 1 <= j <= 8:
                from_xy[:, y, :, e, :] = basis[1:9, :, None] * basis[j][None, None, :]
    to_xy = np.pad(to_xy.reshape(200, YW), ((0, AB - 200), (0, 256 - YW)))
    from_xy = np.pad(from_xy.reshape(BX * BY, 200), ((0, 0), (0, 256 - 200)))
    column = np.zeros((AB, 128), np.float32)
    grid = np.zeros((10, EY, 10, 2))
    grid[..., 0] = values[:, None, None] + values[None, None, :]
    grid[..., 1] = np.arange(EY)[None, :, None]
    column[:200, :2] = grid.reshape(200, 2)
    column[200:, 0] = 1.0
    return split_const(to_xy) + split_const(to_z) + split_const(from_xy) + split_const(from_z) + (column, beyond)


def dot(a, b):
    return jnp.dot(a, b, preferred_element_type=F32)


def split2(x):
    high = x.astype(BF16)
    return high, (x - high.astype(F32)).astype(BF16)


def split3(x):
    high = x.astype(BF16)
    rest = x - high.astype(F32)
    middle = rest.astype(BF16)
    return high, middle, (rest - middle.astype(F32)).astype(BF16)


def dot3(a, b):
    return dot(a[0], b[0]) + dot(a[0], b[1]) + dot(a[1], b[0])


def iota(shape, axis):
    return lax.broadcasted_iota(jnp.int32, shape, axis)


def total(x):
    while x.ndim > 2:
        x = jnp.sum(x, axis=0)
    return jnp.sum(jnp.sum(x, axis=0, keepdims=True), axis=1, keepdims=True)


def gather_table():
    shape = (BZ, EY * ELEMS)
    node, at = iota(shape, 0), iota(shape, 1)
    return jnp.where(at == node // 8 + (at // ELEMS) * (ELEMS + EZ), 1.0, 0.0).astype(BF16)


def spread_table():
    shape = (ELEMS, EY * BZ)
    element, at = iota(shape, 0), iota(shape, 1)
    return jnp.where(at // 8 == element, 1.0, 0.0).astype(BF16)


def element_row(field, table):
    parts = jnp.concatenate(split3(jnp.sum(field, axis=0)), axis=0)
    sums = dot(parts, table)
    sums = sums[0:16] + sums[16:32] + sums[32:48]
    return jnp.sum(sums[0:8, 0:ELEMS], axis=0, keepdims=True) + jnp.sum(sums[8:16, ELEMS:], axis=0, keepdims=True)


def expand_rows(rows):
    count = rows.shape[0]
    tall = jnp.broadcast_to(rows, (16, ELEMS)) if count == 1 else jnp.concatenate([rows, jnp.zeros((16 - count, ELEMS), F32)], axis=0)
    wide = dot(jnp.concatenate(split3(tall), axis=0), spread_table())
    return (wide[0:16] + wide[16:32] + wide[32:48])[0:count]


def expand_block(row):
    wide = expand_rows(row)
    low = jnp.broadcast_to(wide[:, 0:BZ], (8, BZ))
    high = jnp.broadcast_to(wide[:, BZ:], (8, BZ))
    return jnp.concatenate([low, high], axis=0)


def slot_mask(slots, offset):
    slot_of_row = lax.rem(iota((ELEMS, ELEMS), 0) + offset, ELEMS)
    return slot_of_row.astype(F32) == slots


def to_rows(element_values, slots, offset):
    return jnp.sum(jnp.where(slot_mask(slots, offset), element_values, 0.0), axis=1, keepdims=True)


def to_elements(row_values, slots, offset):
    return jnp.sum(jnp.where(slot_mask(slots, offset), row_values, 0.0), axis=0, keepdims=True)


def project(column, parts):
    out = 0.0
    at = 0
    for part in parts:
        size = part.shape[0]
        out = out + jnp.sum(column[at : at + size] * part[...], axis=0, keepdims=True)
        at += size
    return out


def correct(row, parts):
    out = []
    for part in parts:
        products = part[...] * row
        folded = products[:, 0:128]
        for at in range(128, KCOL, 128):
            folded = folded + products[:, at : at + 128]
        out.append(jnp.sum(folded, axis=1, keepdims=True))
    return jnp.concatenate(out, axis=0)


def store_sum(out_ref, first, second):
    count, _, width = out_ref.shape
    cut = width - 128
    out_ref[:, :, 0:cut] = jnp.broadcast_to(first[None], (count, 1, cut))
    out_ref[:, :, cut:width] = jnp.broadcast_to(second[None], (count, 1, 128))


def lanes(values):
    at = iota((1, 128), 1)
    row = jnp.zeros((1, 128), F32)
    for i, value in enumerate(values):
        row = jnp.where(at == i, value, row)
    return row


def lane(row, i):
    return jnp.sum(jnp.where(iota(row.shape, 1) == i, row, 0.0), axis=1, keepdims=True)


def odd(index):
    return lax.rem(index, 2) == 1


def pair_out(index, low, high):
    return jnp.where(odd(index), low, high), jnp.where(odd(index), high, low)


def pair_in(index, first, second):
    return jnp.where(odd(index), first, second), jnp.where(odd(index), second, first)


def extend_y(block, low, high, depth):
    at = iota((8, BZ), 0)
    tails = []
    for x in range(block.shape[0]):
        tail = jnp.zeros((8, BZ), F32)
        for i in range(depth):
            tail = jnp.where(at == i, high[i][x : x + 1], tail)
            tail = jnp.where(at == 8 - depth + i, low[i][x : x + 1], tail)
        tails.append(tail)
    return jnp.concatenate([block, jnp.stack(tails)], axis=1)


def roll_sum(x):
    count, rows, _ = x.shape
    beside = pltpu.roll(x, 1, 1) + pltpu.roll(x, rows - 1, 1)
    flat = x.reshape(count * rows, BZ)
    at = iota(flat.shape, 1)
    beside_z = jnp.where(at == 0, 0.0, pltpu.roll(flat, 1, 1)) + jnp.where(at == BZ - 1, 0.0, pltpu.roll(flat, BZ - 1, 1))
    return beside + beside_z.reshape(x.shape)


def fine_solve(rows, sigma, tables):
    wh, wl, th, tl, vh, vl, uh, ul, column, beyond = tables
    high, low = value(wh), value(wl)
    for table in tables:
        if isinstance(table, Loaded):
            table.begin()
    rows = jnp.concatenate([rows, jnp.zeros((256 - YW, BZ), F32)], axis=0)
    spectra = dot3((high, low), split2(rows))
    th, tl, vh, vl, uh, ul, column, beyond = [value(table) for table in (th, tl, vh, vl, uh, ul, column, beyond)]
    nodal = []
    for half in range(2):
        part = spectra[:, half * HZ : (half + 1) * HZ]
        edge = spectra[:, HZ : HZ + 1] if half == 0 else spectra[:, HZ - 1 : HZ]
        part = dot3(split2(part), (th, tl)) + edge * beyond[half : half + 1]
        sig = jnp.where(column[:, 1:2] == 0.0, repeat_lanes(sigma, half), repeat_lanes(sigma, 2 + half))
        part = part / (column[:, 0:1] + beyond[2:3] + sig)
        part = jnp.concatenate([part, jnp.zeros((256 - AB, HW), F32)], axis=0)
        part = dot3((vh, vl), split2(part))
        nodal.append(dot3(split2(part), (uh, ul)).reshape(BX, BY, HZ))
    return jnp.concatenate(nodal, axis=2)


def value(table):
    return (table.here() if isinstance(table, Loaded) else table)[...]


def repeat_lanes(row, group):
    only = jnp.where(iota((1, ELEMS), 1) // 32 == group, row, 0.0)
    only = only + pltpu.roll(only, 64, 1)
    only = only + pltpu.roll(only, 32, 1)
    return jnp.concatenate([only] * 3, axis=1)


def eye_mask():
    return iota((ELEMS, ELEMS), 0) == iota((ELEMS, ELEMS), 1)


def row_to_column(row):
    return jnp.sum(jnp.where(eye_mask(), row, 0.0), axis=1, keepdims=True)


def column_to_row(column):
    return jnp.sum(jnp.where(eye_mask(), column, 0.0), axis=0, keepdims=True)


def pad_tile(rows):
    at = iota((8, ELEMS), 0)
    tile = jnp.zeros((8, ELEMS), F32)
    for i, row in enumerate(rows):
        tile = jnp.where(at == i, row, tile)
    return jnp.concatenate([tile, jnp.zeros((8, BZ - ELEMS), F32)], axis=1)


def start_kernel(
    late, right_far, diagonal_far, slots_far, c, ya, yb, right, diagonal, slots_out, table_out
):
    d = lax.axis_index("narrow")
    right_load = late.start(right_far, right)
    diagonal_load = late.start(diagonal_far, diagonal)
    slots_in = slots_far.here()
    slots = jnp.concatenate([slots_in[0:1], slots_in[1:2]], axis=1).astype(F32)
    slots_out[...] = slots
    table = gather_table()
    table_out[...] = table
    right_load.wait()
    row = column_to_row(to_rows(element_row(right[...], table) * (1.0 / 16.0), slots, 0))
    c[...] = row
    diagonal_load.wait()
    for i, ref in enumerate((right, diagonal)):
        ya[i], yb[i] = pair_out(d, ref[:, 0, :], ref[:, BY - 1, :])
    ya[2] = pad_tile([row, slots])
    yb[2] = jnp.zeros((8, BZ), F32)


def stage_kernel(swapped, late, factor, *refs):
    d = lax.axis_index("narrow")
    half = ELEMS // 2
    at = pl.multiple_of(d * half, half) if swapped else 0
    there = pl.multiple_of((1 - d) * half, half) if swapped else half
    after, diagonal, table, sent, kept, done, sigma = refs[STAGED : STAGED + 7]
    late.start(factor.at[pl.ds(at, half)], kept)
    late.start(factor.at[pl.ds(there, half)], sent)
    for source, target in zip(refs[:STAGED], refs[STAGED + 7 :]):
        late.start(source, target)
    done[...] = after[...]
    sigma[...] = element_row(diagonal[...], table[...]) * (1.0 / 512.0)


def project_kernel(swapped, late, c, ra, rb, right, diagonal, kept, sent, sums, xa, xb):
    w, d = lax.axis_index("wide"), lax.axis_index("narrow")
    row = c[...]
    if swapped:
        half = ELEMS // 2
        other = ra[2, 0:1, 0:ELEMS]
        row = jnp.where(d == 0, row, pltpu.roll(row, half, 1))
        other = jnp.where(d == 0, pltpu.roll(other, half, 1), other)
        row = jnp.where(iota((1, ELEMS), 1) < half, row, other)
    store_sum(sums, project(row_to_column(row), (kept, sent)), jnp.zeros((1, 128), F32))
    for i, ref in enumerate((right, diagonal)):
        low, high = pair_in(d, ra[i], rb[i])
        layers = [extend_y(ref[x : x + 1], [low[x : x + 1]], [high[x : x + 1]], 1)[0] for x in (0, BX - 1)]
        xa[i], xb[i] = pair_out(w, *layers)


def widened(block, ya, yb, xa, xb, i):
    w, d = lax.axis_index("wide"), lax.axis_index("narrow")
    low, high = pair_in(d, ya[i], yb[i])
    x_low, x_high = pair_in(w, xa[i], xb[i])
    return jnp.concatenate([x_low[None], extend_y(block, [low], [high], 1), x_high[None]], axis=0)


def first_fine_kernel(late, *rest):
    right, ya, yb, xa, xb, sigma, solved = rest[TABLES:]
    rows = widened(right[...], ya, yb, xa, xb, 0)
    tables = rest[TABLES - STAGED : TABLES] + rest[: TABLES - STAGED]
    solved[...] = fine_solve(rows.reshape(YW, BZ), sigma[...], tables)


def first_coarse_kernel(swapped, late, sums, solved, slots, kept, sent, ya, yb):
    d = lax.axis_index("narrow")
    row = jnp.sum(sums[...], axis=0)[:, 0:KCOL]
    column = correct(row, (kept, sent))
    for i in range(2):
        ya[i], yb[i] = pair_out(d, solved[:, i, :], solved[:, BY - 2 + i, :])
    if swapped:
        values = column_to_row(column)
        values = jnp.where(d == 0, values, pltpu.roll(values, ELEMS // 2, 1))
    else:
        values = to_elements(column, slots[...], 0)
    ya[2] = pad_tile([values])
    yb[2] = ya[2]


def extend_kernel(swapped, late, solved, slots, ra_first, own_ref, ra, rb, search, xa, xb):
    w, d = lax.axis_index("wide"), lax.axis_index("narrow")
    groups = lax.axis_size("narrow")
    own = own_ref[2, 0:1, 0:ELEMS]
    theirs = ra[2, 0:1, 0:ELEMS]
    if swapped:
        half = ELEMS // 2
        at = iota((1, ELEMS), 1) // half
        other = jnp.where(at == d, pltpu.roll(own, half, 1), theirs)
        own = jnp.where(at == d, own, pltpu.roll(theirs, half, 1))
        own = to_elements(row_to_column(own), slots[...], 0)
        other = to_elements(row_to_column(other), ra_first[2, 1:2, 0:ELEMS], 0)
        values_low, values_high = other, other
    else:
        values_low, values_high = pair_in(d, theirs, rb[2, 0:1, 0:ELEMS])
    values_low = jnp.where(d > 0, values_low, 0.0)
    values_high = jnp.where(d < groups - 1, values_high, 0.0)
    wide = expand_rows(jnp.concatenate([own, values_low, values_high], axis=0)) * (1.0 / 16.0)
    coarse = jnp.concatenate(
        [jnp.broadcast_to(wide[0:1, 0:BZ], (8, BZ)), jnp.broadcast_to(wide[0:1, BZ:], (8, BZ))], axis=0
    )
    low, high = [], []
    for i in range(2):
        one, two = pair_in(d, ra[i], rb[i])
        low.append(one + wide[1:2, BZ:])
        high.append(two + wide[2:3, 0:BZ])
    block = extend_y(solved[...] + coarse[None], low, high, 2)
    search[...] = block
    xa[...], xb[...] = pair_out(w, block[0:2], block[BX - 2 : BX])


def interior_kernel(late, *refs):
    for source, target in zip(refs[:AGAIN], refs[AGAIN + 9 :]):
        late.start(source, target)
    diagonal_late, right, search, ya, yb, image, product, table, diagonal = refs[AGAIN : AGAIN + 9]
    d = lax.axis_index("narrow")
    low, high = pair_in(d, ya[1], yb[1])
    centre = search[...]
    diagonal[...] = diagonal_late.here()[...]
    part = (6.0 + extend_y(diagonal[...], [low], [high], 1)) * centre - roll_sum(centre)
    zero = jnp.zeros((1, YR, BZ), F32)
    part = part - jnp.concatenate([zero, centre[0 : BX - 1]], axis=0) - jnp.concatenate([centre[1:BX], zero], axis=0)
    image[...] = part
    product[...] = lanes([total(right[...] * centre[:, 0:BY])])
    table[...] = gather_table()


def operator_kernel(
    swapped, sizes, late, kept, received, search, inner, product, table, sa, sb, xa, xb, slots, sums, image_out, halo
):
    w, d = lax.axis_index("wide"), lax.axis_index("narrow")
    owned, offset = (kept, received), d * (ELEMS // 2) if swapped else 0
    s_low, s_high = pair_in(w, sa[...], sb[...])
    d_low, d_high = pair_in(w, xa[1], xb[1])
    low = (6.0 + d_low) * s_low[1] - s_low[0] - search[0] - roll_sum(s_low[1:2])[0]
    high = (6.0 + d_high) * s_high[0] - s_high[1] - search[BX - 1] - roll_sum(s_high[0:1])[0]
    y = iota((YR, BZ), 0)
    inside = (y < BY) | ((y == BY) & (d < sizes[1] - 1)) | ((y == YR - 1) & (d > 0))
    image_out[0] = jnp.where(inside & (w > 0), low, 0.0)
    image_out[1] = jnp.where(inside, inner[0] - s_low[1], 0.0)
    image_out[2:BX] = jnp.where(inside[None], inner[1 : BX - 1], 0.0)
    image_out[BX] = jnp.where(inside, inner[BX - 1] - s_high[0], 0.0)
    image_out[BX + 1] = jnp.where(inside & (w < sizes[0] - 1), high, 0.0)
    halo[0:BY] = s_low[1, 0:BY]
    halo[BY : 2 * BY] = s_high[0, 0:BY]
    halo[2 * BY : 2 * BY + 8] = search[:, YR - 1, :]
    halo[2 * BY + 8 : 3 * BY] = search[:, BY, :]
    own = image_out[1 : BX + 1, 0:BY, :]
    column = to_rows(element_row(own, table[...]) * (1.0 / 16.0), slots[...], offset)
    extra = lanes([lane(product[...], 0), total(search[:, 0:BY, :] * own)])
    store_sum(sums, project(column, owned), extra)


def second_fine_kernel(late, *rest):
    w, d = lax.axis_index("wide"), lax.axis_index("narrow")
    image, sigma, solved, ya, yb, xa, xb = rest[TABLES:]
    out = fine_solve(image[...].reshape(YW, BZ), sigma[...], rest[TABLES - AGAIN : TABLES] + rest[: TABLES - AGAIN])
    solved[...] = out
    ya[...], yb[...] = pair_out(d, solved[:, 0, :], solved[:, BY - 1, :])
    xa[...], xb[...] = pair_out(w, out[0], out[BX - 1])


def second_coarse_kernel(
    swapped, late, right, diagonal, kept, received, sums, solved, fya, fyb, fxa, fxb, search, halo, image, slots,
    search_out, image_out, last, products,
):
    w, d = lax.axis_index("wide"), lax.axis_index("narrow")
    owned, offset = (kept, received), d * (ELEMS // 2) if swapped else 0
    row = jnp.sum(sums[...], axis=0)
    products[...] = row[:, KCOL:WIDTH]
    step = lane(row[:, KCOL:WIDTH], 0) / lane(row[:, KCOL:WIDTH], 1)
    values = to_elements(correct(row[:, 0:KCOL], owned), slots[...], offset)
    coarse = expand_block(values * (1.0 / 16.0))
    own_search = search[:, 0:BY, :]
    own_image = image[1 : BX + 1, 0:BY, :]
    vector = own_search - step * (solved[...] + coarse[None])
    f_low, f_high = pair_in(w, fxa[...], fxb[...])
    x_low = halo[0:BY] - step * f_low
    x_high = halo[BY : 2 * BY] - step * f_high
    g_low, g_high = pair_in(d, fya[...], fyb[...])
    y_low = halo[2 * BY : 2 * BY + 8] - step * g_low
    y_high = halo[2 * BY + 8 : 3 * BY] - step * g_high
    beside = roll_sum(extend_y(vector, [y_low], [y_high], 1))[:, 0:BY]
    beside = beside + jnp.concatenate([x_low[None], vector[0 : BX - 1]], axis=0)
    beside = beside + jnp.concatenate([vector[1:BX], x_high[None]], axis=0)
    next_image = (6.0 + diagonal[...]) * vector - beside
    search_out[...] = vector
    image_out[...] = next_image
    residual = right[...] - step * own_image
    edges = total(coarse * (x_low + x_high)) + total(y_low * coarse[0:1]) + total(y_high * coarse[BY - 1 : BY])
    store_sum(
        last,
        values,
        lanes([total(residual * vector), total(vector * next_image) + step * edges, total(vector * own_image)]),
    )


def last_kernel(sizes, late, right, products, last, search, image, next_search, next_image, x_out, r_out):
    w, d = lax.axis_index("wide"), lax.axis_index("narrow")
    groups = sizes[1]
    count = sizes[0] * groups
    product, bottom = lane(products[...], 0), lane(products[...], 1)
    step = product / bottom
    z = last[:, 0, 0:ELEMS]
    rows = iota((count, ELEMS), 0)
    at = iota((count, ELEMS), 1)
    faces = jnp.where(rows < count - groups, z * pltpu.roll(z, count - groups, 0), 0.0)
    across = pltpu.roll(pltpu.roll(z, count - 1, 0), EZ, 1)
    faces = faces + jnp.where((lax.rem(rows, groups) < groups - 1) & (at >= EZ), z * across, 0.0)
    sums = jnp.sum(last[:, :, ELEMS:], axis=0)
    next_product = lane(sums, 0)
    quadratic = lane(sums, 1) - step * step * 0.5 * total(faces)
    cross = lane(sums, 2)
    me = w * groups + d
    picked = []
    for index, there in ((me - groups, w > 0), (me + groups, w < sizes[0] - 1), (me - 1, d > 0), (me + 1, d < groups - 1)):
        picked.append(jnp.sum(jnp.where((rows == index) & there, z, 0.0), axis=0, keepdims=True))
    wide = expand_rows(jnp.concatenate(picked, axis=0)) * (1.0 / 16.0)
    layers = []
    for i in range(2):
        low = jnp.broadcast_to(wide[i : i + 1, 0:BZ], (8, BZ))
        high = jnp.broadcast_to(wide[i : i + 1, BZ:], (8, BZ))
        layers.append(jnp.concatenate([low, high], axis=0)[None])
    shape = (BX, BY, BZ)
    x, y = iota(shape, 0), iota(shape, 1)
    missing = jnp.where(x == 0, layers[0], 0.0) + jnp.where(x == BX - 1, layers[1], 0.0)
    missing = missing + jnp.where(y == 0, wide[2:3, BZ:][None], 0.0) + jnp.where(y == BY - 1, wide[3:4, 0:BZ][None], 0.0)
    ratio = next_product / product
    curvature = quadratic + 2.0 * ratio * cross + ratio * ratio * bottom
    step_next = next_product / curvature
    own_search = search[:, 0:BY, :]
    own_image = image[1 : BX + 1, 0:BY, :]
    direction = next_search[...] + ratio * own_search
    total_image = next_image[...] + step * missing + ratio * own_image
    x_out[...] = step * own_search + step_next * direction
    r_out[...] = (right[...] - step * own_image) - step_next * total_image


class Loaded:
    def __init__(self, copy, ref):
        self.copy, self.ref, self.begun, self.ready = copy, ref, False, False

    def begin(self):
        if not self.begun:
            self.copy.start()
            self.begun = True

    def wait(self):
        self.begin()
        if not self.ready:
            self.copy.wait()
            self.ready = True

    def here(self):
        self.wait()
        return self.ref


class Copies:
    def __init__(self, semaphores):
        self.semaphores, self.all = semaphores, []

    def start(self, source, target, begin=True):
        self.all.append(Loaded(pltpu.make_async_copy(source, target, self.semaphores.at[len(self.all)]), target))
        if begin:
            self.all[-1].begin()
        return self.all[-1]

    def finish(self):
        for loaded in self.all:
            loaded.wait()


def call(kernel, outs, far=(), late=(), near=(), final=False, first_wave=99):
    first, second = len(far), len(far) + len(late)

    def run(*refs):
        end = len(refs) - 1 - len(late)
        copies = Copies(refs[-1])
        loaded = [
            copies.start(source, target, i < first_wave)
            for i, (source, target) in enumerate(zip(refs[first:second], refs[end:-1]))
        ]
        kernel(copies, *refs[:first], *loaded, *refs[second:end])
        copies.finish()

    shape_of = jax.ShapeDtypeStruct if final else pltpu.VMEM
    spaces = [pltpu.HBM] * second + [pltpu.VMEM] * len(near)
    return pl.pallas_call(
        run,
        out_shape=[shape_of(getattr(out, "shape", out), getattr(out, "dtype", F32)) for out in outs],
        in_specs=[pl.BlockSpec(memory_space=space) for space in spaces],
        out_specs=[pl.BlockSpec(memory_space=pltpu.VMEM)] * len(outs),
        scratch_shapes=[*(pltpu.VMEM(array.shape, array.dtype) for array in late), pltpu.SemaphoreType.DMA((second + 2,))],
        compiler_params=pltpu.CompilerParams(vmem_limit_bytes=16 * 1024 * 1024),
    )(*(pltpu.with_memory_space_constraint(array, pltpu.HBM) for array in (*far, *late)), *near)


def pair_swap(first, second, axis):
    size = lax.axis_size(axis)
    received = []
    for value, begin in ((first, 0), (second, 1)):
        perm = []
        for i in range(begin, size - 1, 2):
            perm += [(i, i + 1), (i + 1, i)]
        received.append(lax.ppermute(value, axis, perm) if perm else jnp.zeros_like(value))
    return received


def everywhere(rows):
    return lax.all_to_all(rows, AXES, split_axis=0, concat_axis=0, tiled=True)


def body(right, diagonal, coarse_slot, factor):
    sizes = (lax.axis_size("wide"), lax.axis_size("narrow"))
    groups = sizes[1]
    count = sizes[0] * groups
    fine = [jnp.asarray(c) for c in tables()]
    slots = coarse_slot.reshape(EY, EZ)
    swapped = groups == 2
    if not swapped:
        factor = factor.reshape(groups, ELEMS // groups, KCOL)
        factor = lax.all_to_all(factor, "narrow", split_axis=0, concat_axis=0, tiled=True).reshape(ELEMS, KCOL)
    part = functools.partial

    block, layer, extended = (BX, BY, BZ), (YR, BZ), (BX, YR, BZ)
    y_shape, x_shape, half = (3, BX, BZ), (2, YR, BZ), (ELEMS // 2, KCOL)
    gather = jax.ShapeDtypeStruct((BZ, EY * ELEMS), BF16)
    diagonal_far = diagonal
    c, ya, yb, right, diagonal, slots, table = call(
        start_kernel,
        [(1, ELEMS), y_shape, y_shape, block, block, (1, ELEMS), gather],
        far=[right, diagonal],
        late=[slots],
    )
    ya, yb = pair_swap(ya, yb, "narrow")
    sent, kept, c, sigma, *near = call(
        part(stage_kernel, swapped),
        [half, half, (1, ELEMS), (1, ELEMS), *fine[:STAGED]],
        far=[factor, *fine[:STAGED]],
        near=[c, diagonal, table],
    )
    sums, xa, xb = call(
        part(project_kernel, swapped), [(count, 1, WIDTH), x_shape, x_shape], near=[c, ya, yb, right, diagonal, kept, sent]
    )
    sums = everywhere(sums)
    xa, xb = pair_swap(xa, xb, "wide")
    (solved,) = call(first_fine_kernel, [block], late=fine[STAGED:], near=[*near, right, ya, yb, xa, xb, sigma])
    ta, tb = call(part(first_coarse_kernel, swapped), [y_shape, y_shape], near=[sums, solved, slots, kept, sent])
    ra, rb = pair_swap(ta, tb, "narrow")
    received = lax.ppermute(sent, "narrow", [(0, 1), (1, 0)]) if swapped else sent
    search, sa, sb = call(
        part(extend_kernel, swapped),
        [extended, (2,) + layer, (2,) + layer],
        near=[solved, slots, ya, ta, ra, rb],
    )
    sa, sb = pair_swap(sa, sb, "wide")
    inner, product, table, diagonal, *near = call(
        interior_kernel,
        [extended, (1, 128), gather, block, *fine[:AGAIN]],
        far=fine[:AGAIN],
        late=[diagonal_far],
        near=[right, search, ya, yb],
    )
    sums, image, halo = call(
        part(operator_kernel, swapped, sizes),
        [(count, 1, WIDTH), (BX + 2, YR, BZ), (3 * BY, BZ)],
        near=[kept, received, search, inner, product, table, sa, sb, xa, xb, slots],
    )
    sums = everywhere(sums)
    solved, ya, yb, fa, fb = call(
        second_fine_kernel, [block, (BX, BZ), (BX, BZ), (BY, BZ), (BY, BZ)], late=fine[AGAIN:], near=[*near, image, sigma]
    )
    ya, yb = pair_swap(ya, yb, "narrow")
    fa, fb = pair_swap(fa, fb, "wide")
    next_search, next_image, last, products = call(
        part(second_coarse_kernel, swapped),
        [block, block, (count, 1, 2 * ELEMS), (1, 128)],
        near=[right, diagonal, kept, received, sums, solved, ya, yb, fa, fb, search, halo, image, slots],
    )
    last = everywhere(last)
    return tuple(
        call(
            part(last_kernel, sizes),
            [block, block],
            near=[right, products, last, search, image, next_search, next_image],
            final=True,
        )
    )


def solution(mesh):
    in_specs = (
        P("wide", "narrow", None),
        P("wide", "narrow", None),
        P("wide", "narrow", None),
        P(("wide", "narrow"), None),
    )
    out_specs = (P("wide", "narrow", None), P("wide", "narrow", None))
    return jax.shard_map(body, mesh=mesh, in_specs=in_specs, out_specs=out_specs, check_vma=False)
```

```python
import functools

import jax
import jax.numpy as jnp
import numpy as np
from jax import lax
from jax.experimental import pallas as pl
from jax.experimental.pallas import tpu as pltpu
from jax.sharding import PartitionSpec as P

F32 = jnp.float32
BF16 = jnp.bfloat16
BX, BY, BZ = 8, 16, 512
EY, EZ = 2, 64
ELEMS = EY * EZ
YR = 24
YW = YR * (BX + 2)
AB = 208
HZ = 256
HW = 384
STAGED = 6
TABLES = 10
KCOL = 2048
WIDTH = KCOL + 128
AXES = ("wide", "narrow")


def split_const(values):
    high = values.astype(jnp.bfloat16)
    low = (values - high.astype(np.float64)).astype(jnp.bfloat16)
    return high, low


@functools.lru_cache(maxsize=None)
def tables():
    index = np.arange(10, dtype=np.float64)
    basis = np.sqrt(2.0 / 11.0) * np.sin(np.pi * (index[:, None] + 1.0) * (index[None, :] + 1.0) / 11.0)
    values = 2.0 - 2.0 * np.cos(np.pi * (index + 1.0) / 11.0)
    to_z = np.zeros((HZ, HW))
    from_z = np.zeros((HW, HZ))
    beyond = np.zeros((8, HW), np.float32)
    last = HZ // 8 - 1
    for e in range(last + 1):
        at = slice(e, 10 * (last + 1), last + 1)
        for k in range(10):
            z = 8 * e + k - 1
            if 0 <= z < HZ:
                to_z[z, at] = basis[k]
            if 1 <= k <= 8:
                from_z[at, z] = basis[k]
    beyond[0, last : 10 * (last + 1) : last + 1] = basis[9]
    beyond[1, 0 : 10 * (last + 1) : last + 1] = basis[0]
    beyond[2] = 1.0
    beyond[2, : 10 * (last + 1)] = np.repeat(values, last + 1)
    to_xy = np.zeros((10, EY, 10, 10, YR))
    from_xy = np.zeros((BX, BY, 10, EY, 10))
    for e in range(EY):
        for j in range(10):
            y = 8 * e + j - 1
            to_xy[:, e, :, :, y % YR] += basis.T[:, None, :] * basis[j][None, :, None]
            if 1 <= j <= 8:
                from_xy[:, y, :, e, :] = basis[1:9, :, None] * basis[j][None, None, :]
    to_xy = np.pad(to_xy.reshape(200, YW), ((0, AB - 200), (0, 256 - YW)))
    from_xy = np.pad(from_xy.reshape(BX * BY, 200), ((0, 0), (0, 256 - 200)))
    column = np.zeros((AB, 128), np.float32)
    grid = np.zeros((10, EY, 10, 2))
    grid[..., 0] = values[:, None, None] + values[None, None, :]
    grid[..., 1] = np.arange(EY)[None, :, None]
    column[:200, :2] = grid.reshape(200, 2)
    column[200:, 0] = 1.0
    return split_const(to_xy) + split_const(to_z) + split_const(from_xy) + split_const(from_z) + (column, beyond)


def dot(a, b):
    return jnp.dot(a, b, preferred_element_type=F32)


def split2(x):
    high = x.astype(BF16)
    return high, (x - high.astype(F32)).astype(BF16)


def split3(x):
    high = x.astype(BF16)
    rest = x - high.astype(F32)
    middle = rest.astype(BF16)
    return high, middle, (rest - middle.astype(F32)).astype(BF16)


def dot3(a, b):
    return dot(a[0], b[0]) + dot(a[0], b[1]) + dot(a[1], b[0])


def iota(shape, axis):
    return lax.broadcasted_iota(jnp.int32, shape, axis)


def total(x):
    while x.ndim > 2:
        x = jnp.sum(x, axis=0)
    return jnp.sum(jnp.sum(x, axis=0, keepdims=True), axis=1, keepdims=True)


def gather_table():
    shape = (BZ, EY * ELEMS)
    node, at = iota(shape, 0), iota(shape, 1)
    return jnp.where(at == node // 8 + (at // ELEMS) * (ELEMS + EZ), 1.0, 0.0).astype(BF16)


def spread_table():
    shape = (ELEMS, EY * BZ)
    element, at = iota(shape, 0), iota(shape, 1)
    return jnp.where(at // 8 == element, 1.0, 0.0).astype(BF16)


def element_row(field, table):
    parts = jnp.concatenate(split3(jnp.sum(field, axis=0)), axis=0)
    sums = dot(parts, table)
    sums = sums[0:16] + sums[16:32] + sums[32:48]
    return jnp.sum(sums[0:8, 0:ELEMS], axis=0, keepdims=True) + jnp.sum(sums[8:16, ELEMS:], axis=0, keepdims=True)


def expand_rows(rows):
    count = rows.shape[0]
    tall = jnp.broadcast_to(rows, (16, ELEMS)) if count == 1 else jnp.concatenate([rows, jnp.zeros((16 - count, ELEMS), F32)], axis=0)
    wide = dot(jnp.concatenate(split3(tall), axis=0), spread_table())
    return (wide[0:16] + wide[16:32] + wide[32:48])[0:count]


def expand_block(row):
    wide = expand_rows(row)
    low = jnp.broadcast_to(wide[:, 0:BZ], (8, BZ))
    high = jnp.broadcast_to(wide[:, BZ:], (8, BZ))
    return jnp.concatenate([low, high], axis=0)


def slot_mask(slots, offset):
    slot_of_row = lax.rem(iota((ELEMS, ELEMS), 0) + offset, ELEMS)
    return slot_of_row.astype(F32) == slots


def to_rows(element_values, slots, offset):
    return jnp.sum(jnp.where(slot_mask(slots, offset), element_values, 0.0), axis=1, keepdims=True)


def to_elements(row_values, slots, offset):
    return jnp.sum(jnp.where(slot_mask(slots, offset), row_values, 0.0), axis=0, keepdims=True)


def project(column, parts):
    out = 0.0
    at = 0
    for part in parts:
        size = part.shape[0]
        out = out + jnp.sum(column[at : at + size] * part[...], axis=0, keepdims=True)
        at += size
    return out


def correct(row, parts):
    out = []
    for part in parts:
        products = part[...] * row
        folded = products[:, 0:128]
        for at in range(128, KCOL, 128):
            folded = folded + products[:, at : at + 128]
        out.append(jnp.sum(folded, axis=1, keepdims=True))
    return jnp.concatenate(out, axis=0)


def store_sum(out_ref, first, second):
    count, _, width = out_ref.shape
    cut = width - 128
    out_ref[:, :, 0:cut] = jnp.broadcast_to(first[None], (count, 1, cut))
    out_ref[:, :, cut:width] = jnp.broadcast_to(second[None], (count, 1, 128))


def lanes(values):
    at = iota((1, 128), 1)
    row = jnp.zeros((1, 128), F32)
    for i, value in enumerate(values):
        row = jnp.where(at == i, value, row)
    return row


def lane(row, i):
    return jnp.sum(jnp.where(iota(row.shape, 1) == i, row, 0.0), axis=1, keepdims=True)


def odd(index):
    return lax.rem(index, 2) == 1


def pair_out(index, low, high):
    return jnp.where(odd(index), low, high), jnp.where(odd(index), high, low)


def pair_in(index, first, second):
    return jnp.where(odd(index), first, second), jnp.where(odd(index), second, first)


def extend_y(block, low, high, depth):
    at = iota((8, BZ), 0)
    tails = []
    for x in range(block.shape[0]):
        tail = jnp.zeros((8, BZ), F32)
        for i in range(depth):
            tail = jnp.where(at == i, high[i][x : x + 1], tail)
            tail = jnp.where(at == 8 - depth + i, low[i][x : x + 1], tail)
        tails.append(tail)
    return jnp.concatenate([block, jnp.stack(tails)], axis=1)


def roll_sum(x):
    count, rows, _ = x.shape
    beside = pltpu.roll(x, 1, 1) + pltpu.roll(x, rows - 1, 1)
    flat = x.reshape(count * rows, BZ)
    at = iota(flat.shape, 1)
    beside_z = jnp.where(at == 0, 0.0, pltpu.roll(flat, 1, 1)) + jnp.where(at == BZ - 1, 0.0, pltpu.roll(flat, BZ - 1, 1))
    return beside + beside_z.reshape(x.shape)


def fine_solve(rows, sigma, tables):
    wh, wl, th, tl, vh, vl, uh, ul, column, beyond = tables
    high, low = value(wh), value(wl)
    for table in tables:
        if isinstance(table, Loaded):
            table.begin()
    rows = jnp.concatenate([rows, jnp.zeros((256 - YW, BZ), F32)], axis=0)
    spectra = dot3((high, low), split2(rows))
    th, tl, vh, vl, uh, ul, column, beyond = [value(table) for table in (th, tl, vh, vl, uh, ul, column, beyond)]
    nodal = []
    for half in range(2):
        part = spectra[:, half * HZ : (half + 1) * HZ]
        edge = spectra[:, HZ : HZ + 1] if half == 0 else spectra[:, HZ - 1 : HZ]
        part = dot3(split2(part), (th, tl)) + edge * beyond[half : half + 1]
        sig = jnp.where(column[:, 1:2] == 0.0, repeat_lanes(sigma, half), repeat_lanes(sigma, 2 + half))
        part = part / (column[:, 0:1] + beyond[2:3] + sig)
        part = jnp.concatenate([part, jnp.zeros((256 - AB, HW), F32)], axis=0)
        part = dot3((vh, vl), split2(part))
        nodal.append(dot3(split2(part), (uh, ul)).reshape(BX, BY, HZ))
    return jnp.concatenate(nodal, axis=2)


def value(table):
    return (table.here() if isinstance(table, Loaded) else table)[...]


def repeat_lanes(row, group):
    only = jnp.where(iota((1, ELEMS), 1) // 32 == group, row, 0.0)
    only = only + pltpu.roll(only, 64, 1)
    only = only + pltpu.roll(only, 32, 1)
    return jnp.concatenate([only] * 3, axis=1)


def eye_mask():
    return iota((ELEMS, ELEMS), 0) == iota((ELEMS, ELEMS), 1)


def row_to_column(row):
    return jnp.sum(jnp.where(eye_mask(), row, 0.0), axis=1, keepdims=True)


def column_to_row(column):
    return jnp.sum(jnp.where(eye_mask(), column, 0.0), axis=0, keepdims=True)


def pad_tile(rows):
    at = iota((8, ELEMS), 0)
    tile = jnp.zeros((8, ELEMS), F32)
    for i, row in enumerate(rows):
        tile = jnp.where(at == i, row, tile)
    return jnp.concatenate([tile, jnp.zeros((8, BZ - ELEMS), F32)], axis=1)


def start_kernel(
    late, right_far, diagonal_far, slots_far, c, ya, yb, right, diagonal, slots_out, table_out
):
    d = lax.axis_index("narrow")
    right_load = late.start(right_far, right)
    diagonal_load = late.start(diagonal_far, diagonal)
    slots_in = slots_far.here()
    slots = jnp.concatenate([slots_in[0:1], slots_in[1:2]], axis=1).astype(F32)
    slots_out[...] = slots
    table = gather_table()
    table_out[...] = table
    right_load.wait()
    row = column_to_row(to_rows(element_row(right[...], table) * (1.0 / 16.0), slots, 0))
    c[...] = row
    diagonal_load.wait()
    for i, ref in enumerate((right, diagonal)):
        ya[i], yb[i] = pair_out(d, ref[:, 0, :], ref[:, BY - 1, :])
    ya[2] = pad_tile([row, slots])
    yb[2] = jnp.zeros((8, BZ), F32)


def stage_kernel(swapped, late, factor, *refs):
    d = lax.axis_index("narrow")
    half = ELEMS // 2
    at = pl.multiple_of(d * half, half) if swapped else 0
    there = pl.multiple_of((1 - d) * half, half) if swapped else half
    after, diagonal, table, sent, kept, done, sigma = refs[STAGED : STAGED + 7]
    late.start(factor.at[pl.ds(at, half)], kept)
    late.start(factor.at[pl.ds(there, half)], sent)
    for source, target in zip(refs[:STAGED], refs[STAGED + 7 :]):
        late.start(source, target)
    done[...] = after[...]
    sigma[...] = element_row(diagonal[...], table[...]) * (1.0 / 512.0)


def project_kernel(swapped, late, c, ra, rb, right, diagonal, kept, sent, sums, xa, xb):
    w, d = lax.axis_index("wide"), lax.axis_index("narrow")
    row = c[...]
    if swapped:
        half = ELEMS // 2
        other = ra[2, 0:1, 0:ELEMS]
        row = jnp.where(d == 0, row, pltpu.roll(row, half, 1))
        other = jnp.where(d == 0, pltpu.roll(other, half, 1), other)
        row = jnp.where(iota((1, ELEMS), 1) < half, row, other)
    sums[...] = jnp.broadcast_to(project(row_to_column(row), (kept, sent))[None], sums.shape)
    for i, ref in enumerate((right, diagonal)):
        low, high = pair_in(d, ra[i], rb[i])
        layers = [extend_y(ref[x : x + 1], [low[x : x + 1]], [high[x : x + 1]], 1)[0] for x in (0, BX - 1)]
        xa[i], xb[i] = pair_out(w, *layers)


def widened(block, ya, yb, xa, xb, i):
    w, d = lax.axis_index("wide"), lax.axis_index("narrow")
    low, high = pair_in(d, ya[i], yb[i])
    x_low, x_high = pair_in(w, xa[i], xb[i])
    return jnp.concatenate([x_low[None], extend_y(block, [low], [high], 1), x_high[None]], axis=0)


def first_fine_kernel(late, *rest):
    right, ya, yb, xa, xb, sigma, solved = rest[TABLES:]
    rows = widened(right[...], ya, yb, xa, xb, 0)
    tables = rest[TABLES - STAGED : TABLES] + rest[: TABLES - STAGED]
    solved[...] = fine_solve(rows.reshape(YW, BZ), sigma[...], tables)


def first_coarse_kernel(swapped, late, sums, solved, slots, kept, sent, ya, yb):
    d = lax.axis_index("narrow")
    row = jnp.sum(sums[...], axis=0)[:, 0:KCOL]
    column = correct(row, (kept, sent))
    for i in range(2):
        ya[i], yb[i] = pair_out(d, solved[:, i, :], solved[:, BY - 2 + i, :])
    if swapped:
        values = column_to_row(column)
        values = jnp.where(d == 0, values, pltpu.roll(values, ELEMS // 2, 1))
    else:
        values = to_elements(column, slots[...], 0)
    ya[2] = pad_tile([values])
    yb[2] = ya[2]


def extend_kernel(swapped, late, solved, slots, ra_first, own_ref, ra, rb, search, xa, xb):
    w, d = lax.axis_index("wide"), lax.axis_index("narrow")
    groups = lax.axis_size("narrow")
    own = own_ref[2, 0:1, 0:ELEMS]
    theirs = ra[2, 0:1, 0:ELEMS]
    if swapped:
        half = ELEMS // 2
        at = iota((1, ELEMS), 1) // half
        other = jnp.where(at == d, pltpu.roll(own, half, 1), theirs)
        own = jnp.where(at == d, own, pltpu.roll(theirs, half, 1))
        own = to_elements(row_to_column(own), slots[...], 0)
        other = to_elements(row_to_column(other), ra_first[2, 1:2, 0:ELEMS], 0)
        values_low, values_high = other, other
    else:
        values_low, values_high = pair_in(d, theirs, rb[2, 0:1, 0:ELEMS])
    values_low = jnp.where(d > 0, values_low, 0.0)
    values_high = jnp.where(d < groups - 1, values_high, 0.0)
    wide = expand_rows(jnp.concatenate([own, values_low, values_high], axis=0)) * (1.0 / 16.0)
    coarse = jnp.concatenate(
        [jnp.broadcast_to(wide[0:1, 0:BZ], (8, BZ)), jnp.broadcast_to(wide[0:1, BZ:], (8, BZ))], axis=0
    )
    low, high = [], []
    for i in range(2):
        one, two = pair_in(d, ra[i], rb[i])
        low.append(one + wide[1:2, BZ:])
        high.append(two + wide[2:3, 0:BZ])
    block = extend_y(solved[...] + coarse[None], low, high, 2)
    search[...] = block
    xa[...], xb[...] = pair_out(w, block[0:2], block[BX - 2 : BX])


def interior_kernel(late, diagonal_late, right, search, ya, yb, image, product, table, diagonal):
    d = lax.axis_index("narrow")
    low, high = pair_in(d, ya[1], yb[1])
    centre = search[...]
    diagonal[...] = diagonal_late.here()[...]
    part = (6.0 + extend_y(diagonal[...], [low], [high], 1)) * centre - roll_sum(centre)
    zero = jnp.zeros((1, YR, BZ), F32)
    part = part - jnp.concatenate([zero, centre[0 : BX - 1]], axis=0) - jnp.concatenate([centre[1:BX], zero], axis=0)
    image[...] = part
    product[...] = lanes([total(right[...] * centre[:, 0:BY])])
    table[...] = gather_table()


def operator_kernel(
    swapped, sizes, late, kept, received, search, inner, product, table, sa, sb, xa, xb, slots, sums, image_out, halo
):
    w, d = lax.axis_index("wide"), lax.axis_index("narrow")
    owned, offset = (kept, received), d * (ELEMS // 2) if swapped else 0
    s_low, s_high = pair_in(w, sa[...], sb[...])
    d_low, d_high = pair_in(w, xa[1], xb[1])
    low = (6.0 + d_low) * s_low[1] - s_low[0] - search[0] - roll_sum(s_low[1:2])[0]
    high = (6.0 + d_high) * s_high[0] - s_high[1] - search[BX - 1] - roll_sum(s_high[0:1])[0]
    y = iota((YR, BZ), 0)
    inside = (y < BY) | ((y == BY) & (d < sizes[1] - 1)) | ((y == YR - 1) & (d > 0))
    image_out[0] = jnp.where(inside & (w > 0), low, 0.0)
    image_out[1] = jnp.where(inside, inner[0] - s_low[1], 0.0)
    image_out[2:BX] = jnp.where(inside[None], inner[1 : BX - 1], 0.0)
    image_out[BX] = jnp.where(inside, inner[BX - 1] - s_high[0], 0.0)
    image_out[BX + 1] = jnp.where(inside & (w < sizes[0] - 1), high, 0.0)
    halo[0:BY] = s_low[1, 0:BY]
    halo[BY : 2 * BY] = s_high[0, 0:BY]
    halo[2 * BY : 2 * BY + 8] = search[:, YR - 1, :]
    halo[2 * BY + 8 : 3 * BY] = search[:, BY, :]
    own = image_out[1 : BX + 1, 0:BY, :]
    column = to_rows(element_row(own, table[...]) * (1.0 / 16.0), slots[...], offset)
    extra = lanes([lane(product[...], 0), total(search[:, 0:BY, :] * own)])
    store_sum(sums, project(column, owned), extra)


def second_fine_kernel(late, *rest):
    w, d = lax.axis_index("wide"), lax.axis_index("narrow")
    image, sigma, solved, ya, yb, xa, xb = rest[TABLES:]
    out = fine_solve(image[...].reshape(YW, BZ), sigma[...], rest[:TABLES])
    solved[...] = out
    ya[...], yb[...] = pair_out(d, solved[:, 0, :], solved[:, BY - 1, :])
    xa[...], xb[...] = pair_out(w, out[0], out[BX - 1])


def second_coarse_kernel(
    swapped, late, right, diagonal, kept, received, sums, solved, fya, fyb, fxa, fxb, search, halo, image, slots,
    search_out, image_out, last, products,
):
    w, d = lax.axis_index("wide"), lax.axis_index("narrow")
    owned, offset = (kept, received), d * (ELEMS // 2) if swapped else 0
    row = jnp.sum(sums[...], axis=0)
    products[...] = row[:, KCOL:WIDTH]
    step = lane(row[:, KCOL:WIDTH], 0) / lane(row[:, KCOL:WIDTH], 1)
    values = to_elements(correct(row[:, 0:KCOL], owned), slots[...], offset)
    coarse = expand_block(values * (1.0 / 16.0))
    own_search = search[:, 0:BY, :]
    own_image = image[1 : BX + 1, 0:BY, :]
    vector = own_search - step * (solved[...] + coarse[None])
    f_low, f_high = pair_in(w, fxa[...], fxb[...])
    x_low = halo[0:BY] - step * f_low
    x_high = halo[BY : 2 * BY] - step * f_high
    g_low, g_high = pair_in(d, fya[...], fyb[...])
    y_low = halo[2 * BY : 2 * BY + 8] - step * g_low
    y_high = halo[2 * BY + 8 : 3 * BY] - step * g_high
    beside = roll_sum(extend_y(vector, [y_low], [y_high], 1))[:, 0:BY]
    beside = beside + jnp.concatenate([x_low[None], vector[0 : BX - 1]], axis=0)
    beside = beside + jnp.concatenate([vector[1:BX], x_high[None]], axis=0)
    next_image = (6.0 + diagonal[...]) * vector - beside
    search_out[...] = vector
    image_out[...] = next_image
    residual = right[...] - step * own_image
    edges = total(coarse * (x_low + x_high)) + total(y_low * coarse[0:1]) + total(y_high * coarse[BY - 1 : BY])
    store_sum(
        last,
        values,
        lanes([total(residual * vector), total(vector * next_image) + step * edges, total(vector * own_image)]),
    )


def last_kernel(sizes, late, right, products, last, search, image, next_search, next_image, x_out, r_out):
    w, d = lax.axis_index("wide"), lax.axis_index("narrow")
    groups = sizes[1]
    count = sizes[0] * groups
    product, bottom = lane(products[...], 0), lane(products[...], 1)
    step = product / bottom
    z = last[:, 0, 0:ELEMS]
    rows = iota((count, ELEMS), 0)
    at = iota((count, ELEMS), 1)
    faces = jnp.where(rows < count - groups, z * pltpu.roll(z, count - groups, 0), 0.0)
    across = pltpu.roll(pltpu.roll(z, count - 1, 0), EZ, 1)
    faces = faces + jnp.where((lax.rem(rows, groups) < groups - 1) & (at >= EZ), z * across, 0.0)
    sums = jnp.sum(last[:, :, ELEMS:], axis=0)
    next_product = lane(sums, 0)
    quadratic = lane(sums, 1) - step * step * 0.5 * total(faces)
    cross = lane(sums, 2)
    me = w * groups + d
    picked = []
    for index, there in ((me - groups, w > 0), (me + groups, w < sizes[0] - 1), (me - 1, d > 0), (me + 1, d < groups - 1)):
        picked.append(jnp.sum(jnp.where((rows == index) & there, z, 0.0), axis=0, keepdims=True))
    wide = expand_rows(jnp.concatenate(picked, axis=0)) * (1.0 / 16.0)
    layers = []
    for i in range(2):
        low = jnp.broadcast_to(wide[i : i + 1, 0:BZ], (8, BZ))
        high = jnp.broadcast_to(wide[i : i + 1, BZ:], (8, BZ))
        layers.append(jnp.concatenate([low, high], axis=0)[None])
    shape = (BX, BY, BZ)
    x, y = iota(shape, 0), iota(shape, 1)
    missing = jnp.where(x == 0, layers[0], 0.0) + jnp.where(x == BX - 1, layers[1], 0.0)
    missing = missing + jnp.where(y == 0, wide[2:3, BZ:][None], 0.0) + jnp.where(y == BY - 1, wide[3:4, 0:BZ][None], 0.0)
    ratio = next_product / product
    curvature = quadratic + 2.0 * ratio * cross + ratio * ratio * bottom
    step_next = next_product / curvature
    own_search = search[:, 0:BY, :]
    own_image = image[1 : BX + 1, 0:BY, :]
    direction = next_search[...] + ratio * own_search
    total_image = next_image[...] + step * missing + ratio * own_image
    x_out[...] = step * own_search + step_next * direction
    r_out[...] = (right[...] - step * own_image) - step_next * total_image


class Loaded:
    def __init__(self, copy, ref):
        self.copy, self.ref, self.begun, self.ready = copy, ref, False, False

    def begin(self):
        if not self.begun:
            self.copy.start()
            self.begun = True

    def wait(self):
        self.begin()
        if not self.ready:
            self.copy.wait()
            self.ready = True

    def here(self):
        self.wait()
        return self.ref


class Copies:
    def __init__(self, semaphores):
        self.semaphores, self.all = semaphores, []

    def start(self, source, target, begin=True):
        self.all.append(Loaded(pltpu.make_async_copy(source, target, self.semaphores.at[len(self.all)]), target))
        if begin:
            self.all[-1].begin()
        return self.all[-1]

    def finish(self):
        for loaded in self.all:
            loaded.wait()


def call(kernel, outs, far=(), late=(), near=(), final=False, first_wave=99):
    first, second = len(far), len(far) + len(late)

    def run(*refs):
        end = len(refs) - 1 - len(late)
        copies = Copies(refs[-1])
        loaded = [
            copies.start(source, target, i < first_wave)
            for i, (source, target) in enumerate(zip(refs[first:second], refs[end:-1]))
        ]
        kernel(copies, *refs[:first], *loaded, *refs[second:end])
        copies.finish()

    shape_of = jax.ShapeDtypeStruct if final else pltpu.VMEM
    spaces = [pltpu.HBM] * second + [pltpu.VMEM] * len(near)
    return pl.pallas_call(
        run,
        out_shape=[shape_of(getattr(out, "shape", out), getattr(out, "dtype", F32)) for out in outs],
        in_specs=[pl.BlockSpec(memory_space=space) for space in spaces],
        out_specs=[pl.BlockSpec(memory_space=pltpu.VMEM)] * len(outs),
        scratch_shapes=[*(pltpu.VMEM(array.shape, array.dtype) for array in late), pltpu.SemaphoreType.DMA((second + 2,))],
        compiler_params=pltpu.CompilerParams(vmem_limit_bytes=16 * 1024 * 1024),
    )(*(pltpu.with_memory_space_constraint(array, pltpu.HBM) for array in (*far, *late)), *near)


def pair_swap(first, second, axis):
    size = lax.axis_size(axis)
    received = []
    for value, begin in ((first, 0), (second, 1)):
        perm = []
        for i in range(begin, size - 1, 2):
            perm += [(i, i + 1), (i + 1, i)]
        received.append(lax.ppermute(value, axis, perm) if perm else jnp.zeros_like(value))
    return received


def everywhere(rows):
    return lax.all_to_all(rows, AXES, split_axis=0, concat_axis=0, tiled=True)


def body(right, diagonal, coarse_slot, factor):
    sizes = (lax.axis_size("wide"), lax.axis_size("narrow"))
    groups = sizes[1]
    count = sizes[0] * groups
    fine = [jnp.asarray(c) for c in tables()]
    slots = coarse_slot.reshape(EY, EZ)
    swapped = groups == 2
    if not swapped:
        factor = factor.reshape(groups, ELEMS // groups, KCOL)
        factor = lax.all_to_all(factor, "narrow", split_axis=0, concat_axis=0, tiled=True).reshape(ELEMS, KCOL)
    part = functools.partial

    block, layer, extended = (BX, BY, BZ), (YR, BZ), (BX, YR, BZ)
    y_shape, x_shape, half = (3, BX, BZ), (2, YR, BZ), (ELEMS // 2, KCOL)
    gather = jax.ShapeDtypeStruct((BZ, EY * ELEMS), BF16)
    diagonal_far = diagonal
    c, ya, yb, right, diagonal, slots, table = call(
        start_kernel,
        [(1, ELEMS), y_shape, y_shape, block, block, (1, ELEMS), gather],
        far=[right, diagonal],
        late=[slots],
    )
    ya, yb = pair_swap(ya, yb, "narrow")
    sent, kept, c, sigma, *near = call(
        part(stage_kernel, swapped),
        [half, half, (1, ELEMS), (1, ELEMS), *fine[:STAGED]],
        far=[factor, *fine[:STAGED]],
        near=[c, diagonal, table],
    )
    sums, xa, xb = call(
        part(project_kernel, swapped), [(count, 1, KCOL), x_shape, x_shape], near=[c, ya, yb, right, diagonal, kept, sent]
    )
    sums = everywhere(sums)
    xa, xb = pair_swap(xa, xb, "wide")
    (solved,) = call(first_fine_kernel, [block], late=fine[STAGED:], near=[*near, right, ya, yb, xa, xb, sigma])
    ta, tb = call(part(first_coarse_kernel, swapped), [y_shape, y_shape], near=[sums, solved, slots, kept, sent])
    ra, rb = pair_swap(ta, tb, "narrow")
    received = lax.ppermute(sent, "narrow", [(0, 1), (1, 0)]) if swapped else sent
    search, sa, sb = call(
        part(extend_kernel, swapped),
        [extended, (2,) + layer, (2,) + layer],
        near=[solved, slots, ya, ta, ra, rb],
    )
    sa, sb = pair_swap(sa, sb, "wide")
    inner, product, table, diagonal = call(
        interior_kernel, [extended, (1, 128), gather, block], late=[diagonal_far], near=[right, search, ya, yb]
    )
    sums, image, halo = call(
        part(operator_kernel, swapped, sizes),
        [(count, 1, WIDTH), (BX + 2, YR, BZ), (3 * BY, BZ)],
        near=[kept, received, search, inner, product, table, sa, sb, xa, xb, slots],
    )
    sums = everywhere(sums)
    solved, ya, yb, fa, fb = call(
        second_fine_kernel, [block, (BX, BZ), (BX, BZ), (BY, BZ), (BY, BZ)], late=fine, near=[image, sigma]
    )
    ya, yb = pair_swap(ya, yb, "narrow")
    fa, fb = pair_swap(fa, fb, "wide")
    next_search, next_image, last, products = call(
        part(second_coarse_kernel, swapped),
        [block, block, (count, 1, 2 * ELEMS), (1, 128)],
        near=[right, diagonal, kept, received, sums, solved, ya, yb, fa, fb, search, halo, image, slots],
    )
    last = everywhere(last)
    return tuple(
        call(
            part(last_kernel, sizes),
            [block, block],
            near=[right, products, last, search, image, next_search, next_image],
            final=True,
        )
    )


def solution(mesh):
    in_specs = (
        P("wide", "narrow", None),
        P("wide", "narrow", None),
        P("wide", "narrow", None),
        P(("wide", "narrow"), None),
    )
    out_specs = (P("wide", "narrow", None), P("wide", "narrow", None))
    return jax.shard_map(body, mesh=mesh, in_specs=in_specs, out_specs=out_specs, check_vma=False)
```
